256 devices in a mesh: gx: 8 (over x, core), gy: 32 (over z, y).
Axes of the slice: x: 4, y: 4, z: 8, core: 2. Of those that a mesh axis runs over, the one named last changes fastest.
Arguments:
- right_side: float32 [256, 1024, 128], P('gx', 'gy'), may hold values from -38 to 38
- guess: float32 [256, 1024, 128], P('gx', 'gy'), may hold values from -3 to 3
- conductivity: float32 [256, 1024, 128], P('gx', 'gy'), may hold values from 0.5 to 4
- wet_mask: int32 [256, 1024, 128], P('gx', 'gy'), may hold values from 0 to 1, as said below
- coarse_map: int32 [16, 64, 1], P('gx', 'gy'), may hold values from 0 to 1023
- coarse_inverse: float32 [1024, 1024], P(('gx', 'gy')), may hold values from -6.473756e-05 to 0.0028268734
Outputs:
- pressure: float32 [256, 1024, 128], P('gx', 'gy')
- residual: float32 [256, 1024, 128], P('gx', 'gy')
The draws below stay inside these ranges and needn't reach their ends.
Inputs may be any that keep to these rules, and one draw needn't show every extreme that they name: `wet_mask`: 1 marks a wet cell and 0 a dry one; the dry cells of each column of levels are its lowest ones. `coarse_map`: every coarse node 0 to 1023 is named by at least one block.
All inputs are finite; a program needn't handle non-finite values.
Results may differ from the reference program's by a relative error of at most 0.0003.
Values sent between devices are 32-bit elements; how exact they have to be, the bound alone decides.
A program may use at most 64 MiB of HBM per device.

```python
import math
import jax
import jax.numpy as jnp
from jax import lax

TX = 32
TY = 32
NZ = 128
BLK = 16
MARGIN = 2
SWEEPS = 4
NX = 256
NY = 1024
NC = 1024
CELLS_NODE = 32768
N_GX = 8
N_GY = 32


def draw_right_side(key, part):
    core_key, column_key = jax.random.split(jax.random.fold_in(key, 11))
    ypos = jnp.arange(NY, dtype=jnp.float32) / NY
    rows = (10.0 ** (ypos - 0.5))[None, :, None]
    columns = jnp.exp(jax.random.uniform(column_key, (NX, 1, 1), jnp.float32, 0.0, jnp.log(3.0)))
    core = jax.random.truncated_normal(core_key, -4.0, 4.0, (NX, NY, NZ), jnp.float32)
    return core * rows * columns


def draw_wet_mask(key, part):
    depth = jax.random.randint(jax.random.fold_in(key, 23), (NX, NY, 1), 0, NZ // 4 + 1)
    level = jnp.arange(NZ, dtype=jnp.int32)[None, None, :]
    return (level >= depth).astype(jnp.int32)


def draw_coarse_inverse(key, part):
    diag_key, off_key = jax.random.split(jax.random.fold_in(key, 37))
    scale = 0.25 / CELLS_NODE ** 0.5
    rows = jnp.arange(NC, dtype=jnp.int32)[:, None]
    cols = jnp.arange(NC, dtype=jnp.int32)[None, :]
    diag = jax.random.uniform(diag_key, (NC, 1), jnp.float32, 1.0, 2.0)
    off = jax.random.truncated_normal(off_key, -3.0, 3.0, (NC, NC), jnp.float32) * (0.5 / NC ** 0.5)
    return scale * (jnp.where(rows == cols, diag, 0.0) + off)


def level_of(own_key, dims, shards, smallest, largest):
    loudness, own = 1.0, jax.random.fold_in(own_key, 6)
    for dim, blocks in shards:
        heights = jnp.exp(jax.random.uniform(jax.random.fold_in(own, dim), (blocks,), jnp.float32, smallest / len(shards), largest / len(shards)))
        loudness = loudness * jnp.repeat(heights, dims[dim] // blocks).reshape([-1 if axis == dim else 1 for axis in range(len(dims))])
    return loudness


def picks_of(own_key, rows, count, top, lift):
    ranking = jax.random.permutation(jax.random.fold_in(own_key, 1), count)
    boost = ranking
    for power in range(3):
        boost = boost * boost // count
    boost = boost * lift // count
    tickets = jax.random.randint(jax.random.fold_in(own_key, 2), (rows, count), 0, 4096) + boost
    holders = jax.random.permutation(jax.random.fold_in(own_key, 3), rows)[jnp.arange(count) % rows]
    tickets = jnp.where(jnp.arange(rows)[:, None] == holders[None, :], 1 << 14, tickets)
    score = tickets * count + jnp.arange(count)
    return lax.top_k(score.astype(jnp.int32), top)[1].astype(jnp.int32)


def centred(key, shape, width, bound, cuts=(), kind=jnp.bfloat16):
    factor_of = level_of(key, shape, cuts, -0.22, 0.18) if cuts else 1.0
    drawn = jax.random.normal(key, shape, jnp.float32) * width * factor_of
    return jnp.minimum(jnp.maximum(drawn, -bound), bound).astype(kind)


def setup_inputs(seed: int = 0) -> dict:
    splits = jax.random.split(jax.random.key(seed), 7)
    right_side = draw_right_side(jax.random.fold_in(splits[6], 71), 0)
    guess = centred(splits[1], (NX, NY, NZ), 0.2, 3.0, ((0, 8), (1, 32)), jnp.float32)
    conductivity = jnp.clip(jnp.exp(math.log(4.0) - 2.0794415 * jax.random.uniform(splits[2], (NX, NY, NZ), jnp.float32) ** level_of(splits[2], (NX, NY, NZ), ((0, 8), (1, 32)), -0.2, 0.2)), 0.5, 4.0)
    wet_mask = draw_wet_mask(jax.random.fold_in(splits[6], 71), 0)
    coarse_map = picks_of(splits[4], (NX // BLK) * (NY // BLK), NC, 1, 8).reshape((NX // BLK, NY // BLK, 1))
    coarse_inverse = draw_coarse_inverse(jax.random.fold_in(splits[6], 71), 0)
    return {"right_side": right_side, "guess": guess, "conductivity": conductivity, "wet_mask": wet_mask, "coarse_map": coarse_map, "coarse_inverse": coarse_inverse}


screen = 0.02
relax = 0.8


def face_weights(cond):
    zpad = jnp.pad(cond, ((0, 0), (0, 0), (1, 1)))
    center = cond[1:-1, 1:-1, :]
    west = jnp.minimum(center, cond[:-2, 1:-1, :])
    east = jnp.minimum(center, cond[2:, 1:-1, :])
    south = jnp.minimum(center, cond[1:-1, :-2, :])
    north = jnp.minimum(center, cond[1:-1, 2:, :])
    below = jnp.minimum(center, zpad[1:-1, 1:-1, :-2])
    above = jnp.minimum(center, zpad[1:-1, 1:-1, 2:])
    diag = screen + jnp.maximum(0.0, 1.0 - 2.0 * center) + west + east + south + north + below + above
    return diag, (west, east, south, north, below, above)


def neighbours(field, weights):
    west, east, south, north, below, above = weights
    zpad = jnp.pad(field, ((0, 0), (0, 0), (1, 1)))
    total = west * field[:-2, 1:-1] + east * field[2:, 1:-1]
    total = total + south * field[1:-1, :-2] + north * field[1:-1, 2:]
    return total + below * zpad[1:-1, 1:-1, :-2] + above * zpad[1:-1, 1:-1, 2:]


def operate(field, diag, weights):
    return diag * field[1:-1, 1:-1] - neighbours(field, weights)


def smooth(resid, diag, weights):
    correction = relax * resid / diag
    for sweep in range(SWEEPS - 1):
        padded = jnp.pad(correction, ((1, 1), (1, 1), (0, 0)))
        correction = correction + relax * (resid - diag * correction + neighbours(padded, weights)) / diag
    return correction


def tile_start(index):
    first = (index // N_GY).astype(jnp.int32)
    second = (index % N_GY).astype(jnp.int32)
    return first * TX, second * TY


def untile(tiles):
    return tiles.reshape(N_GX, N_GY, TX, TY, NZ).transpose(0, 2, 1, 3, 4).reshape(NX, NY, NZ)


def reference(right_side, guess, conductivity, wet_mask, coarse_map, coarse_inverse):
    wide = MARGIN + 1
    spread = ((wide, wide), (wide, wide), (0, 0))
    cond_pad = jnp.pad(conductivity * wet_mask.astype(jnp.float32), spread)
    guess_pad = jnp.pad(guess, spread)
    right_pad = jnp.pad(right_side, spread)
    zero = jnp.zeros((), jnp.int32)
    ext_x = TX + 2 * wide
    ext_y = TY + 2 * wide
    tiles_all = jnp.arange(N_GX * N_GY, dtype=jnp.int32)

    def first_pass(index):
        start_x, start_y = tile_start(index)
        cond_ext = lax.dynamic_slice(cond_pad, (start_x, start_y, zero), (ext_x, ext_y, NZ))
        guess_ext = lax.dynamic_slice(guess_pad, (start_x, start_y, zero), (ext_x, ext_y, NZ))
        right_ext = lax.dynamic_slice(right_pad, (start_x, start_y, zero), (ext_x, ext_y, NZ))[1:-1, 1:-1]
        diag_ext, weights_ext = face_weights(cond_ext)
        resid_ext = right_ext - operate(guess_ext, diag_ext, weights_ext)
        local = smooth(resid_ext, diag_ext, weights_ext)[MARGIN:MARGIN + TX, MARGIN:MARGIN + TY]
        return local, resid_ext[MARGIN:MARGIN + TX, MARGIN:MARGIN + TY]

    local_tiles, resid_tiles = lax.map(first_pass, tiles_all)
    local = untile(local_tiles)
    resid = untile(resid_tiles)

    block_sums = resid.reshape(NX // BLK, BLK, NY // BLK, BLK, NZ).sum(axis=(1, 3, 4)).reshape(-1)
    nodes = coarse_map.reshape(-1)
    onehot = (nodes[:, None] == jnp.arange(NC, dtype=jnp.int32)[None, :]).astype(jnp.float32)
    coarse_resid = jnp.dot(block_sums, onehot, precision=lax.Precision.HIGHEST)
    coarse_corr = jnp.dot(coarse_inverse, coarse_resid, precision=lax.Precision.HIGHEST)
    block_corr = jnp.dot(onehot, coarse_corr, precision=lax.Precision.HIGHEST).reshape(NX // BLK, NY // BLK)
    direction = (local.reshape(NX // BLK, BLK, NY // BLK, BLK, NZ)
                 + block_corr[:, None, :, None, None]).reshape(NX, NY, NZ)
    direction_pad = jnp.pad(direction, ((1, 1), (1, 1), (0, 0)))

    def second_pass(index):
        start_x, start_y = tile_start(index)
        cond_near = lax.dynamic_slice(cond_pad, (start_x + MARGIN, start_y + MARGIN, zero), (TX + 2, TY + 2, NZ))
        field_near = lax.dynamic_slice(direction_pad, (start_x, start_y, zero), (TX + 2, TY + 2, NZ))
        diag, weights = face_weights(cond_near)
        return operate(field_near, diag, weights)

    image = untile(lax.map(second_pass, tiles_all))
    alpha = jnp.sum(resid * direction) / jnp.sum(direction * image)
    return guess + alpha * direction, resid - alpha * image
```

```python
import jax
import jax.numpy as jnp
from jax import lax
from jax.experimental import pallas as pl
from jax.experimental.pallas import tpu as pltpu
from jax.sharding import PartitionSpec as P

F32 = jnp.float32
MESH = pl.DeviceIdType.MESH
BLK = 16
T = 32
NZ = 128
SWEEPS = 4
STRIDE = 40
ROWS = 40
FLAT = ROWS * STRIDE
NODES = 1024
GROUP = 16
screen = 0.02
relax = 0.8
LO, CHUNK, STEPS = 72, 112, 13


def flat_of(x, y):
    return (x + 4) * STRIDE + y


def view(ref):
    return ref.reshape(FLAT, NZ)


def kernel(
    cmap, cinv, right, guess, conductivity, wet,
    d_out, image_out, resid_out, alpha_out,
    ext, mask, w_east, w_north, w_above, diag, dinv, first, e_a, e_b, resid, d_ext, image, inverse,
    ya_send, ya_recv, yb_send, yb_recv, k_send, k_recv, map_send, map_recv, l_send, l_recv,
    part, recv,
    load_sem, out_sem, xa_ss, xa_rs, xb_ss, xb_rs, xr_ss, xr_rs, ya_ss, ya_rs, yb_ss, yb_rs,
    k_ss, k_rs, map_ss, map_rs, l_ss, l_rs, g_ss, g_rs,
):
    gx, gy = lax.axis_index("gx"), lax.axis_index("gy")
    n_gx, n_gy = lax.axis_size("gx"), lax.axis_size("gy")
    west = (lax.rem(gx + n_gx - 1, n_gx), gy)
    east = (lax.rem(gx + 1, n_gx), gy)
    south = (gx, lax.rem(gy + n_gy - 1, n_gy))
    north = (gx, lax.rem(gy + 1, n_gy))
    corners = [(px[0], py[1]) for px in (west, east) for py in (south, north)]
    sides = (west, east, south, north)
    near = gx * 2 + lax.rem(gy, 2)
    far = gy // 2

    def near_peer(k):
        j = lax.rem(near + k, GROUP)
        return (j // 2, far * 2 + lax.rem(j, 2))

    def far_peer(k):
        j = lax.rem(far + k, GROUP)
        return (gx, j * 2 + lax.rem(gy, 2))

    own = (pl.ds(4, T), pl.ds(0, T))
    loads = [
        pltpu.make_async_copy(conductivity, ext.at[(0,) + own], load_sem.at[0]),
        pltpu.make_async_copy(wet, mask, load_sem.at[1]),
        pltpu.make_async_copy(guess, ext.at[(1,) + own], load_sem.at[2]),
        pltpu.make_async_copy(right, ext.at[(2,) + own], load_sem.at[3]),
        pltpu.make_async_copy(cinv, inverse, load_sem.at[4]),
    ]
    for copy in loads:
        copy.start()

    pad = jnp.zeros((8, NZ), F32)
    wide = jnp.zeros((STRIDE, NZ), F32)
    for a in range(3):
        for r in (0, 1, 2, 3, 36, 37, 38, 39):
            ext[a, r] = wide
        for r in range(4, 36):
            ext[a, r, pl.ds(32, 8)] = pad
    for ref in (w_east, w_north, first, e_a, e_b):
        view(ref)[pl.ds(0, LO)] = jnp.zeros((LO, NZ), F32)
        view(ref)[pl.ds(LO + CHUNK * STEPS, FLAT - LO - CHUNK * STEPS)] = jnp.zeros(
            (FLAT - LO - CHUNK * STEPS, NZ), F32)

    barrier = pltpu.get_barrier_semaphore()
    for peer in list(sides) + corners:
        pl.semaphore_signal(barrier, inc=1, device_id=peer, device_id_type=MESH)

    def greet(k, carry):
        pl.semaphore_signal(barrier, inc=1, device_id=near_peer(k), device_id_type=MESH)
        pl.semaphore_signal(barrier, inc=1, device_id=far_peer(k), device_id_type=MESH)
        return carry

    lax.fori_loop(1, GROUP, greet, 0)

    sub = lax.broadcasted_iota(jnp.int32, (8, NZ), 0)
    lane = lax.broadcasted_iota(jnp.int32, (8, NZ), 1)
    node_of = sub * NZ + lane
    nodes = [[cmap[bx, by, 0] for by in range(2)] for bx in range(2)]
    packed = jnp.zeros((8, NZ), jnp.int32)
    for bx in range(2):
        for by in range(2):
            packed = jnp.where(sub == 2 * bx + by, nodes[bx][by], packed)
    map_send[...] = packed

    def remote(src, dst, ss, rs, peer):
        return pltpu.make_async_remote_copy(
            src_ref=src, dst_ref=dst, send_sem=ss, recv_sem=rs, device_id=peer, device_id_type=MESH)

    loads[0].wait()
    loads[1].wait()

    def masked(r, carry):
        ext[0, r + 4, pl.ds(0, T)] = ext[0, r + 4, pl.ds(0, T)] * mask[r].astype(F32)
        return carry

    lax.fori_loop(0, T, masked, 0, unroll=4)
    loads[2].wait()
    cond_f, guess_f, right_f = (view(ext.at[a]) for a in range(3))
    fields = (cond_f, guess_f)

    def column(ref, y):
        return ref[pl.ds(flat_of(0, y), T, stride=STRIDE)]

    for a in range(2):
        ya_send[0, a] = column(fields[a], 0)
        ya_send[1, a] = column(fields[a], T - 1)
    pl.semaphore_wait(barrier, 8 + 2 * (GROUP - 1))

    x_from, x_to = (4, 35), (36, 3)
    started = []

    def start(copy):
        copy.start()
        started.append(copy)
        return copy

    xa = [start(remote(ext.at[pl.ds(0, 2), x_from[s], pl.ds(0, T)], ext.at[pl.ds(0, 2), x_to[s], pl.ds(0, T)],
                       xa_ss.at[s], xa_rs.at[s], sides[s])) for s in range(2)]
    ya = [start(remote(ya_send.at[s], ya_recv.at[s], ya_ss.at[s], ya_rs.at[s], sides[2 + s])) for s in range(2)]
    loads[3].wait()
    for s, rows in enumerate(((1, 2), (T - 3, T - 2))):
        for a in range(2):
            for i in range(2):
                yb_send[s, 2 * a + i] = column(fields[a], rows[i])
    for s, rows in enumerate(((0, 1), (T - 2, T - 1))):
        for i in range(2):
            yb_send[s, 4 + i] = column(right_f, rows[i])
    xb_from, xb_to = (5, 33), (37, 1)
    xr_from, xr_to = (4, 34), (36, 2)
    xb, xr = [], []
    for s in range(2):
        xb.append(start(remote(ext.at[pl.ds(0, 2), pl.ds(xb_from[s], 2), pl.ds(0, T)],
                               ext.at[pl.ds(0, 2), pl.ds(xb_to[s], 2), pl.ds(0, T)],
                               xb_ss.at[s], xb_rs.at[s], sides[s])))
        xr.append(start(remote(ext.at[2, pl.ds(xr_from[s], 2), pl.ds(0, T)],
                               ext.at[2, pl.ds(xr_to[s], 2), pl.ds(0, T)],
                               xr_ss.at[s], xr_rs.at[s], sides[s])))
    yb = [start(remote(yb_send.at[s], yb_recv.at[s], yb_ss.at[s], yb_rs.at[s], sides[2 + s])) for s in range(2)]
    kc = []
    for q in range(4):
        sx, sy = q // 2, q % 2
        x3, y3 = (0, T - 3)[sx], (0, T - 3)[sy]
        x2, y2 = (0, T - 2)[sx], (0, T - 2)[sy]
        for a in range(2):
            for i in range(3):
                k_send[q, pl.ds(9 * a + 3 * i, 3)] = fields[a][pl.ds(flat_of(x3 + i, y3), 3)]
        k_send[q, pl.ds(22, 2)] = jnp.zeros((2, NZ), F32)
        for i in range(2):
            k_send[q, pl.ds(18 + 2 * i, 2)] = right_f[pl.ds(flat_of(x2 + i, y2), 2)]
        kc.append(start(remote(k_send.at[q], k_recv.at[q], k_ss.at[q], k_rs.at[q], corners[q])))
    mc = [start(remote(map_send, map_recv.at[s], map_ss.at[s], map_rs.at[s], sides[s])) for s in range(4)]

    def cells(bx):
        def add(r, acc):
            c = ext[0, 4 + 16 * bx + r, pl.ds(0, T)]
            g = ext[1, 4 + 16 * bx + r, pl.ds(0, T)]
            b = ext[2, 4 + 16 * bx + r, pl.ds(0, T)]
            return acc + (b - (screen + jnp.maximum(0.0, 1.0 - 2.0 * c)) * g)
        return lax.fori_loop(0, BLK, add, jnp.zeros((T, NZ), F32), unroll=4)

    def halves(v):
        return v[:BLK], v[BLK:]

    sums = [list(halves(cells(0))), list(halves(cells(1)))]

    def flux(c0, g0, c1, g1):
        return halves(jnp.minimum(c0, c1) * (g0 - g1))

    def row(a, x):
        return ext[a, 4 + x, pl.ds(0, T)]

    mid = flux(row(0, 15), row(1, 15), row(0, 16), row(1, 16))
    for i in range(2):
        sums[0][i] -= mid[i]
        sums[1][i] += mid[i]
    mid = flux(column(cond_f, 15), column(guess_f, 15), column(cond_f, 16), column(guess_f, 16))
    for i in range(2):
        sums[i][0] -= mid[i]
        sums[i][1] += mid[i]

    def clear(rows):
        cond_f[pl.ds(rows[0], rows[1])] = jnp.zeros((rows[1], NZ), F32)

    for s in range(2):
        xa[s].wait_recv()

    @pl.when(gx == 0)
    def _():
        clear((flat_of(-1, 0), T))

    @pl.when(gx == n_gx - 1)
    def _():
        clear((flat_of(T, 0), T))

    for s in range(2):
        ya[s].wait_recv()
    for a in range(2):
        fields[a][pl.ds(flat_of(0, T), T, stride=STRIDE)] = ya_recv[0, a]
        fields[a][pl.ds(flat_of(0, -1), T, stride=STRIDE)] = ya_recv[1, a]

    @pl.when(gy == 0)
    def _():
        cond_f[pl.ds(flat_of(0, -1), T, stride=STRIDE)] = jnp.zeros((T, NZ), F32)

    @pl.when(gy == n_gy - 1)
    def _():
        cond_f[pl.ds(flat_of(0, T), T, stride=STRIDE)] = jnp.zeros((T, NZ), F32)

    edge_x = [flux(row(0, x), row(1, x), row(0, n), row(1, n)) for x, n in ((0, -1), (T - 1, T))]
    edge_y = [flux(column(cond_f, y), column(guess_f, y), column(cond_f, n), column(guess_f, n))
              for y, n in ((0, -1), (T - 1, T))]
    vec = jnp.zeros((8, NZ), F32)
    for bx in range(2):
        for by in range(2):
            total = sums[bx][by] - edge_x[bx][by] - edge_y[by][bx]
            total = jnp.sum(jnp.sum(total, axis=0, keepdims=True), axis=1, keepdims=True)
            vec = vec + jnp.where(node_of == nodes[bx][by], total, 0.0)

    def send_group(stage, value, peer_of):
        part[stage] = value
        for k in range(1, GROUP):
            remote(part.at[stage], recv.at[stage, GROUP - 1 - k], g_ss.at[stage], g_rs.at[stage], peer_of(k)).start()

    def recv_group(stage):
        pltpu.make_async_copy(recv.at[stage], recv.at[stage], g_rs.at[stage]).wait()
        return part[stage] + jnp.sum(recv[stage], axis=0)

    send_group(0, vec, near_peer)

    for s in range(2):
        xb[s].wait_recv()
        xr[s].wait_recv()
        yb[s].wait_recv()
    for s, rows in enumerate(((T + 1, T + 2), (-3, -2))):
        for a in range(2):
            for i in range(2):
                fields[a][pl.ds(flat_of(0, rows[i]), T, stride=STRIDE)] = yb_recv[s, 2 * a + i]
    for s, rows in enumerate(((T, T + 1), (-2, -1))):
        for i in range(2):
            right_f[pl.ds(flat_of(0, rows[i]), T, stride=STRIDE)] = yb_recv[s, 4 + i]
    for q in range(4):
        kc[q].wait_recv()
        sx, sy = q // 2, q % 2
        x3, y3 = (T, -3)[sx], (T, -3)[sy]
        x2, y2 = (T, -2)[sx], (T, -2)[sy]
        for a in range(2):
            for i in range(3):
                fields[a][pl.ds(flat_of(x3 + i, y3), 3)] = k_recv[q, pl.ds(9 * a + 3 * i, 3)]
        for i in range(2):
            right_f[pl.ds(flat_of(x2 + i, y2), 2)] = k_recv[q, pl.ds(18 + 2 * i, 2)]

    @pl.when(gx == 0)
    def _():
        clear((flat_of(-3, -4), 3 * STRIDE))

    @pl.when(gx == n_gx - 1)
    def _():
        clear((flat_of(T, -4), 3 * STRIDE))

    @pl.when(gy == 0)
    def _():
        for y in (-3, -2, -1):
            cond_f[pl.ds(flat_of(-3, y), T + 6, stride=STRIDE)] = jnp.zeros((T + 6, NZ), F32)

    @pl.when(gy == n_gy - 1)
    def _():
        for y in (T, T + 1, T + 2):
            cond_f[pl.ds(flat_of(-3, y), T + 6, stride=STRIDE)] = jnp.zeros((T + 6, NZ), F32)

    w_east_f, w_north_f, w_above_f, diag_f, dinv_f, first_f, resid_f, e_a_f, e_b_f, d_f = (
        view(ref) for ref in (w_east, w_north, w_above, diag, dinv, first, resid, e_a, e_b, d_ext))
    top = lax.broadcasted_iota(jnp.int32, (CHUNK, NZ), 1) == NZ - 1

    def up(v):
        return pltpu.roll(v, NZ - 1, 1)

    def down(v):
        return pltpu.roll(v, 1, 1)

    def prepare(i, carry):
        f = pl.multiple_of(LO + i * CHUNK, 8)
        at = pl.ds(f, CHUNK)
        c = cond_f[at]
        g = guess_f[at]
        we = jnp.minimum(c, cond_f[pl.ds(f + STRIDE, CHUNK)])
        ww = jnp.minimum(c, cond_f[pl.ds(f - STRIDE, CHUNK)])
        wn = jnp.minimum(c, cond_f[pl.ds(f + 1, CHUNK)])
        ws = jnp.minimum(c, cond_f[pl.ds(f - 1, CHUNK)])
        wa = jnp.where(top, 0.0, jnp.minimum(c, up(c)))
        wb = down(wa)
        w_east_f[at] = we
        w_north_f[at] = wn
        w_above_f[at] = wa
        dg = screen + jnp.maximum(0.0, 1.0 - 2.0 * c) + ww + we + ws + wn + wb + wa
        diag_f[at] = dg
        total = ww * guess_f[pl.ds(f - STRIDE, CHUNK)] + we * guess_f[pl.ds(f + STRIDE, CHUNK)]
        total = total + ws * guess_f[pl.ds(f - 1, CHUNK)] + wn * guess_f[pl.ds(f + 1, CHUNK)]
        total = total + down(wa * g) + wa * up(g)
        r = right_f[at] - dg * g + total
        resid_f[at] = r
        di = relax / dg
        dinv_f[at] = di
        first_f[at] = di * r
        return carry

    lax.fori_loop(0, STEPS, prepare, 0)
    for ref in (dinv_f, first_f):
        ref[pl.ds(flat_of(-3, 32), 6)] = jnp.zeros((6, NZ), F32)
        for x in range(-2, 33):
            ref[pl.ds(flat_of(x, 34), 4)] = jnp.zeros((4, NZ), F32)
        last = flat_of(33, 34)
        ref[pl.ds(last, LO + CHUNK * STEPS - last)] = jnp.zeros((LO + CHUNK * STEPS - last, NZ), F32)

    @pl.when(gx == 0)
    def _():
        first_f[pl.ds(flat_of(-2, -4), 2 * STRIDE)] = jnp.zeros((2 * STRIDE, NZ), F32)

    @pl.when(gx == n_gx - 1)
    def _():
        first_f[pl.ds(flat_of(T, -4), 2 * STRIDE)] = jnp.zeros((2 * STRIDE, NZ), F32)

    @pl.when(gy == 0)
    def _():
        for y in (-2, -1):
            first_f[pl.ds(flat_of(-2, y), T + 4, stride=STRIDE)] = jnp.zeros((T + 4, NZ), F32)

    @pl.when(gy == n_gy - 1)
    def _():
        for y in (T, T + 1):
            first_f[pl.ds(flat_of(-2, y), T + 4, stride=STRIDE)] = jnp.zeros((T + 4, NZ), F32)

    def around(ref, f, n):
        at = pl.ds(f, n)
        v = ref[at]
        wa = w_above_f[at]
        total = w_east_f[at] * ref[pl.ds(f + STRIDE, n)]
        total = total + w_east_f[pl.ds(f - STRIDE, n)] * ref[pl.ds(f - STRIDE, n)]
        total = total + w_north_f[at] * ref[pl.ds(f + 1, n)]
        total = total + w_north_f[pl.ds(f - 1, n)] * ref[pl.ds(f - 1, n)]
        return total + wa * up(v) + down(wa * v), v

    def sweep(src, dst):
        def step(i, carry):
            f = pl.multiple_of(LO + i * CHUNK, 8)
            at = pl.ds(f, CHUNK)
            total, v = around(src, f, CHUNK)
            dst[at] = (1.0 - relax) * v + first_f[at] + dinv_f[at] * total
            return carry
        lax.fori_loop(0, STEPS, step, 0)

    send_group(1, recv_group(0), far_peer)
    sweep(first_f, e_a_f)

    loads[4].wait()
    coarse_resid = recv_group(1)
    acc = jnp.zeros((4, NZ), F32)
    for k in range(8):
        acc = acc + inverse[:, pl.ds(NZ * k, NZ)] * coarse_resid[k:k + 1]
    acc = jnp.sum(acc, axis=1, keepdims=True)
    vec = jnp.zeros((8, NZ), F32)
    base = (gx * n_gy + gy) * 4
    for i in range(4):
        vec = vec + jnp.where(node_of == base + i, acc[i:i + 1], 0.0)
    send_group(2, vec, near_peer)
    sweep(e_a_f, e_b_f)
    send_group(3, recv_group(2), far_peer)
    sweep(e_b_f, e_a_f)
    l_send[0] = row_of(e_a, 0)
    l_send[1] = row_of(e_a, T - 1)
    l_send[2] = column(e_a_f, 0)
    l_send[3] = column(e_a_f, T - 1)
    lc = [start(remote(l_send.at[s], l_recv.at[s], l_ss.at[s], l_rs.at[s], sides[s])) for s in range(4)]

    coarse = recv_group(3)

    def lookup(node):
        found = jnp.where(node_of == node, coarse, 0.0)
        return jnp.sum(jnp.sum(found, axis=0, keepdims=True), axis=1, keepdims=True)

    high = lax.broadcasted_iota(jnp.int32, (T, NZ), 0) >= BLK

    def spread(lower, upper):
        return jnp.where(high, upper, lower)

    mine = [spread(lookup(nodes[bx][0]), lookup(nodes[bx][1])) for bx in range(2)]
    for bx in range(2):
        def place(r, carry):
            d_ext[4 + BLK * bx + r, pl.ds(0, T)] = e_a[4 + BLK * bx + r, pl.ds(0, T)] + mine[bx]
            return carry
        lax.fori_loop(0, BLK, place, 0, unroll=4)
    for s in range(4):
        mc[s].wait_recv()
        lc[s].wait_recv()
    pairs = ((0, 1), (2, 3), (0, 2), (1, 3))
    beside = []
    for s in range(4):
        ids = map_recv[s]
        beside.append(spread(*(lookup(ids[p:p + 1]) for p in pairs[s])) + l_recv[s])
    d_ext[36, pl.ds(0, T)] = beside[0]
    d_ext[3, pl.ds(0, T)] = beside[1]
    d_f[pl.ds(flat_of(0, T), T, stride=STRIDE)] = beside[2]
    d_f[pl.ds(flat_of(0, -1), T, stride=STRIDE)] = beside[3]

    def apply(x, carry):
        numer, denom = carry
        f = pl.multiple_of((x + 4) * STRIDE, 8)
        total, v = around(d_f, f, T)
        im = diag_f[pl.ds(f, T)] * v - total
        image[x] = im
        return numer + resid_f[pl.ds(f, T)] * v, denom + v * im

    zero = jnp.zeros((T, NZ), F32)
    numer, denom = lax.fori_loop(0, T, apply, (zero, zero), unroll=2)
    outs = [
        pltpu.make_async_copy(d_ext.at[own], d_out, out_sem.at[0]),
        pltpu.make_async_copy(image, image_out, out_sem.at[1]),
        pltpu.make_async_copy(resid.at[own], resid_out, out_sem.at[2]),
    ]
    for copy in outs:
        copy.start()
    numer = jnp.sum(numer, axis=0, keepdims=True)
    denom = jnp.sum(denom, axis=0, keepdims=True)
    send_group(4, jnp.where(sub == 0, numer, jnp.where(sub == 1, denom, 0.0)), near_peer)
    send_group(5, recv_group(4), far_peer)
    both = jnp.sum(recv_group(5), axis=1, keepdims=True)
    alpha_out[...] = jnp.broadcast_to(both[0:1] / both[1:2], (8, NZ))

    for copy in started:
        copy.wait_send()
    for stage in range(6):
        pltpu.make_async_copy(recv.at[stage], recv.at[stage], g_ss.at[stage]).wait()
    for copy in outs:
        copy.wait()


def row_of(ref, x):
    return ref[4 + x, pl.ds(0, T)]


def body(right_side, guess, conductivity, wet_mask, coarse_map, coarse_inverse):
    tile = jax.ShapeDtypeStruct((T, T, NZ), F32)
    anywhere = pl.BlockSpec(memory_space=pl.ANY)
    field = pltpu.VMEM((ROWS, STRIDE, NZ), F32)
    dma = pltpu.SemaphoreType.DMA
    d, image, resid, alpha = pl.pallas_call(
        kernel,
        out_shape=(tile, tile, tile, jax.ShapeDtypeStruct((8, NZ), F32)),
        in_specs=[pl.BlockSpec(memory_space=pltpu.SMEM)] + [anywhere] * 5,
        out_specs=(anywhere, anywhere, anywhere, pl.BlockSpec(memory_space=pltpu.VMEM)),
        scratch_shapes=[
            pltpu.VMEM((3, ROWS, STRIDE, NZ), F32), pltpu.VMEM((T, T, NZ), jnp.int32),
        ] + [field] * 10 + [
            pltpu.VMEM((T, T, NZ), F32), pltpu.VMEM((4, NODES), F32),
            pltpu.VMEM((2, 2, T, NZ), F32), pltpu.VMEM((2, 2, T, NZ), F32),
            pltpu.VMEM((2, 6, T, NZ), F32), pltpu.VMEM((2, 6, T, NZ), F32),
            pltpu.VMEM((4, 24, NZ), F32), pltpu.VMEM((4, 24, NZ), F32),
            pltpu.VMEM((8, NZ), jnp.int32), pltpu.VMEM((4, 8, NZ), jnp.int32),
            pltpu.VMEM((4, T, NZ), F32), pltpu.VMEM((4, T, NZ), F32),
            pltpu.VMEM((6, 8, NZ), F32), pltpu.VMEM((6, GROUP - 1, 8, NZ), F32),
            dma((5,)), dma((3,)),
        ] + [dma((2,))] * 10 + [dma((4,))] * 6 + [dma((6,))] * 2,
        compiler_params=pltpu.CompilerParams(
            collective_id=0, has_side_effects=True, vmem_limit_bytes=40 * 1024 * 1024),
    )(coarse_map, coarse_inverse, right_side, guess, conductivity, wet_mask)
    step = alpha[0, 0]
    return guess + step * d, resid - step * image


def solution(mesh):
    grid = P("gx", "gy", None)
    in_specs = (grid, grid, grid, grid, grid, P(("gx", "gy"), None))
    return jax.shard_map(body, mesh=mesh, in_specs=in_specs, out_specs=(grid, grid), check_vma=False)
```

```python
import jax
import jax.numpy as jnp
from jax import lax
from jax.experimental import pallas as pl
from jax.experimental.pallas import tpu as pltpu
from jax.sharding import PartitionSpec as P

F32 = jnp.float32
MESH = pl.DeviceIdType.MESH
BLK = 16
T = 32
NZ = 128
STRIDE = 40
ROWS = 40
FLAT = ROWS * STRIDE
NODES = 1024
GROUP = 16
screen = 0.02
relax = 0.8
LO, CHUNK, STEPS = 72, 112, 13


def flat_of(x, y):
    return (x + 4) * STRIDE + y


def view(ref):
    return ref.reshape(FLAT, NZ)


def up(v):
    return pltpu.roll(v, NZ - 1, 1)


def down(v):
    return pltpu.roll(v, 1, 1)


def kernel(
    cmap, cinv, right, guess, conductivity, wet,
    d_out, image_out, resid_out, coarse_out, near_out, far_out,
    ext, mask, w_east, w_north, w_above, diag, dinv, first, e_a, e_b, d_ext, inverse,
    a_send, a_recv, b_send, b_recv, k_send, k_recv, l_send, l_recv,
    part, recv,
    load_sem, a_ss, a_rs, b_ss, b_rs, k_ss, k_rs, l_ss, l_rs, g_ss, g_rs,
):
    gx, gy = lax.axis_index("gx"), lax.axis_index("gy")
    n_gx, n_gy = lax.axis_size("gx"), lax.axis_size("gy")
    west = (lax.rem(gx + n_gx - 1, n_gx), gy)
    east = (lax.rem(gx + 1, n_gx), gy)
    south = (gx, lax.rem(gy + n_gy - 1, n_gy))
    north = (gx, lax.rem(gy + 1, n_gy))
    corners = [(px[0], py[1]) for px in (west, east) for py in (south, north)]
    sides = (west, east, south, north)
    near = gx * 2 + lax.rem(gy, 2)
    far = gy // 2

    def near_peer(k):
        j = lax.rem(near + k, GROUP)
        return (j // 2, far * 2 + lax.rem(j, 2))

    def far_peer(k):
        j = lax.rem(far + k, GROUP)
        return (gx, j * 2 + lax.rem(gy, 2))

    near_order = (8, 7, 9, 6, 10, 5, 11, 4, 12, 3, 13, 2, 14, 1, 15)
    far_order = (8, 7, 9, 6, 10, 5, 11, 4, 12, 3, 13, 2, 14, 1, 15)

    barrier = pltpu.get_barrier_semaphore()
    for peer in [far_peer(k) for k in far_order] + [near_peer(k) for k in near_order] + corners + list(sides):
        pl.semaphore_signal(barrier, inc=1, device_id=peer, device_id_type=MESH)

    own = (pl.ds(4, T), pl.ds(0, T))
    loads = [
        pltpu.make_async_copy(conductivity, ext.at[(0,) + own], load_sem.at[0]),
        pltpu.make_async_copy(wet, mask, load_sem.at[1]),
        pltpu.make_async_copy(guess, ext.at[(1,) + own], load_sem.at[2]),
        pltpu.make_async_copy(right, ext.at[(2,) + own], load_sem.at[3]),
        pltpu.make_async_copy(cinv, inverse, load_sem.at[4]),
    ]
    for copy in loads:
        copy.start()

    pad = jnp.zeros((8, NZ), F32)
    wide = jnp.zeros((STRIDE, NZ), F32)
    for a in range(3):
        for r in (0, 1, 2, 3, 36, 37, 38, 39):
            ext[a, r] = wide
        for r in range(4, 36):
            ext[a, r, pl.ds(32, 8)] = pad
    for ref in (w_east, w_north, first, e_a, e_b):
        view(ref)[pl.ds(0, LO)] = jnp.zeros((LO, NZ), F32)
        view(ref)[pl.ds(LO + CHUNK * STEPS, FLAT - LO - CHUNK * STEPS)] = jnp.zeros(
            (FLAT - LO - CHUNK * STEPS, NZ), F32)

    sub = lax.broadcasted_iota(jnp.int32, (8, NZ), 0)
    lane = lax.broadcasted_iota(jnp.int32, (8, NZ), 1)
    node_of = sub * NZ + lane
    nodes = [[cmap[bx, 0, by] for by in range(2)] for bx in range(2)]
    spot = [[8 * gx + 4 * bx + 2 * lax.rem(gy, 2) + by for by in range(2)] for bx in range(2)]
    packed = jnp.zeros((8, NZ), jnp.int32)
    for bx in range(2):
        for by in range(2):
            packed = jnp.where(sub == 2 * bx + by, nodes[bx][by], packed)
    packed = packed.astype(F32)
    started = []

    def remote(src, dst, ss, rs, peer):
        copy = pltpu.make_async_remote_copy(
            src_ref=src, dst_ref=dst, send_sem=ss, recv_sem=rs, device_id=peer, device_id_type=MESH)
        copy.start()
        started.append(copy)
        return copy

    loads[0].wait()
    loads[1].wait()

    def masked(r, carry):
        ext[0, r + 4, pl.ds(0, T)] = ext[0, r + 4, pl.ds(0, T)] * mask[r].astype(F32)
        return carry

    lax.fori_loop(0, T, masked, 0, unroll=4)
    loads[2].wait()
    cond_f, guess_f, right_f = (view(ext.at[a]) for a in range(3))
    fields = (cond_f, guess_f)

    def column(ref, y):
        return ref[pl.ds(flat_of(0, y), T, stride=STRIDE)]

    def row(ref, x):
        return ref[pl.ds(flat_of(x, 0), T)]

    def line(ref, s, n):
        at = n if s % 2 == 0 else T - 1 - n
        return row(ref, at) if s < 2 else column(ref, at)

    def put(ref, s, n, value):
        at = T + n if s % 2 == 0 else -1 - n
        if s < 2:
            ref[pl.ds(flat_of(at, 0), T)] = value
        else:
            ref[pl.ds(flat_of(0, at), T, stride=STRIDE)] = value

    for s in range(4):
        for a in range(2):
            a_send[s, a] = line(fields[a], s, 0)
    pl.semaphore_wait(barrier, 8 + 2 * (GROUP - 1))
    ac = [remote(a_send.at[s], a_recv.at[s], a_ss.at[s], a_rs.at[s], sides[s]) for s in (2, 3, 0, 1)]
    ac = [ac[2], ac[3], ac[0], ac[1]]
    loads[3].wait()
    bc = [None] * 4
    for s in (2, 3, 0, 1):
        for i in range(2):
            for a in range(2):
                b_send[s, pl.ds(T * (2 * a + i), T)] = line(fields[a], s, 1 + i)
            b_send[s, pl.ds(T * (4 + i), T)] = line(right_f, s, i)
        b_send[s, pl.ds(T * 6, 8)] = packed
        bc[s] = remote(b_send.at[s], b_recv.at[s], b_ss.at[s], b_rs.at[s], sides[s])
    kc = []
    for q in range(4):
        sx, sy = q // 2, q % 2
        x3, y3 = (0, T - 3)[sx], (0, T - 3)[sy]
        x2, y2 = (0, T - 2)[sx], (0, T - 2)[sy]
        for a in range(2):
            for i in range(3):
                k_send[q, pl.ds(9 * a + 3 * i, 3)] = fields[a][pl.ds(flat_of(x3 + i, y3), 3)]
        k_send[q, pl.ds(22, 2)] = jnp.zeros((2, NZ), F32)
        for i in range(2):
            k_send[q, pl.ds(18 + 2 * i, 2)] = right_f[pl.ds(flat_of(x2 + i, y2), 2)]
        kc.append(remote(k_send.at[q], k_recv.at[q], k_ss.at[q], k_rs.at[q], corners[q]))

    def cells(bx):
        def add(r, carry):
            acc, kd = carry
            at = pl.ds(pl.multiple_of((4 + BLK * bx + r) * STRIDE, 8), T)
            q = screen + jnp.maximum(0.0, 1.0 - 2.0 * cond_f[at])
            return acc + (right_f[at] - q * guess_f[at]), kd + q
        zero = jnp.zeros((T, NZ), F32)
        return lax.fori_loop(0, BLK, add, (zero, zero), unroll=4)

    def halves(v):
        return [v[:BLK], v[BLK:]]

    def face(c0, g0, c1, g1):
        w = jnp.minimum(c0, c1)
        return halves(w * (g0 - g1)), halves(w)

    sums, k_cell = [], []
    for bx in range(2):
        acc, kd = cells(bx)
        sums.append(halves(acc))
        k_cell.append(halves(kd))
    mid_x, mid_xw = face(row(cond_f, 15), row(guess_f, 15), row(cond_f, 16), row(guess_f, 16))
    mid_y, mid_yw = face(column(cond_f, 15), column(guess_f, 15), column(cond_f, 16), column(guess_f, 16))
    for i in range(2):
        sums[0][i] -= mid_x[i]
        sums[1][i] += mid_x[i]
        sums[i][0] -= mid_y[i]
        sums[i][1] += mid_y[i]

    def clear(ref, start, n):
        ref[pl.ds(start, n)] = jnp.zeros((n, NZ), F32)

    def clear_column(ref, x, y, n):
        ref[pl.ds(flat_of(x, y), n, stride=STRIDE)] = jnp.zeros((n, NZ), F32)

    for s in range(4):
        ac[s].wait_recv()
        for a in range(2):
            put(fields[a], s, 0, a_recv[s, a])

    @pl.when(gx == 0)
    def _():
        clear(cond_f, flat_of(-1, 0), T)

    @pl.when(gx == n_gx - 1)
    def _():
        clear(cond_f, flat_of(T, 0), T)

    @pl.when(gy == 0)
    def _():
        clear_column(cond_f, 0, -1, T)

    @pl.when(gy == n_gy - 1)
    def _():
        clear_column(cond_f, 0, T, T)

    edge_x = [face(row(cond_f, x), row(guess_f, x), row(cond_f, n), row(guess_f, n)) for x, n in ((0, -1), (T - 1, T))]
    edge_y = [face(column(cond_f, y), column(guess_f, y), column(cond_f, n), column(guess_f, n))
              for y, n in ((0, -1), (T - 1, T))]

    def totals(parts):
        found = []
        for base in range(0, len(parts), 8):
            group = parts[base:base + 8]
            stack = jnp.zeros((8, NZ), F32)
            for i, value in enumerate(group):
                stack = jnp.where(sub == i, jnp.sum(value, axis=0, keepdims=True), stack)
            stack = jnp.sum(stack, axis=1, keepdims=True)
            found += [stack[i:i + 1] for i in range(len(group))]
        return found

    blocks = [(bx, by) for bx in range(2) for by in range(2)]
    k_east = [mid_xw, edge_x[1][1]]
    k_north = [[mid_yw[bx], edge_y[1][1][bx]] for bx in range(2)]
    found = totals(
        [sums[bx][by] - edge_x[bx][0][by] - edge_y[by][0][bx] for bx, by in blocks]
        + [k_cell[bx][by] for bx, by in blocks]
        + [k_east[bx][by] for bx, by in blocks]
        + [k_north[bx][by] for bx, by in blocks])
    vec = jnp.zeros((8, NZ), F32)
    table = jnp.zeros((8, NZ), F32)
    for i, (bx, by) in enumerate(blocks):
        vec = vec + jnp.where(node_of == nodes[bx][by], found[i], 0.0)
        here = lane == spot[bx][by]
        table = jnp.where(here & (sub == 0), packed[i:i + 1], table)
        for q in range(1, 4):
            table = jnp.where(here & (sub == q), found[4 * q + i], table)

    def send_group(stage, value0, value1, peer_of, order):
        part[stage, 0] = value0
        part[stage, 1] = value1
        for k in order:
            pltpu.make_async_remote_copy(
                src_ref=part.at[stage], dst_ref=recv.at[stage, GROUP - 1 - k], send_sem=g_ss.at[stage],
                recv_sem=g_rs.at[stage], device_id=peer_of(k), device_id_type=MESH).start()

    def recv_group(stage):
        pltpu.make_async_copy(recv.at[stage], recv.at[stage], g_rs.at[stage]).wait()

    def relay(stage):
        recv_group(stage)
        both = part[stage] + jnp.sum(recv[stage], axis=0)
        send_group(stage + 1, both[0], both[1], far_peer, far_order)

    def collect(stage, table_out):
        recv_group(stage)
        table_out[pl.ds(0, GROUP - 1)] = recv[stage, :, 1]
        table_out[GROUP - 1] = part[stage, 1]
        return part[stage, 0] + jnp.sum(recv[stage, :, 0], axis=0)

    send_group(0, vec, table, near_peer, near_order)

    w_east_f, w_north_f, w_above_f, diag_f, dinv_f, first_f, e_a_f, e_b_f, d_f = (
        view(ref) for ref in (w_east, w_north, w_above, diag, dinv, first, e_a, e_b, d_ext))

    def prepare(f, n):
        at = pl.ds(f, n)
        c = cond_f[at]
        g = guess_f[at]
        we = jnp.minimum(c, cond_f[pl.ds(f + STRIDE, n)])
        ww = jnp.minimum(c, cond_f[pl.ds(f - STRIDE, n)])
        wn = jnp.minimum(c, cond_f[pl.ds(f + 1, n)])
        ws = jnp.minimum(c, cond_f[pl.ds(f - 1, n)])
        top = lax.broadcasted_iota(jnp.int32, (n, NZ), 1) == NZ - 1
        wa = jnp.where(top, 0.0, jnp.minimum(c, up(c)))
        w_east_f[at] = we
        w_north_f[at] = wn
        w_above_f[at] = wa
        dg = screen + jnp.maximum(0.0, 1.0 - 2.0 * c) + ww + we + ws + wn + down(wa) + wa
        diag_f[at] = dg
        total = ww * guess_f[pl.ds(f - STRIDE, n)] + we * guess_f[pl.ds(f + STRIDE, n)]
        total = total + ws * guess_f[pl.ds(f - 1, n)] + wn * guess_f[pl.ds(f + 1, n)]
        total = total + down(wa * g) + wa * up(g)
        r = right_f[at] - dg * g + total
        di = relax / dg
        dinv_f[at] = di
        first_f[at] = di * r
        return r

    def own_rows(x, carry):
        resid_out[x] = prepare(pl.multiple_of((x + 4) * STRIDE, 8), T)
        return carry

    lax.fori_loop(0, T, own_rows, 0, unroll=4)

    for s in (2, 3, 0, 1):
        bc[s].wait_recv()
        for i in range(2):
            for a in range(2):
                put(fields[a], s, 1 + i, b_recv[s, pl.ds(T * (2 * a + i), T)])
            put(right_f, s, i, b_recv[s, pl.ds(T * (4 + i), T)])
    for q in range(4):
        kc[q].wait_recv()
        sx, sy = q // 2, q % 2
        x3, y3 = (T, -3)[sx], (T, -3)[sy]
        x2, y2 = (T, -2)[sx], (T, -2)[sy]
        for a in range(2):
            for i in range(3):
                fields[a][pl.ds(flat_of(x3 + i, y3), 3)] = k_recv[q, pl.ds(9 * a + 3 * i, 3)]
        for i in range(2):
            right_f[pl.ds(flat_of(x2 + i, y2), 2)] = k_recv[q, pl.ds(18 + 2 * i, 2)]

    @pl.when(gx == 0)
    def _():
        clear(cond_f, flat_of(-3, -4), 3 * STRIDE)

    @pl.when(gx == n_gx - 1)
    def _():
        clear(cond_f, flat_of(T, -4), 3 * STRIDE)

    @pl.when(gy == 0)
    def _():
        for y in (-3, -2, -1):
            clear_column(cond_f, -3, y, T + 6)

    @pl.when(gy == n_gy - 1)
    def _():
        for y in (T, T + 1, T + 2):
            clear_column(cond_f, -3, y, T + 6)

    for x in (-2, -1, T, T + 1):
        prepare(flat_of(x, 0), T)

    def pads(x, carry):
        prepare(pl.multiple_of((x + 1) * STRIDE + T, 8), 8)
        return carry

    lax.fori_loop(0, 37, pads, 0, unroll=4)
    for ref in (dinv_f, first_f):
        clear(ref, flat_of(-3, 32), 6)
        for x in range(-2, 33):
            clear(ref, flat_of(x, 34), 4)
        last = flat_of(33, 34)
        clear(ref, last, LO + CHUNK * STEPS - last)
    for ref in (w_east_f, w_north_f, w_above_f):
        clear(ref, flat_of(34, 0), LO + CHUNK * STEPS - flat_of(34, 0))

    @pl.when(gx == 0)
    def _():
        clear(first_f, flat_of(-2, -4), 2 * STRIDE)

    @pl.when(gx == n_gx - 1)
    def _():
        clear(first_f, flat_of(T, -4), 2 * STRIDE)

    @pl.when(gy == 0)
    def _():
        for y in (-2, -1):
            clear_column(first_f, -2, y, T + 4)

    @pl.when(gy == n_gy - 1)
    def _():
        for y in (T, T + 1):
            clear_column(first_f, -2, y, T + 4)

    def around(ref, f, n):
        at = pl.ds(f, n)
        v = ref[at]
        wa = w_above_f[at]
        total = w_east_f[at] * ref[pl.ds(f + STRIDE, n)]
        total = total + w_east_f[pl.ds(f - STRIDE, n)] * ref[pl.ds(f - STRIDE, n)]
        total = total + w_north_f[at] * ref[pl.ds(f + 1, n)]
        total = total + w_north_f[pl.ds(f - 1, n)] * ref[pl.ds(f - 1, n)]
        return total + wa * up(v) + down(wa * v), v

    def relaxed(src, dst, f, n):
        at = pl.ds(f, n)
        total, v = around(src, f, n)
        dst[at] = (1.0 - relax) * v + first_f[at] + dinv_f[at] * total

    def sweep(src, dst):
        def step(i, carry):
            relaxed(src, dst, pl.multiple_of(LO + i * CHUNK, 8), CHUNK)
            return carry
        lax.fori_loop(0, STEPS, step, 0)

    sweep(first_f, e_a_f)
    relay(0)
    sweep(e_a_f, e_b_f)

    def last_sweep(x, carry):
        relaxed(e_b_f, e_a_f, pl.multiple_of((x + 4) * STRIDE, 8), T)
        return carry

    lax.fori_loop(0, T, last_sweep, 0, unroll=4)
    lc = []
    for s in range(4):
        l_send[s] = line(e_a_f, s, 0)
        lc.append(remote(l_send.at[s], l_recv.at[s], l_ss.at[s], l_rs.at[s], sides[s]))

    coarse_resid = collect(1, near_out)
    coarse_out[1] = coarse_resid
    loads[4].wait()
    acc = jnp.zeros((4, NZ), F32)
    for k in range(8):
        acc = acc + inverse[:, pl.ds(NZ * k, NZ)] * coarse_resid[k:k + 1]
    acc = jnp.sum(acc, axis=1, keepdims=True)
    vec = jnp.zeros((8, NZ), F32)
    base = (gx * n_gy + gy) * 4
    for i in range(4):
        vec = vec + jnp.where(node_of == base + i, acc[i:i + 1], 0.0)

    for s in range(4):
        lc[s].wait_recv()
        put(e_a_f, s, 0, l_recv[s])

    def products(bx):
        def add(r, carry):
            al, lal, rl = carry
            x = BLK * bx + r
            f = pl.multiple_of((x + 4) * STRIDE, 8)
            total, v = around(e_a_f, f, T)
            im = diag_f[pl.ds(f, T)] * v - total
            return al + im, lal + v * im, rl + v * resid_out[x]
        zero = jnp.zeros((T, NZ), F32)
        return [halves(v) for v in lax.fori_loop(0, BLK, add, (zero, zero, zero), unroll=4)]

    sums = [products(0), products(1)]
    found = totals([sums[bx][q][by] for q in range(3) for bx, by in blocks])
    table = jnp.zeros((8, NZ), F32)
    for i, (bx, by) in enumerate(blocks):
        for q in range(3):
            table = jnp.where((lane == spot[bx][by]) & (sub == q), found[4 * q + i], table)
    send_group(2, vec, table, near_peer, near_order)
    relay(2)
    coarse = collect(3, far_out)
    coarse_out[0] = coarse

    def lookup(node):
        hit = jnp.where(node_of == node, coarse, 0.0)
        return jnp.sum(jnp.sum(hit, axis=0, keepdims=True), axis=1, keepdims=True)

    high = lax.broadcasted_iota(jnp.int32, (T, NZ), 0) >= BLK

    def spread(lower, upper):
        return jnp.where(high, upper, lower)

    for bx in range(2):
        mine = spread(lookup(nodes[bx][0]), lookup(nodes[bx][1]))

        def place(r, carry):
            x = BLK * bx + r
            v = e_a[4 + x, pl.ds(0, T)] + mine
            d_ext[4 + x, pl.ds(0, T)] = v
            d_out[x] = v
            return carry

        lax.fori_loop(0, BLK, place, 0, unroll=4)
    pairs = ((0, 1), (2, 3), (0, 2), (1, 3))
    for s in range(4):
        ids = b_recv[s, pl.ds(T * 6, 8)].astype(jnp.int32)
        put(d_f, s, 0, spread(*(lookup(ids[p:p + 1]) for p in pairs[s])) + l_recv[s])

    def apply(x, carry):
        f = pl.multiple_of((x + 4) * STRIDE, 8)
        total, v = around(d_f, f, T)
        image_out[x] = diag_f[pl.ds(f, T)] * v - total
        return carry

    lax.fori_loop(0, T, apply, 0, unroll=4)
    for copy in started:
        copy.wait_send()
    for stage in range(4):
        pltpu.make_async_copy(recv.at[stage], recv.at[stage], g_ss.at[stage]).wait()


def finish(d, image, resid, coarse, near, far, guess, pressure, residual, guess_v, press_v, resid_v, load_sem, out_sem):
    load = pltpu.make_async_copy(guess, guess_v, load_sem)
    load.start()
    near_f, far_f = near.reshape(GROUP * 8, NZ), far.reshape(GROUP * 8, NZ)

    def pick(ref, q):
        return ref[pl.ds(q, GROUP, stride=8)]

    c = coarse[0]
    node = pick(near_f, 0).astype(jnp.int32)
    at_sub, at_lane = node // NZ, lax.rem(node, NZ)
    block = jnp.zeros((GROUP, NZ), F32)
    for s in range(8):
        line = jnp.broadcast_to(c[s:s + 1], (GROUP, NZ))
        hit = jnp.take_along_axis(line, at_lane, axis=1, mode="promise_in_bounds")
        block = jnp.where(at_sub == s, hit, block)
    east = pltpu.roll(block, NZ - 4, 1)
    lane = lax.broadcasted_iota(jnp.int32, (GROUP, NZ), 1)
    north = jnp.where(lax.rem(lane, 4) == 3, pltpu.roll(pltpu.roll(block, 3, 1), GROUP - 1, 0),
                      pltpu.roll(block, NZ - 1, 1))
    to_east, to_north = block - east, block - north
    numer = pick(far_f, 2)
    denom = (pick(far_f, 1) + 2.0 * block * pick(far_f, 0) + pick(near_f, 1) * block * block
             + pick(near_f, 2) * to_east * to_east + pick(near_f, 3) * to_north * to_north)

    def total(v):
        return jnp.sum(jnp.sum(v, axis=0, keepdims=True), axis=1, keepdims=True)

    step = (total(numer) + total(c * coarse[1])) / total(denom)
    load.wait()
    copies = []
    for part in range(4):
        rows = pl.ds(8 * part, 8)
        press_v[rows] = guess_v[rows] + step * d[rows]
        resid_v[rows] = resid[rows] - step * image[rows]
        copies.append(pltpu.make_async_copy(press_v.at[rows], pressure.at[rows], out_sem.at[2 * part]))
        copies.append(pltpu.make_async_copy(resid_v.at[rows], residual.at[rows], out_sem.at[2 * part + 1]))
        copies[-2].start()
        copies[-1].start()
    for copy in copies:
        copy.wait()


def body(right_side, guess, conductivity, wet_mask, coarse_map, coarse_inverse):
    tile = jax.ShapeDtypeStruct((T, T, NZ), F32)
    table = jax.ShapeDtypeStruct((GROUP, 8, NZ), F32)
    hbm = pl.BlockSpec(memory_space=pltpu.HBM)
    vmem = pl.BlockSpec(memory_space=pltpu.VMEM)
    field = pltpu.VMEM((ROWS, STRIDE, NZ), F32)
    dma = pltpu.SemaphoreType.DMA
    state = pl.pallas_call(
        kernel,
        out_shape=(tile, tile, tile, jax.ShapeDtypeStruct((2, 8, NZ), F32), table, table),
        in_specs=[pl.BlockSpec(memory_space=pltpu.SMEM)] + [hbm] * 5,
        out_specs=(vmem,) * 6,
        scratch_shapes=[
            pltpu.VMEM((3, ROWS, STRIDE, NZ), F32), pltpu.VMEM((T, T, NZ), jnp.int32),
        ] + [field] * 9 + [
            pltpu.VMEM((4, NODES), F32),
            pltpu.VMEM((4, 2, T, NZ), F32), pltpu.VMEM((4, 2, T, NZ), F32),
            pltpu.VMEM((4, 6 * T + 8, NZ), F32), pltpu.VMEM((4, 6 * T + 8, NZ), F32),
            pltpu.VMEM((4, 24, NZ), F32), pltpu.VMEM((4, 24, NZ), F32),
            pltpu.VMEM((4, T, NZ), F32), pltpu.VMEM((4, T, NZ), F32),
            pltpu.VMEM((4, 2, 8, NZ), F32), pltpu.VMEM((4, GROUP - 1, 2, 8, NZ), F32),
            dma((5,)),
        ] + [dma((4,))] * 10,
        compiler_params=pltpu.CompilerParams(
            collective_id=0, has_side_effects=True, vmem_limit_bytes=40 * 1024 * 1024),
    )(*(pltpu.with_memory_space_constraint(array, pltpu.HBM) for array in (
        coarse_map.transpose(0, 2, 1), coarse_inverse, right_side, guess, conductivity, wet_mask)))
    return pl.pallas_call(
        finish,
        out_shape=(tile, tile),
        in_specs=[vmem] * 6 + [hbm],
        out_specs=(hbm, hbm),
        scratch_shapes=[pltpu.VMEM((T, T, NZ), F32)] * 3 + [dma, dma((8,))],
        compiler_params=pltpu.CompilerParams(vmem_limit_bytes=16 * 1024 * 1024),
    )(*state, pltpu.with_memory_space_constraint(guess, pltpu.HBM))


def solution(mesh):
    grid = P("gx", "gy", None)
    in_specs = (grid, grid, grid, grid, grid, P(("gx", "gy"), None))
    return jax.shard_map(body, mesh=mesh, in_specs=in_specs, out_specs=(grid, grid), check_vma=False)
```

```python
import jax
import jax.numpy as jnp
from jax import lax
from jax.experimental import pallas as pl
from jax.experimental.pallas import tpu as pltpu
from jax.sharding import PartitionSpec as P

F32 = jnp.float32
MESH = pl.DeviceIdType.MESH
BLK = 16
T = 32
NZ = 128
STRIDE = 40
ROWS = 40
FLAT = ROWS * STRIDE
NODES = 1024
GROUP = 16
screen = 0.02
relax = 0.8
LO, CHUNK, STEPS = 72, 112, 13


def flat_of(x, y):
    return (x + 4) * STRIDE + y


def view(ref):
    return ref.reshape(FLAT, NZ)


def up(v):
    return pltpu.roll(v, NZ - 1, 1)


def down(v):
    return pltpu.roll(v, 1, 1)


def kernel(
    cmap, cinv, right, guess, conductivity, wet,
    l_out, image_out, resid_out, q_out, faces_out, coarse_out, near_out, far_out,
    ext, mask, w_east, w_north, w_above, diag, dinv, first, e_a, e_b, e_c, inverse,
    a_send, a_recv, b_send, b_recv, k_send, k_recv, l_send, l_recv,
    part, recv,
    load_sem, a_ss, a_rs, b_ss, b_rs, k_ss, k_rs, l_ss, l_rs, g_ss, g_rs,
):
    gx, gy = lax.axis_index("gx"), lax.axis_index("gy")
    n_gx, n_gy = lax.axis_size("gx"), lax.axis_size("gy")
    west = (lax.rem(gx + n_gx - 1, n_gx), gy)
    east = (lax.rem(gx + 1, n_gx), gy)
    south = (gx, lax.rem(gy + n_gy - 1, n_gy))
    north = (gx, lax.rem(gy + 1, n_gy))
    corners = [(px[0], py[1]) for px in (west, east) for py in (south, north)]
    sides = (west, east, south, north)
    near = gx * 2 + lax.rem(gy, 2)
    far = gy // 2

    def near_peer(k):
        j = lax.rem(near + k, GROUP)
        return (j // 2, far * 2 + lax.rem(j, 2))

    def far_peer(k):
        j = lax.rem(far + k, GROUP)
        return (gx, j * 2 + lax.rem(gy, 2))

    near_order = (8, 7, 9, 6, 10, 5, 11, 4, 12, 3, 13, 2, 14, 1, 15)
    far_order = (8, 7, 9, 6, 10, 5, 11, 4, 12, 3, 13, 2, 14, 1, 15)

    own = (pl.ds(4, T), pl.ds(0, T))
    loads = [
        pltpu.make_async_copy(conductivity, ext.at[(0,) + own], load_sem.at[0]),
        pltpu.make_async_copy(wet, mask, load_sem.at[1]),
        pltpu.make_async_copy(guess, ext.at[(1,) + own], load_sem.at[2]),
        pltpu.make_async_copy(right, ext.at[(2,) + own], load_sem.at[3]),
        pltpu.make_async_copy(cinv, inverse, load_sem.at[4]),
    ]
    for copy in loads:
        copy.start()

    barrier = pltpu.get_barrier_semaphore()
    for peer in [far_peer(k) for k in far_order] + [near_peer(k) for k in near_order] + corners + list(sides):
        pl.semaphore_signal(barrier, inc=1, device_id=peer, device_id_type=MESH)

    pad = jnp.zeros((8, NZ), F32)
    wide = jnp.zeros((STRIDE, NZ), F32)
    for ref in [ext.at[a] for a in range(3)] + [w_east, w_north, w_above, dinv, first]:
        for r in (0, 1, 2, 3, 36, 37, 38, 39):
            ref[r] = wide
        for r in range(4, 36):
            ref[r, pl.ds(32, 8)] = pad
    for ref in (e_a, e_b):
        view(ref)[pl.ds(0, LO)] = jnp.zeros((LO, NZ), F32)
        view(ref)[pl.ds(LO + CHUNK * STEPS, FLAT - LO - CHUNK * STEPS)] = jnp.zeros(
            (FLAT - LO - CHUNK * STEPS, NZ), F32)
    for r in (3, 36):
        e_c[r] = wide
    for r in range(4, 36):
        e_c[r, pl.ds(32, 8)] = pad

    sub = lax.broadcasted_iota(jnp.int32, (8, NZ), 0)
    lane = lax.broadcasted_iota(jnp.int32, (8, NZ), 1)
    node_of = sub * NZ + lane
    nodes = [[cmap[bx, 0, by] for by in range(2)] for bx in range(2)]
    spot = [[8 * gx + 4 * bx + 2 * lax.rem(gy, 2) + by for by in range(2)] for bx in range(2)]
    packed = jnp.zeros((8, NZ), jnp.int32)
    for bx in range(2):
        for by in range(2):
            packed = jnp.where(sub == 2 * bx + by, nodes[bx][by], packed)
    packed = packed.astype(F32)
    started = []

    def remote(src, dst, ss, rs, peer):
        copy = pltpu.make_async_remote_copy(
            src_ref=src, dst_ref=dst, send_sem=ss, recv_sem=rs, device_id=peer, device_id_type=MESH)
        copy.start()
        started.append(copy)
        return copy

    loads[0].wait()
    loads[1].wait()

    def masked(r, carry):
        ext[0, r + 4, pl.ds(0, T)] = ext[0, r + 4, pl.ds(0, T)] * mask[r].astype(F32)
        return carry

    lax.fori_loop(0, T, masked, 0, unroll=4)
    loads[2].wait()
    cond_f, guess_f, right_f = (view(ext.at[a]) for a in range(3))
    fields = (cond_f, guess_f)

    def column(ref, y):
        return ref[pl.ds(flat_of(0, y), T, stride=STRIDE)]

    def row(ref, x):
        return ref[pl.ds(flat_of(x, 0), T)]

    def line(ref, s, n):
        at = n if s % 2 == 0 else T - 1 - n
        return row(ref, at) if s < 2 else column(ref, at)

    def put(ref, s, n, value):
        at = T + n if s % 2 == 0 else -1 - n
        if s < 2:
            ref[pl.ds(flat_of(at, 0), T)] = value
        else:
            ref[pl.ds(flat_of(0, at), T, stride=STRIDE)] = value

    for s in range(4):
        for a in range(2):
            a_send[s, a] = line(fields[a], s, 0)
    pl.semaphore_wait(barrier, 8 + 2 * (GROUP - 1))
    ac = [remote(a_send.at[s], a_recv.at[s], a_ss.at[s], a_rs.at[s], sides[s]) for s in (2, 3, 0, 1)]
    ac = [ac[2], ac[3], ac[0], ac[1]]
    loads[3].wait()
    bc = [None] * 4
    for s in (2, 3, 0, 1):
        for i in range(2):
            for a in range(2):
                b_send[s, pl.ds(T * (2 * a + i), T)] = line(fields[a], s, 1 + i)
            b_send[s, pl.ds(T * (4 + i), T)] = line(right_f, s, i)
        b_send[s, pl.ds(T * 6, 8)] = packed
        bc[s] = remote(b_send.at[s], b_recv.at[s], b_ss.at[s], b_rs.at[s], sides[s])
    kc = []
    for q in range(4):
        sx, sy = q // 2, q % 2
        x3, y3 = (0, T - 3)[sx], (0, T - 3)[sy]
        x2, y2 = (0, T - 2)[sx], (0, T - 2)[sy]
        for a in range(2):
            for i in range(3):
                k_send[q, pl.ds(9 * a + 3 * i, 3)] = fields[a][pl.ds(flat_of(x3 + i, y3), 3)]
        k_send[q, pl.ds(22, 2)] = jnp.zeros((2, NZ), F32)
        for i in range(2):
            k_send[q, pl.ds(18 + 2 * i, 2)] = right_f[pl.ds(flat_of(x2 + i, y2), 2)]
        kc.append(remote(k_send.at[q], k_recv.at[q], k_ss.at[q], k_rs.at[q], corners[q]))

    w_east_f, w_north_f, w_above_f, diag_f, dinv_f, first_f, e_a_f, e_b_f, e_c_f = (
        view(ref) for ref in (w_east, w_north, w_above, diag, dinv, first, e_a, e_b, e_c))
    resid_f, image_f = (ref.reshape(T * T, NZ) for ref in (resid_out, image_out))

    def prepare(f, n, stride):
        def at(shift=0):
            return pl.ds(f + shift, n) if stride == 1 else pl.ds(f + shift, n, stride=stride)
        c = cond_f[at()]
        g = guess_f[at()]
        we = jnp.minimum(c, cond_f[at(STRIDE)])
        ww = jnp.minimum(c, cond_f[at(-STRIDE)])
        wn = jnp.minimum(c, cond_f[at(1)])
        ws = jnp.minimum(c, cond_f[at(-1)])
        top = lax.broadcasted_iota(jnp.int32, (n, NZ), 1) == NZ - 1
        wa = jnp.where(top, 0.0, jnp.minimum(c, up(c)))
        w_east_f[at()] = we
        w_north_f[at()] = wn
        w_above_f[at()] = wa
        dg = screen + jnp.maximum(0.0, 1.0 - 2.0 * c) + ww + we + ws + wn + down(wa) + wa
        diag_f[at()] = dg
        total = ww * guess_f[at(-STRIDE)] + we * guess_f[at(STRIDE)]
        total = total + ws * guess_f[at(-1)] + wn * guess_f[at(1)]
        total = total + down(wa * g) + wa * up(g)
        r = right_f[at()] - dg * g + total
        di = relax / dg
        dinv_f[at()] = di
        first_f[at()] = di * r
        return r

    def own_rows(x, carry):
        resid_out[x] = prepare(pl.multiple_of((x + 4) * STRIDE, 8), T, 1)
        return carry

    lax.fori_loop(0, T, own_rows, 0, unroll=4)

    def cells(bx):
        def add(r, carry):
            acc, kd = carry
            at = pl.ds(pl.multiple_of((4 + BLK * bx + r) * STRIDE, 8), T)
            q = screen + jnp.maximum(0.0, 1.0 - 2.0 * cond_f[at])
            q_out[BLK * bx + r] = q
            return acc + (right_f[at] - q * guess_f[at]), kd + q
        zero = jnp.zeros((T, NZ), F32)
        return lax.fori_loop(0, BLK, add, (zero, zero), unroll=4)

    def halves(v):
        return [v[:BLK], v[BLK:]]

    def face(c0, g0, c1, g1):
        w = jnp.minimum(c0, c1)
        return halves(w * (g0 - g1)), w

    sums, k_cell = [], []
    for bx in range(2):
        acc, kd = cells(bx)
        sums.append(halves(acc))
        k_cell.append(halves(kd))
    mid_x, mid_xw = face(row(cond_f, 15), row(guess_f, 15), row(cond_f, 16), row(guess_f, 16))
    mid_y, mid_yw = face(column(cond_f, 15), column(guess_f, 15), column(cond_f, 16), column(guess_f, 16))
    for i in range(2):
        sums[0][i] -= mid_x[i]
        sums[1][i] += mid_x[i]
        sums[i][0] -= mid_y[i]
        sums[i][1] += mid_y[i]

    def clear(ref, start, n):
        ref[pl.ds(start, n)] = jnp.zeros((n, NZ), F32)

    def clear_column(ref, x, y, n):
        ref[pl.ds(flat_of(x, y), n, stride=STRIDE)] = jnp.zeros((n, NZ), F32)

    for s in range(4):
        ac[s].wait_recv()
        for a in range(2):
            put(fields[a], s, 0, a_recv[s, a])

    @pl.when(gx == 0)
    def _():
        clear(cond_f, flat_of(-1, 0), T)

    @pl.when(gx == n_gx - 1)
    def _():
        clear(cond_f, flat_of(T, 0), T)

    @pl.when(gy == 0)
    def _():
        clear_column(cond_f, 0, -1, T)

    @pl.when(gy == n_gy - 1)
    def _():
        clear_column(cond_f, 0, T, T)

    edge_x = [face(row(cond_f, x), row(guess_f, x), row(cond_f, n), row(guess_f, n)) for x, n in ((0, -1), (T - 1, T))]
    edge_y = [face(column(cond_f, y), column(guess_f, y), column(cond_f, n), column(guess_f, n))
              for y, n in ((0, -1), (T - 1, T))]

    def totals(parts):
        found = []
        for base in range(0, len(parts), 8):
            group = parts[base:base + 8]
            stack = jnp.zeros((8, NZ), F32)
            for i, value in enumerate(group):
                stack = jnp.where(sub == i, jnp.sum(value, axis=0, keepdims=True), stack)
            stack = jnp.sum(stack, axis=1, keepdims=True)
            found += [stack[i:i + 1] for i in range(len(group))]
        return found

    blocks = [(bx, by) for bx in range(2) for by in range(2)]
    w_side = [edge_x[0][1], edge_x[1][1], edge_y[0][1], edge_y[1][1]]
    for i, w in enumerate((w_side[0], mid_xw, w_side[1], w_side[2], mid_yw, w_side[3])):
        faces_out[i] = w
    k_east = [halves(mid_xw), halves(w_side[1])]
    k_north = [[halves(mid_yw)[bx], halves(w_side[3])[bx]] for bx in range(2)]
    found = totals(
        [sums[bx][by] - edge_x[bx][0][by] - edge_y[by][0][bx] for bx, by in blocks]
        + [k_cell[bx][by] for bx, by in blocks]
        + [k_east[bx][by] for bx, by in blocks]
        + [k_north[bx][by] for bx, by in blocks])
    vec = jnp.zeros((8, NZ), F32)
    table = jnp.zeros((8, NZ), F32)
    for i, (bx, by) in enumerate(blocks):
        vec = vec + jnp.where(node_of == nodes[bx][by], found[i], 0.0)
        here = lane == spot[bx][by]
        table = jnp.where(here & (sub == 0), packed[i:i + 1], table)
        for q in range(1, 4):
            table = jnp.where(here & (sub == q), found[4 * q + i], table)

    def send_group(stage, value0, value1, peer_of, order):
        part[stage, 0] = value0
        part[stage, 1] = value1
        for k in order:
            pltpu.make_async_remote_copy(
                src_ref=part.at[stage], dst_ref=recv.at[stage, GROUP - 1 - k], send_sem=g_ss.at[stage],
                recv_sem=g_rs.at[stage], device_id=peer_of(k), device_id_type=MESH).start()

    def recv_group(stage):
        pltpu.make_async_copy(recv.at[stage], recv.at[stage], g_rs.at[stage]).wait()

    def sent(stage):
        pltpu.make_async_copy(recv.at[stage], recv.at[stage], g_ss.at[stage]).wait()

    def relay(stage):
        recv_group(stage)
        both = part[stage] + jnp.sum(recv[stage], axis=0)
        send_group(stage + 1, both[0], both[1], far_peer, far_order)

    def collect(stage, table_out):
        recv_group(stage)
        table_out[pl.ds(0, GROUP - 1)] = recv[stage, :, 1]
        table_out[GROUP - 1] = part[stage, 1]
        return part[stage, 0] + jnp.sum(recv[stage, :, 0], axis=0)

    send_group(0, vec, table, near_peer, near_order)

    for x in (0, T - 1):
        resid_f[pl.ds(T * x, T)] = prepare(flat_of(x, 0), T, 1)
    for y in (0, T - 1):
        resid_f[pl.ds(y, T, stride=T)] = prepare(flat_of(0, y), T, STRIDE)

    for s in (2, 3, 0, 1):
        bc[s].wait_recv()
        for i in range(2):
            for a in range(2):
                put(fields[a], s, 1 + i, b_recv[s, pl.ds(T * (2 * a + i), T)])
            put(right_f, s, i, b_recv[s, pl.ds(T * (4 + i), T)])
    for q in range(4):
        kc[q].wait_recv()
        sx, sy = q // 2, q % 2
        x3, y3 = (T, -3)[sx], (T, -3)[sy]
        x2, y2 = (T, -2)[sx], (T, -2)[sy]
        for a in range(2):
            for i in range(3):
                fields[a][pl.ds(flat_of(x3 + i, y3), 3)] = k_recv[q, pl.ds(9 * a + 3 * i, 3)]
        for i in range(2):
            right_f[pl.ds(flat_of(x2 + i, y2), 2)] = k_recv[q, pl.ds(18 + 2 * i, 2)]

    @pl.when(gx == 0)
    def _():
        clear(cond_f, flat_of(-3, -4), 3 * STRIDE)

    @pl.when(gx == n_gx - 1)
    def _():
        clear(cond_f, flat_of(T, -4), 3 * STRIDE)

    @pl.when(gy == 0)
    def _():
        for y in (-3, -2, -1):
            clear_column(cond_f, -3, y, T + 6)

    @pl.when(gy == n_gy - 1)
    def _():
        for y in (T, T + 1, T + 2):
            clear_column(cond_f, -3, y, T + 6)

    for x in (-2, -1, T, T + 1):
        prepare(flat_of(x, 0), T, 1)
    for y in (-2, -1, T, T + 1):
        prepare(flat_of(-2, y), T + 4, STRIDE)

    @pl.when(gx == 0)
    def _():
        clear(first_f, flat_of(-2, -4), 2 * STRIDE)

    @pl.when(gx == n_gx - 1)
    def _():
        clear(first_f, flat_of(T, -4), 2 * STRIDE)

    @pl.when(gy == 0)
    def _():
        for y in (-2, -1):
            clear_column(first_f, -2, y, T + 4)

    @pl.when(gy == n_gy - 1)
    def _():
        for y in (T, T + 1):
            clear_column(first_f, -2, y, T + 4)

    def around(ref, f, n):
        at = pl.ds(f, n)
        v = ref[at]
        wa = w_above_f[at]
        total = w_east_f[at] * ref[pl.ds(f + STRIDE, n)]
        total = total + w_east_f[pl.ds(f - STRIDE, n)] * ref[pl.ds(f - STRIDE, n)]
        total = total + w_north_f[at] * ref[pl.ds(f + 1, n)]
        total = total + w_north_f[pl.ds(f - 1, n)] * ref[pl.ds(f - 1, n)]
        return total + wa * up(v) + down(wa * v), v

    def relaxed(src, dst, f, n):
        at = pl.ds(f, n)
        total, v = around(src, f, n)
        dst[at] = (1.0 - relax) * v + first_f[at] + dinv_f[at] * total

    def sweep(src, dst):
        def step(i, carry):
            relaxed(src, dst, pl.multiple_of(LO + i * CHUNK, 8), CHUNK)
            return carry
        lax.fori_loop(0, STEPS, step, 0)

    sweep(first_f, e_a_f)
    relay(0)
    sweep(e_a_f, e_b_f)

    def last_sweep(x, carry):
        relaxed(e_b_f, e_c_f, pl.multiple_of((x + 4) * STRIDE, 8), T)
        return carry

    lax.fori_loop(0, T, last_sweep, 0, unroll=4)
    lc = []
    for s in range(4):
        l_send[s] = line(e_c_f, s, 0)
        lc.append(remote(l_send.at[s], l_recv.at[s], l_ss.at[s], l_rs.at[s], sides[s]))

    def products(bx):
        def add(r, carry):
            al, lal, rl = carry
            x = BLK * bx + r
            f = pl.multiple_of((x + 4) * STRIDE, 8)
            total, v = around(e_c_f, f, T)
            im = diag_f[pl.ds(f, T)] * v - total
            image_out[x] = im
            l_out[x] = v
            return al + im, lal + v * im, rl + v * resid_out[x]
        zero = jnp.zeros((T, NZ), F32)
        return [halves(v) for v in lax.fori_loop(0, BLK, add, (zero, zero, zero), unroll=4)]

    sums = [products(0), products(1)]

    coarse_resid = collect(1, near_out)
    coarse_out[1] = coarse_resid
    loads[4].wait()
    acc = jnp.zeros((4, NZ), F32)
    for k in range(8):
        acc = acc + inverse[:, pl.ds(NZ * k, NZ)] * coarse_resid[k:k + 1]
    acc = jnp.sum(acc, axis=1, keepdims=True)
    vec = jnp.zeros((8, NZ), F32)
    base = (gx * n_gy + gy) * 4
    for i in range(4):
        vec = vec + jnp.where(node_of == base + i, acc[i:i + 1], 0.0)

    for copy in lc:
        copy.wait_recv()
    for s in range(4):
        out = w_side[s] * l_recv[s ^ 1]
        lost = halves(out), halves(out * l_send[s])
        for i in range(2):
            bx, by = (s % 2, i) if s < 2 else (i, s % 2)
            for q in range(2):
                sums[bx][q][by] -= lost[q][i]
        at = pl.ds((T - 1) * T * (s % 2), T) if s < 2 else pl.ds((T - 1) * (s % 2), T, stride=T)
        image_f[at] -= out

    found = totals([sums[bx][q][by] for q in range(3) for bx, by in blocks])
    table = jnp.zeros((8, NZ), F32)
    for i, (bx, by) in enumerate(blocks):
        for q in range(3):
            table = jnp.where((lane == spot[bx][by]) & (sub == q), found[4 * q + i], table)
    send_group(2, vec, table, near_peer, near_order)
    relay(2)
    for copy in started:
        copy.wait_send()
    for stage in range(3):
        sent(stage)
    coarse_out[0] = collect(3, far_out)
    sent(3)


def finish(l, image, resid, q, faces, coarse, near, far, guess, pressure, residual, guess_v, press_v, resid_v, load_sem, out_sem):
    load = pltpu.make_async_copy(guess, guess_v, load_sem)
    load.start()
    gx, gy = lax.axis_index("gx"), lax.axis_index("gy")
    near_f, far_f = near.reshape(GROUP * 8, NZ), far.reshape(GROUP * 8, NZ)

    def pick(ref, i):
        return ref[pl.ds(i, GROUP, stride=8)]

    c = coarse[0]
    node = pick(near_f, 0).astype(jnp.int32)
    at_sub, at_lane = node // NZ, lax.rem(node, NZ)
    block = jnp.zeros((GROUP, NZ), F32)
    for s in range(8):
        line = jnp.broadcast_to(c[s:s + 1], (GROUP, NZ))
        hit = jnp.take_along_axis(line, at_lane, axis=1, mode="promise_in_bounds")
        block = jnp.where(at_sub == s, hit, block)
    east = pltpu.roll(block, NZ - 4, 1)
    lane = lax.broadcasted_iota(jnp.int32, (GROUP, NZ), 1)
    north = jnp.where(lax.rem(lane, 4) == 3, pltpu.roll(pltpu.roll(block, 3, 1), GROUP - 1, 0),
                      pltpu.roll(block, NZ - 1, 1))
    to_east, to_north = block - east, block - north
    numer = pick(far_f, 2)
    denom = (pick(far_f, 1) + 2.0 * block * pick(far_f, 0) + pick(near_f, 1) * block * block
             + pick(near_f, 2) * to_east * to_east + pick(near_f, 3) * to_north * to_north)

    def total(v):
        return jnp.sum(jnp.sum(v, axis=0, keepdims=True), axis=1, keepdims=True)

    step = (total(numer) + total(c * coarse[1])) / total(denom)
    odd = lax.rem(gy, 2)
    turn = lax.rem(NZ - 8 * gx - 2 * odd, NZ)
    block, to_east, to_north = (pltpu.roll(v, turn, 1) for v in (block, to_east, to_north))

    def value(v, slot, at):
        return v[slot:slot + 1, at % NZ:at % NZ + 1]

    high = lax.broadcasted_iota(jnp.int32, (T, NZ), 0) >= BLK

    def spread(lower, upper):
        return step * jnp.where(high, upper, lower)

    last = GROUP - 1
    mine = [spread(value(block, last, 4 * bx), value(block, last, 4 * bx + 1)) for bx in range(2)]
    flux_x = [faces[i] * spread(value(to_east, last, 4 * (i - 1)), value(to_east, last, 4 * (i - 1) + 1))
              for i in range(3)]
    below = [jnp.where(odd == 1, value(to_north, last, 4 * bx - 1), value(to_north, last - 1, 4 * bx + 3))
             for bx in range(2)]
    flux_y = [faces[3] * spread(*below)] + [
        faces[3 + i] * spread(value(to_north, last, i - 1), value(to_north, last, 4 + i - 1)) for i in (1, 2)]
    flat = resid_v.reshape(T * T, NZ)
    load.wait()
    copies = []
    for part in range(4):
        rows = pl.ds(8 * part, 8)
        add = mine[part // 2]
        press_v[rows] = guess_v[rows] + step * l[rows] + add
        copies.append(pltpu.make_async_copy(press_v.at[rows], pressure.at[rows], out_sem.at[2 * part]))
        copies[-1].start()
        resid_v[rows] = resid[rows] - step * image[rows] - q[rows] * add
        if part == 0:
            resid_v[0] += flux_x[0]
        elif part == 1:
            resid_v[15] -= flux_x[1]
        elif part == 2:
            resid_v[16] += flux_x[1]
        else:
            resid_v[31] -= flux_x[2]
        some = slice(8 * part, 8 * part + 8)
        for y, i, sign in ((0, 0, 1.0), (15, 1, -1.0), (16, 1, 1.0), (31, 2, -1.0)):
            flat[pl.ds(8 * part * T + y, 8, stride=T)] += sign * flux_y[i][some]
        copies.append(pltpu.make_async_copy(resid_v.at[rows], residual.at[rows], out_sem.at[2 * part + 1]))
        copies[-1].start()
    for copy in copies:
        copy.wait()


def body(right_side, guess, conductivity, wet_mask, coarse_map, coarse_inverse):
    tile = jax.ShapeDtypeStruct((T, T, NZ), F32)
    table = jax.ShapeDtypeStruct((GROUP, 8, NZ), F32)
    hbm = pl.BlockSpec(memory_space=pltpu.HBM)
    vmem = pl.BlockSpec(memory_space=pltpu.VMEM)
    field = pltpu.VMEM((ROWS, STRIDE, NZ), F32)
    dma = pltpu.SemaphoreType.DMA
    state = pl.pallas_call(
        kernel,
        out_shape=(tile, tile, tile, tile, jax.ShapeDtypeStruct((6, T, NZ), F32),
                   jax.ShapeDtypeStruct((2, 8, NZ), F32), table, table),
        in_specs=[pl.BlockSpec(memory_space=pltpu.SMEM)] + [hbm] * 5,
        out_specs=(vmem,) * 8,
        scratch_shapes=[
            pltpu.VMEM((3, ROWS, STRIDE, NZ), F32), pltpu.VMEM((T, T, NZ), jnp.int32),
        ] + [field] * 9 + [
            pltpu.VMEM((4, NODES), F32),
            pltpu.VMEM((4, 2, T, NZ), F32), pltpu.VMEM((4, 2, T, NZ), F32),
            pltpu.VMEM((4, 6 * T + 8, NZ), F32), pltpu.VMEM((4, 6 * T + 8, NZ), F32),
            pltpu.VMEM((4, 24, NZ), F32), pltpu.VMEM((4, 24, NZ), F32),
            pltpu.VMEM((4, T, NZ), F32), pltpu.VMEM((4, T, NZ), F32),
            pltpu.VMEM((4, 2, 8, NZ), F32), pltpu.VMEM((4, GROUP - 1, 2, 8, NZ), F32),
            dma((5,)),
        ] + [dma((4,))] * 10,
        compiler_params=pltpu.CompilerParams(
            collective_id=0, has_side_effects=True, vmem_limit_bytes=40 * 1024 * 1024),
    )(*(pltpu.with_memory_space_constraint(array, pltpu.HBM) for array in (
        coarse_map.transpose(0, 2, 1), coarse_inverse, right_side, guess, conductivity, wet_mask)))
    return pl.pallas_call(
        finish,
        out_shape=(tile, tile),
        in_specs=[vmem] * 8 + [hbm],
        out_specs=(hbm, hbm),
        scratch_shapes=[pltpu.VMEM((T, T, NZ), F32)] * 3 + [dma, dma((8,))],
        compiler_params=pltpu.CompilerParams(vmem_limit_bytes=16 * 1024 * 1024),
    )(*state, pltpu.with_memory_space_constraint(guess, pltpu.HBM))


def solution(mesh):
    grid = P("gx", "gy", None)
    in_specs = (grid, grid, grid, grid, grid, P(("gx", "gy"), None))
    return jax.shard_map(body, mesh=mesh, in_specs=in_specs, out_specs=(grid, grid), check_vma=False)
```

```python
import jax
import jax.numpy as jnp
from jax import lax
from jax.experimental import pallas as pl
from jax.experimental.pallas import tpu as pltpu
from jax.sharding import PartitionSpec as P

F32 = jnp.float32
MESH = pl.DeviceIdType.MESH
BLK = 16
T = 32
NZ = 128
STRIDE = 40
ROWS = 40
FLAT = ROWS * STRIDE
NODES = 1024
PLANE, DEPTH = 32, 8
screen = 0.02
relax = 0.8
LO, CHUNK, STEPS = 72, 112, 13


def flat_of(x, y):
    return (x + 4) * STRIDE + y


def view(ref):
    return ref.reshape(FLAT, NZ)


def up(v):
    return pltpu.roll(v, NZ - 1, 1)


def down(v):
    return pltpu.roll(v, 1, 1)


def kernel(
    cmap, cinv, right, guess, conductivity, wet,
    l_out, image_out, resid_out, q_out, faces_out, near_out, far_out,
    ext, mask, w_east, w_north, w_above, diag, dinv, first, e_a, e_b, e_c, inverse,
    a_send, a_recv, b_send, b_recv, k_send, k_recv, l_send, l_recv,
    p_send, p_recv, z_send, z_recv, t_send, t_recv,
    load_sem, a_ss, a_rs, b_ss, b_rs, k_ss, k_rs, l_ss, l_rs, p_ss, p_rs, z_ss, z_rs,
):
    gx, gy = lax.axis_index("gx"), lax.axis_index("gy")
    n_gx, n_gy = lax.axis_size("gx"), lax.axis_size("gy")
    west = (lax.rem(gx + n_gx - 1, n_gx), gy)
    east = (lax.rem(gx + 1, n_gx), gy)
    south = (gx, lax.rem(gy + n_gy - 1, n_gy))
    north = (gx, lax.rem(gy + 1, n_gy))
    corners = [(px[0], py[1]) for px in (west, east) for py in (south, north)]
    sides = (west, east, south, north)
    chip_z, chip_y = gy // 4, lax.rem(gy, 4)
    chip_x, core = gx // 2, lax.rem(gx, 2)

    offsets = sorted(
        ((dx, dc, dy) for dx in range(4) for dc in range(2) for dy in range(4) if dx + dc + dy > 0),
        key=lambda o: (-min(o[0], 4 - o[0]) - min(o[2], 4 - o[2]), -o[1]))
    planes = (4, 3, 5, 2, 6, 1, 7)

    def plane_peer(o):
        return (lax.rem(chip_x + o[0], 4) * 2 + lax.rem(core + o[1], 2), chip_z * 4 + lax.rem(chip_y + o[2], 4))

    def plane_slot(o):
        return offsets.index(((4 - o[0]) % 4, o[1], (4 - o[2]) % 4))

    def depth_peer(k):
        return (gx, lax.rem(chip_z + k, DEPTH) * 4 + chip_y)

    own = (pl.ds(4, T), pl.ds(0, T))
    loads = [
        pltpu.make_async_copy(conductivity, ext.at[(0,) + own], load_sem.at[0]),
        pltpu.make_async_copy(wet, mask, load_sem.at[1]),
        pltpu.make_async_copy(guess, ext.at[(1,) + own], load_sem.at[2]),
        pltpu.make_async_copy(right, ext.at[(2,) + own], load_sem.at[3]),
        pltpu.make_async_copy(cinv, inverse, load_sem.at[4]),
    ]
    for copy in loads:
        copy.start()

    barrier = pltpu.get_barrier_semaphore()
    for peer in [depth_peer(k) for k in planes] + [plane_peer(o) for o in offsets] + corners + list(sides):
        pl.semaphore_signal(barrier, inc=1, device_id=peer, device_id_type=MESH)

    pad = jnp.zeros((8, NZ), F32)
    wide = jnp.zeros((STRIDE, NZ), F32)
    for ref in [ext.at[a] for a in range(3)] + [w_east, w_north, w_above, dinv, first]:
        for r in (0, 1, 2, 3, 36, 37, 38, 39):
            ref[r] = wide
        for r in range(4, 36):
            ref[r, pl.ds(32, 8)] = pad
    for ref in (e_a, e_b):
        view(ref)[pl.ds(0, LO)] = jnp.zeros((LO, NZ), F32)
        view(ref)[pl.ds(LO + CHUNK * STEPS, FLAT - LO - CHUNK * STEPS)] = jnp.zeros(
            (FLAT - LO - CHUNK * STEPS, NZ), F32)
    for r in (3, 36):
        e_c[r] = wide
    for r in range(4, 36):
        e_c[r, pl.ds(32, 8)] = pad

    sub = lax.broadcasted_iota(jnp.int32, (8, NZ), 0)
    lane = lax.broadcasted_iota(jnp.int32, (8, NZ), 1)
    node_of = sub * NZ + lane
    nodes = [[cmap[bx, 0, by] for by in range(2)] for bx in range(2)]
    spot = [[16 * gx + 8 * bx + 2 * chip_y + by for by in range(2)] for bx in range(2)]
    packed = jnp.zeros((8, NZ), jnp.int32)
    for bx in range(2):
        for by in range(2):
            packed = jnp.where(sub == 2 * bx + by, nodes[bx][by], packed)
    packed = packed.astype(F32)
    started = []

    def remote(src, dst, ss, rs, peer):
        copy = pltpu.make_async_remote_copy(
            src_ref=src, dst_ref=dst, send_sem=ss, recv_sem=rs, device_id=peer, device_id_type=MESH)
        copy.start()
        started.append(copy)
        return copy

    loads[0].wait()
    loads[1].wait()

    def masked(r, carry):
        ext[0, r + 4, pl.ds(0, T)] = ext[0, r + 4, pl.ds(0, T)] * mask[r].astype(F32)
        return carry

    lax.fori_loop(0, T, masked, 0, unroll=16)
    loads[2].wait()
    cond_f, guess_f, right_f = (view(ext.at[a]) for a in range(3))
    fields = (cond_f, guess_f)

    def column(ref, y):
        return ref[pl.ds(flat_of(0, y), T, stride=STRIDE)]

    def row(ref, x):
        return ref[pl.ds(flat_of(x, 0), T)]

    def line(ref, s, n):
        at = n if s % 2 == 0 else T - 1 - n
        return row(ref, at) if s < 2 else column(ref, at)

    def put(ref, s, n, value):
        at = T + n if s % 2 == 0 else -1 - n
        if s < 2:
            ref[pl.ds(flat_of(at, 0), T)] = value
        else:
            ref[pl.ds(flat_of(0, at), T, stride=STRIDE)] = value

    for s in range(4):
        for a in range(2):
            a_send[s, a] = line(fields[a], s, 0)
    pl.semaphore_wait(barrier, 8 + len(planes) + len(offsets))
    ac = [remote(a_send.at[s], a_recv.at[s], a_ss.at[s], a_rs.at[s], sides[s]) for s in (2, 3, 0, 1)]
    ac = [ac[2], ac[3], ac[0], ac[1]]
    loads[3].wait()
    bc = [None] * 4
    for s in (2, 3, 0, 1):
        for i in range(2):
            for a in range(2):
                b_send[s, pl.ds(T * (2 * a + i), T)] = line(fields[a], s, 1 + i)
            b_send[s, pl.ds(T * (4 + i), T)] = line(right_f, s, i)
        b_send[s, pl.ds(T * 6, 8)] = packed
        bc[s] = remote(b_send.at[s], b_recv.at[s], b_ss.at[s], b_rs.at[s], sides[s])
    kc = []
    for q in range(4):
        sx, sy = q // 2, q % 2
        x3, y3 = (0, T - 3)[sx], (0, T - 3)[sy]
        x2, y2 = (0, T - 2)[sx], (0, T - 2)[sy]
        for a in range(2):
            for i in range(3):
                k_send[q, pl.ds(9 * a + 3 * i, 3)] = fields[a][pl.ds(flat_of(x3 + i, y3), 3)]
        k_send[q, pl.ds(22, 2)] = jnp.zeros((2, NZ), F32)
        for i in range(2):
            k_send[q, pl.ds(18 + 2 * i, 2)] = right_f[pl.ds(flat_of(x2 + i, y2), 2)]
        kc.append(remote(k_send.at[q], k_recv.at[q], k_ss.at[q], k_rs.at[q], corners[q]))

    w_east_f, w_north_f, w_above_f, diag_f, dinv_f, first_f, e_a_f, e_b_f, e_c_f = (
        view(ref) for ref in (w_east, w_north, w_above, diag, dinv, first, e_a, e_b, e_c))
    resid_f, image_f = (ref.reshape(T * T, NZ) for ref in (resid_out, image_out))

    def prepare(f, n, stride):
        def at(shift=0):
            return pl.ds(f + shift, n) if stride == 1 else pl.ds(f + shift, n, stride=stride)
        c = cond_f[at()]
        g = guess_f[at()]
        we = jnp.minimum(c, cond_f[at(STRIDE)])
        ww = jnp.minimum(c, cond_f[at(-STRIDE)])
        wn = jnp.minimum(c, cond_f[at(1)])
        ws = jnp.minimum(c, cond_f[at(-1)])
        top = lax.broadcasted_iota(jnp.int32, (n, NZ), 1) == NZ - 1
        wa = jnp.where(top, 0.0, jnp.minimum(c, up(c)))
        w_east_f[at()] = we
        w_north_f[at()] = wn
        w_above_f[at()] = wa
        dg = screen + jnp.maximum(0.0, 1.0 - 2.0 * c) + ww + we + ws + wn + down(wa) + wa
        diag_f[at()] = dg
        total = ww * guess_f[at(-STRIDE)] + we * guess_f[at(STRIDE)]
        total = total + ws * guess_f[at(-1)] + wn * guess_f[at(1)]
        total = total + down(wa * g) + wa * up(g)
        r = right_f[at()] - dg * g + total
        di = relax / dg
        dinv_f[at()] = di
        first_f[at()] = di * r
        return r

    def own_rows(x, carry):
        resid_out[x] = prepare(pl.multiple_of((x + 4) * STRIDE, 8), T, 1)
        return carry

    lax.fori_loop(0, T, own_rows, 0, unroll=16)

    def cells(bx):
        def add(r, carry):
            acc, kd = carry
            at = pl.ds(pl.multiple_of((4 + BLK * bx + r) * STRIDE, 8), T)
            q = screen + jnp.maximum(0.0, 1.0 - 2.0 * cond_f[at])
            q_out[BLK * bx + r] = q
            return acc + (right_f[at] - q * guess_f[at]), kd + q
        zero = jnp.zeros((T, NZ), F32)
        return lax.fori_loop(0, BLK, add, (zero, zero), unroll=16)

    def halves(v):
        return [v[:BLK], v[BLK:]]

    def face(c0, g0, c1, g1):
        w = jnp.minimum(c0, c1)
        return halves(w * (g0 - g1)), w

    sums, k_cell = [], []
    for bx in range(2):
        acc, kd = cells(bx)
        sums.append(halves(acc))
        k_cell.append(halves(kd))
    mid_x, mid_xw = face(row(cond_f, 15), row(guess_f, 15), row(cond_f, 16), row(guess_f, 16))
    mid_y, mid_yw = face(column(cond_f, 15), column(guess_f, 15), column(cond_f, 16), column(guess_f, 16))
    for i in range(2):
        sums[0][i] -= mid_x[i]
        sums[1][i] += mid_x[i]
        sums[i][0] -= mid_y[i]
        sums[i][1] += mid_y[i]

    def clear(ref, start, n):
        ref[pl.ds(start, n)] = jnp.zeros((n, NZ), F32)

    def clear_column(ref, x, y, n):
        ref[pl.ds(flat_of(x, y), n, stride=STRIDE)] = jnp.zeros((n, NZ), F32)

    for s in range(4):
        ac[s].wait_recv()
        for a in range(2):
            put(fields[a], s, 0, a_recv[s, a])

    @pl.when(gx == 0)
    def _():
        clear(cond_f, flat_of(-1, 0), T)

    @pl.when(gx == n_gx - 1)
    def _():
        clear(cond_f, flat_of(T, 0), T)

    @pl.when(gy == 0)
    def _():
        clear_column(cond_f, 0, -1, T)

    @pl.when(gy == n_gy - 1)
    def _():
        clear_column(cond_f, 0, T, T)

    edge_x = [face(row(cond_f, x), row(guess_f, x), row(cond_f, n), row(guess_f, n)) for x, n in ((0, -1), (T - 1, T))]
    edge_y = [face(column(cond_f, y), column(guess_f, y), column(cond_f, n), column(guess_f, n))
              for y, n in ((0, -1), (T - 1, T))]

    def totals(parts):
        found = []
        for base in range(0, len(parts), 8):
            group = parts[base:base + 8]
            stack = jnp.zeros((8, NZ), F32)
            for i, value in enumerate(group):
                stack = jnp.where(sub == i, jnp.sum(value, axis=0, keepdims=True), stack)
            stack = jnp.sum(stack, axis=1, keepdims=True)
            found += [stack[i:i + 1] for i in range(len(group))]
        return found

    blocks = [(bx, by) for bx in range(2) for by in range(2)]
    w_side = [edge_x[0][1], edge_x[1][1], edge_y[0][1], edge_y[1][1]]
    for i, w in enumerate((w_side[0], mid_xw, w_side[1], w_side[2], mid_yw, w_side[3])):
        faces_out[i] = w
    k_east = [halves(mid_xw), halves(w_side[1])]
    k_north = [[halves(mid_yw)[bx], halves(w_side[3])[bx]] for bx in range(2)]
    found = totals(
        [sums[bx][by] - edge_x[bx][0][by] - edge_y[by][0][bx] for bx, by in blocks]
        + [k_cell[bx][by] for bx, by in blocks]
        + [k_east[bx][by] for bx, by in blocks]
        + [k_north[bx][by] for bx, by in blocks])
    table = jnp.zeros((8, NZ), F32)
    for i, (bx, by) in enumerate(blocks):
        here = lane == spot[bx][by]
        table = jnp.where(here & (sub == 0), packed[i:i + 1], table)
        for q in range(4):
            table = jnp.where(here & (sub == (4, 1, 2, 3)[q]), found[4 * q + i], table)

    def send_plane(stage, value):
        p_send[stage] = value
        for o in offsets:
            pltpu.make_async_remote_copy(
                src_ref=p_send.at[stage], dst_ref=p_recv.at[stage, plane_slot(o)], send_sem=p_ss.at[stage],
                recv_sem=p_rs.at[stage], device_id=plane_peer(o), device_id_type=MESH).start()

    def settle(buffer, sem):
        pltpu.make_async_copy(buffer, buffer, sem).wait()

    def plane_sum(stage):
        settle(p_recv.at[stage], p_rs.at[stage])
        return p_send[stage] + jnp.sum(p_recv[stage], axis=0)

    def send_depth(src, dst, stage):
        for k in planes:
            pltpu.make_async_remote_copy(
                src_ref=src, dst_ref=dst.at[DEPTH - 1 - k], send_sem=z_ss.at[stage],
                recv_sem=z_rs.at[stage], device_id=depth_peer(k), device_id_type=MESH).start()

    send_plane(0, table)

    for x in (0, T - 1):
        resid_f[pl.ds(T * x, T)] = prepare(flat_of(x, 0), T, 1)
    for y in (0, T - 1):
        resid_f[pl.ds(y, T, stride=T)] = prepare(flat_of(0, y), T, STRIDE)

    for s in (2, 3, 0, 1):
        bc[s].wait_recv()
        for i in range(2):
            for a in range(2):
                put(fields[a], s, 1 + i, b_recv[s, pl.ds(T * (2 * a + i), T)])
            put(right_f, s, i, b_recv[s, pl.ds(T * (4 + i), T)])
    for q in range(4):
        kc[q].wait_recv()
        sx, sy = q // 2, q % 2
        x3, y3 = (T, -3)[sx], (T, -3)[sy]
        x2, y2 = (T, -2)[sx], (T, -2)[sy]
        for a in range(2):
            for i in range(3):
                fields[a][pl.ds(flat_of(x3 + i, y3), 3)] = k_recv[q, pl.ds(9 * a + 3 * i, 3)]
        for i in range(2):
            right_f[pl.ds(flat_of(x2 + i, y2), 2)] = k_recv[q, pl.ds(18 + 2 * i, 2)]

    @pl.when(gx == 0)
    def _():
        clear(cond_f, flat_of(-3, -4), 3 * STRIDE)

    @pl.when(gx == n_gx - 1)
    def _():
        clear(cond_f, flat_of(T, -4), 3 * STRIDE)

    @pl.when(gy == 0)
    def _():
        for y in (-3, -2, -1):
            clear_column(cond_f, -3, y, T + 6)

    @pl.when(gy == n_gy - 1)
    def _():
        for y in (T, T + 1, T + 2):
            clear_column(cond_f, -3, y, T + 6)

    for x in (-2, -1, T, T + 1):
        prepare(flat_of(x, 0), T, 1)
    for y in (-2, -1, T, T + 1):
        prepare(flat_of(-2, y), T + 4, STRIDE)

    @pl.when(gx == 0)
    def _():
        clear(first_f, flat_of(-2, -4), 2 * STRIDE)

    @pl.when(gx == n_gx - 1)
    def _():
        clear(first_f, flat_of(T, -4), 2 * STRIDE)

    @pl.when(gy == 0)
    def _():
        for y in (-2, -1):
            clear_column(first_f, -2, y, T + 4)

    @pl.when(gy == n_gy - 1)
    def _():
        for y in (T, T + 1):
            clear_column(first_f, -2, y, T + 4)

    def around(ref, f, n):
        at = pl.ds(f, n)
        v = ref[at]
        wa = w_above_f[at]
        total = w_east_f[at] * ref[pl.ds(f + STRIDE, n)]
        total = total + w_east_f[pl.ds(f - STRIDE, n)] * ref[pl.ds(f - STRIDE, n)]
        total = total + w_north_f[at] * ref[pl.ds(f + 1, n)]
        total = total + w_north_f[pl.ds(f - 1, n)] * ref[pl.ds(f - 1, n)]
        return total + wa * up(v) + down(wa * v), v

    def relaxed(src, dst, f, n):
        at = pl.ds(f, n)
        total, v = around(src, f, n)
        dst[at] = (1.0 - relax) * v + first_f[at] + dinv_f[at] * total

    def sweep(src, dst):
        def step(i, carry):
            relaxed(src, dst, pl.multiple_of(LO + i * CHUNK, 8), CHUNK)
            return carry
        lax.fori_loop(0, STEPS, step, 0, unroll=13)

    sweep(first_f, e_a_f)
    sweep(e_a_f, e_b_f)
    def last_sweep(x, carry):
        relaxed(e_b_f, e_c_f, pl.multiple_of((x + 4) * STRIDE, 8), T)
        return carry

    lax.fori_loop(0, T, last_sweep, 0, unroll=16)
    lc = []
    for s in range(4):
        l_send[s] = line(e_c_f, s, 0)
        lc.append(remote(l_send.at[s], l_recv.at[s], l_ss.at[s], l_rs.at[s], sides[s]))

    table = plane_sum(0)
    node = table[0:1].astype(jnp.int32)
    by_row = jnp.where(sub == node // NZ, table[4:5], 0.0)
    is_lane = (lax.broadcasted_iota(jnp.int32, (NZ, NZ), 0) == lax.rem(node, NZ)).astype(F32)
    z_send[0] = lax.dot_general(by_row, is_lane, (((1,), (1,)), ((), ())), precision=lax.Precision.HIGHEST,
                                preferred_element_type=F32)
    z_send[1] = table
    send_depth(z_send, z_recv, 0)

    def products(bx):
        def add(r, carry):
            al, lal, rl = carry
            x = BLK * bx + r
            f = pl.multiple_of((x + 4) * STRIDE, 8)
            total, v = around(e_c_f, f, T)
            im = diag_f[pl.ds(f, T)] * v - total
            image_out[x] = im
            l_out[x] = v
            return al + im, lal + v * im, rl + v * resid_out[x]
        zero = jnp.zeros((T, NZ), F32)
        return [halves(v) for v in lax.fori_loop(0, BLK, add, (zero, zero, zero), unroll=16)]

    sums = [products(0), products(1)]

    settle(z_recv, z_rs.at[0])
    near_out[pl.ds(0, DEPTH - 1)] = z_recv[:, 1]
    near_out[DEPTH - 1] = z_send[1]
    coarse_resid = z_send[0] + jnp.sum(z_recv[:, 0], axis=0)
    loads[4].wait()
    acc = jnp.zeros((4, NZ), F32)
    for k in range(8):
        acc = acc + inverse[:, pl.ds(NZ * k, NZ)] * coarse_resid[k:k + 1]
    acc = jnp.sum(acc, axis=1, keepdims=True)
    own_corr = [acc[i:i + 1] for i in range(4)]

    for copy in lc:
        copy.wait_recv()
    for s in range(4):
        out = w_side[s] * l_recv[s ^ 1]
        lost = halves(out), halves(out * l_send[s])
        for i in range(2):
            bx, by = (s % 2, i) if s < 2 else (i, s % 2)
            for q in range(2):
                sums[bx][q][by] -= lost[q][i]
        at = pl.ds((T - 1) * T * (s % 2), T) if s < 2 else pl.ds((T - 1) * (s % 2), T, stride=T)
        image_f[at] -= out

    found = totals([sums[bx][q][by] for q in range(3) for bx, by in blocks])
    table = jnp.zeros((8, NZ), F32)
    for i, (bx, by) in enumerate(blocks):
        for q in range(3):
            table = jnp.where((lane == spot[bx][by]) & (sub == q), found[4 * q + i], table)
    for i in range(4):
        table = jnp.where((lane == 16 * gx + 4 * chip_y + i) & (sub == 3), own_corr[i], table)
    send_plane(1, table)
    for copy in started:
        copy.wait_send()
    settle(p_recv.at[0], p_ss.at[0])
    settle(z_recv, z_ss.at[0])
    t_send[...] = plane_sum(1)
    send_depth(t_send, t_recv, 1)
    far_out[DEPTH - 1] = t_send[...]
    settle(p_recv.at[1], p_ss.at[1])
    settle(t_recv, z_rs.at[1])
    far_out[pl.ds(0, DEPTH - 1)] = t_recv[...]
    settle(t_recv, z_ss.at[1])


def finish(l, image, resid, q, faces, near, far, guess, pressure, residual, guess_v, press_v, resid_v, load_sem, out_sem):
    load = pltpu.make_async_copy(guess, guess_v, load_sem)
    load.start()
    gx, gy = lax.axis_index("gx"), lax.axis_index("gy")
    chip_z, chip_y = gy // 4, lax.rem(gy, 4)
    near_f, far_f = near.reshape(DEPTH * 8, NZ), far.reshape(DEPTH * 8, NZ)

    def pick(ref, i):
        return ref[pl.ds(i, DEPTH, stride=8)]

    c = pick(far_f, 3)
    node = pick(near_f, 0).astype(jnp.int32)
    at_slot = lax.rem(lax.rem(node, NZ) // 16 + 2 * DEPTH - 1 - chip_z, DEPTH)
    at_lane = node // NZ * 16 + lax.rem(node, 16)
    block = jnp.zeros((DEPTH, NZ), F32)
    for s in range(DEPTH):
        line = jnp.broadcast_to(c[s:s + 1], (DEPTH, NZ))
        hit = jnp.take_along_axis(line, at_lane, axis=1, mode="promise_in_bounds")
        block = jnp.where(at_slot == s, hit, block)
    east = pltpu.roll(block, NZ - 8, 1)
    lane = lax.broadcasted_iota(jnp.int32, (DEPTH, NZ), 1)
    north = jnp.where(lax.rem(lane, 8) == 7, pltpu.roll(pltpu.roll(block, 7, 1), DEPTH - 1, 0),
                      pltpu.roll(block, NZ - 1, 1))
    to_east, to_north = block - east, block - north
    numer = pick(far_f, 2) + block * pick(near_f, 4)
    denom = (pick(far_f, 1) + 2.0 * block * pick(far_f, 0) + pick(near_f, 1) * block * block
             + pick(near_f, 2) * to_east * to_east + pick(near_f, 3) * to_north * to_north)

    def total(v):
        return jnp.sum(jnp.sum(v, axis=0, keepdims=True), axis=1, keepdims=True)

    step = total(numer) / total(denom)
    turn = lax.rem(NZ - 16 * gx - 2 * chip_y, NZ)
    block, to_east, to_north = (pltpu.roll(v, turn, 1) for v in (block, to_east, to_north))

    def value(v, slot, at):
        return v[slot:slot + 1, at % NZ:at % NZ + 1]

    high = lax.broadcasted_iota(jnp.int32, (T, NZ), 0) >= BLK

    def spread(lower, upper):
        return step * jnp.where(high, upper, lower)

    last = DEPTH - 1
    mine = [spread(value(block, last, 8 * bx), value(block, last, 8 * bx + 1)) for bx in range(2)]
    flux_x = [faces[i] * spread(value(to_east, last, 8 * (i - 1)), value(to_east, last, 8 * (i - 1) + 1))
              for i in range(3)]
    below = [jnp.where(chip_y > 0, value(to_north, last, 8 * bx - 1), value(to_north, last - 1, 8 * bx + 7))
             for bx in range(2)]
    flux_y = [faces[3] * spread(*below)] + [
        faces[3 + i] * spread(value(to_north, last, i - 1), value(to_north, last, 8 + i - 1)) for i in (1, 2)]
    flat = resid_v.reshape(T * T, NZ)
    load.wait()
    copies = []
    for part in range(4):
        rows = pl.ds(8 * part, 8)
        add = mine[part // 2]
        press_v[rows] = guess_v[rows] + step * l[rows] + add
        copies.append(pltpu.make_async_copy(press_v.at[rows], pressure.at[rows], out_sem.at[2 * part]))
        copies[-1].start()
        resid_v[rows] = resid[rows] - step * image[rows] - q[rows] * add
        if part == 0:
            resid_v[0] += flux_x[0]
        elif part == 1:
            resid_v[15] -= flux_x[1]
        elif part == 2:
            resid_v[16] += flux_x[1]
        else:
            resid_v[31] -= flux_x[2]
        some = slice(8 * part, 8 * part + 8)
        for y, i, sign in ((0, 0, 1.0), (15, 1, -1.0), (16, 1, 1.0), (31, 2, -1.0)):
            flat[pl.ds(8 * part * T + y, 8, stride=T)] += sign * flux_y[i][some]
        copies.append(pltpu.make_async_copy(resid_v.at[rows], residual.at[rows], out_sem.at[2 * part + 1]))
        copies[-1].start()
    for copy in copies:
        copy.wait()


def body(right_side, guess, conductivity, wet_mask, coarse_map, coarse_inverse):
    tile = jax.ShapeDtypeStruct((T, T, NZ), F32)
    table = jax.ShapeDtypeStruct((DEPTH, 8, NZ), F32)
    hbm = pl.BlockSpec(memory_space=pltpu.HBM)
    vmem = pl.BlockSpec(memory_space=pltpu.VMEM)
    field = pltpu.VMEM((ROWS, STRIDE, NZ), F32)
    dma = pltpu.SemaphoreType.DMA
    state = pl.pallas_call(
        kernel,
        out_shape=(tile, tile, tile, tile, jax.ShapeDtypeStruct((6, T, NZ), F32),
                   table, table),
        in_specs=[pl.BlockSpec(memory_space=pltpu.SMEM)] + [hbm] * 5,
        out_specs=(vmem,) * 7,
        scratch_shapes=[
            pltpu.VMEM((3, ROWS, STRIDE, NZ), F32), pltpu.VMEM((T, T, NZ), jnp.int32),
        ] + [field] * 9 + [
            pltpu.VMEM((4, NODES), F32),
            pltpu.VMEM((4, 2, T, NZ), F32), pltpu.VMEM((4, 2, T, NZ), F32),
            pltpu.VMEM((4, 6 * T + 8, NZ), F32), pltpu.VMEM((4, 6 * T + 8, NZ), F32),
            pltpu.VMEM((4, 24, NZ), F32), pltpu.VMEM((4, 24, NZ), F32),
            pltpu.VMEM((4, T, NZ), F32), pltpu.VMEM((4, T, NZ), F32),
            pltpu.VMEM((2, 8, NZ), F32), pltpu.VMEM((2, PLANE - 1, 8, NZ), F32),
            pltpu.VMEM((2, 8, NZ), F32), pltpu.VMEM((DEPTH - 1, 2, 8, NZ), F32),
            pltpu.VMEM((8, NZ), F32), pltpu.VMEM((DEPTH - 1, 8, NZ), F32),
            dma((5,)),
        ] + [dma((4,))] * 8 + [dma((2,))] * 4,
        compiler_params=pltpu.CompilerParams(
            collective_id=0, has_side_effects=True, vmem_limit_bytes=40 * 1024 * 1024),
    )(*(pltpu.with_memory_space_constraint(array, pltpu.HBM) for array in (
        coarse_map.transpose(0, 2, 1), coarse_inverse, right_side, guess, conductivity, wet_mask)))
    return pl.pallas_call(
        finish,
        out_shape=(tile, tile),
        in_specs=[vmem] * 7 + [hbm],
        out_specs=(hbm, hbm),
        scratch_shapes=[pltpu.VMEM((T, T, NZ), F32)] * 3 + [dma, dma((8,))],
        compiler_params=pltpu.CompilerParams(vmem_limit_bytes=16 * 1024 * 1024),
    )(*state, pltpu.with_memory_space_constraint(guess, pltpu.HBM))


def solution(mesh):
    grid = P("gx", "gy", None)
    in_specs = (grid, grid, grid, grid, grid, P(("gx", "gy"), None))
    return jax.shard_map(body, mesh=mesh, in_specs=in_specs, out_specs=(grid, grid), check_vma=False)
```

```python
import jax
import jax.numpy as jnp
from jax import lax
from jax.experimental import pallas as pl
from jax.experimental.pallas import tpu as pltpu
from jax.sharding import PartitionSpec as P

F32 = jnp.float32
MESH = pl.DeviceIdType.MESH
BLK = 16
T = 32
NZ = 128
STRIDE = 40
ROWS = 40
FLAT = ROWS * STRIDE
NODES = 1024
PLANE, DEPTH = 32, 8
screen = 0.02
relax = 0.8
LO, CHUNK, STEPS = 72, 112, 13


def flat_of(x, y):
    return (x + 4) * STRIDE + y


def view(ref):
    return ref.reshape(FLAT, NZ)


def up(v):
    return pltpu.roll(v, NZ - 1, 1)


def down(v):
    return pltpu.roll(v, 1, 1)


def kernel(
    cmap, cinv, right, guess, conductivity, wet,
    guess_out, l_out, image_out, resid_out, q_out, faces_out, near_out, far_out,
    ext, mask, w_east, w_north, w_above, diag, dinv, first, e_a, e_b, e_c, inverse,
    a_send, a_recv, b_send, b_recv, k_send, k_recv, l_send, l_recv,
    p_send, p_recv, z_send, z_recv, t_send, t_recv,
    load_sem, a_ss, a_rs, b_ss, b_rs, k_ss, k_rs, l_ss, l_rs, p_ss, p_rs, z_ss, z_rs,
):
    gx, gy = lax.axis_index("gx"), lax.axis_index("gy")
    n_gx, n_gy = lax.axis_size("gx"), lax.axis_size("gy")
    west = (lax.rem(gx + n_gx - 1, n_gx), gy)
    east = (lax.rem(gx + 1, n_gx), gy)
    south = (gx, lax.rem(gy + n_gy - 1, n_gy))
    north = (gx, lax.rem(gy + 1, n_gy))
    corners = [(px[0], py[1]) for px in (west, east) for py in (south, north)]
    sides = (west, east, south, north)
    chip_z, chip_y = gy // 4, lax.rem(gy, 4)
    chip_x, core = gx // 2, lax.rem(gx, 2)

    offsets = sorted(
        ((dx, dc, dy) for dx in range(4) for dc in range(2) for dy in range(4) if dx + dc + dy > 0),
        key=lambda o: (-min(o[0], 4 - o[0]) - min(o[2], 4 - o[2]), -o[1]))
    planes = (4, 3, 5, 2, 6, 1, 7)

    def plane_peer(o):
        return (lax.rem(chip_x + o[0], 4) * 2 + lax.rem(core + o[1], 2), chip_z * 4 + lax.rem(chip_y + o[2], 4))

    def plane_slot(o):
        return offsets.index(((4 - o[0]) % 4, o[1], (4 - o[2]) % 4))

    def depth_peer(k):
        return (gx, lax.rem(chip_z + k, DEPTH) * 4 + chip_y)

    own = (pl.ds(4, T), pl.ds(0, T))
    loads = [
        pltpu.make_async_copy(conductivity, ext.at[(0,) + own], load_sem.at[0]),
        pltpu.make_async_copy(wet, mask, load_sem.at[1]),
        pltpu.make_async_copy(guess, ext.at[(1,) + own], load_sem.at[2]),
        pltpu.make_async_copy(right, ext.at[(2,) + own], load_sem.at[3]),
        pltpu.make_async_copy(cinv, inverse, load_sem.at[4]),
    ]
    for copy in loads[:4]:
        copy.start()

    barrier = pltpu.get_barrier_semaphore()
    for peer in [depth_peer(k) for k in planes] + [plane_peer(o) for o in offsets] + corners + list(sides):
        pl.semaphore_signal(barrier, inc=1, device_id=peer, device_id_type=MESH)

    sub = lax.broadcasted_iota(jnp.int32, (8, NZ), 0)
    lane = lax.broadcasted_iota(jnp.int32, (8, NZ), 1)
    node_of = sub * NZ + lane
    nodes = [[cmap[bx, 0, by] for by in range(2)] for bx in range(2)]
    spot = [[16 * gx + 8 * bx + 2 * chip_y + by for by in range(2)] for bx in range(2)]
    packed = jnp.zeros((8, NZ), jnp.int32)
    for bx in range(2):
        for by in range(2):
            packed = jnp.where(sub == 2 * bx + by, nodes[bx][by], packed)
    packed = packed.astype(F32)
    started = []

    def remote(src, dst, ss, rs, peer):
        copy = pltpu.make_async_remote_copy(
            src_ref=src, dst_ref=dst, send_sem=ss, recv_sem=rs, device_id=peer, device_id_type=MESH)
        copy.start()
        started.append(copy)
        return copy

    loads[0].wait()
    loads[1].wait()

    def masked(r, carry):
        ext[0, r + 4, pl.ds(0, T)] = ext[0, r + 4, pl.ds(0, T)] * mask[r].astype(F32)
        return carry

    lax.fori_loop(0, T, masked, 0, unroll=16)
    loads[2].wait()
    cond_f, guess_f, right_f = (view(ext.at[a]) for a in range(3))
    fields = (cond_f, guess_f)

    def column(ref, y):
        return ref[pl.ds(flat_of(0, y), T, stride=STRIDE)]

    def row(ref, x):
        return ref[pl.ds(flat_of(x, 0), T)]

    def line(ref, s, n):
        at = n if s % 2 == 0 else T - 1 - n
        return row(ref, at) if s < 2 else column(ref, at)

    def put(ref, s, n, value):
        at = T + n if s % 2 == 0 else -1 - n
        if s < 2:
            ref[pl.ds(flat_of(at, 0), T)] = value
        else:
            ref[pl.ds(flat_of(0, at), T, stride=STRIDE)] = value

    for s in range(4):
        for a in range(2):
            a_send[s, a] = line(fields[a], s, 0)
    pl.semaphore_wait(barrier, 8 + len(planes) + len(offsets))
    ac = [remote(a_send.at[s], a_recv.at[s], a_ss.at[s], a_rs.at[s], sides[s]) for s in (2, 3, 0, 1)]
    ac = [ac[2], ac[3], ac[0], ac[1]]
    loads[3].wait()
    bc = [None] * 4
    for s in (2, 3, 0, 1):
        for i in range(2):
            for a in range(2):
                b_send[s, pl.ds(T * (2 * a + i), T)] = line(fields[a], s, 1 + i)
            b_send[s, pl.ds(T * (4 + i), T)] = line(right_f, s, i)
        b_send[s, pl.ds(T * 6, 8)] = packed
        bc[s] = remote(b_send.at[s], b_recv.at[s], b_ss.at[s], b_rs.at[s], sides[s])
    kc = []
    for q in range(4):
        sx, sy = q // 2, q % 2
        x3, y3 = (0, T - 3)[sx], (0, T - 3)[sy]
        x2, y2 = (0, T - 2)[sx], (0, T - 2)[sy]
        for a in range(2):
            for i in range(3):
                k_send[q, pl.ds(9 * a + 3 * i, 3)] = fields[a][pl.ds(flat_of(x3 + i, y3), 3)]
        k_send[q, pl.ds(22, 2)] = jnp.zeros((2, NZ), F32)
        for i in range(2):
            k_send[q, pl.ds(18 + 2 * i, 2)] = right_f[pl.ds(flat_of(x2 + i, y2), 2)]
        kc.append(remote(k_send.at[q], k_recv.at[q], k_ss.at[q], k_rs.at[q], corners[q]))

    pad = jnp.zeros((8, NZ), F32)
    wide = jnp.zeros((STRIDE, NZ), F32)
    for ref in [ext.at[a] for a in range(3)] + [w_east, w_north, w_above, dinv, first]:
        for r in (0, 1, 2, 3, 36, 37, 38, 39):
            ref[r] = wide
        for r in range(4, 36):
            ref[r, pl.ds(32, 8)] = pad
    for ref in (e_a, e_b):
        view(ref)[pl.ds(0, LO)] = jnp.zeros((LO, NZ), F32)
        view(ref)[pl.ds(LO + CHUNK * STEPS, FLAT - LO - CHUNK * STEPS)] = jnp.zeros(
            (FLAT - LO - CHUNK * STEPS, NZ), F32)
    for r in (3, 36):
        e_c[r] = wide
    for r in range(4, 36):
        e_c[r, pl.ds(32, 8)] = pad

    loads[4].start()
    w_east_f, w_north_f, w_above_f, diag_f, dinv_f, first_f, e_a_f, e_b_f, e_c_f = (
        view(ref) for ref in (w_east, w_north, w_above, diag, dinv, first, e_a, e_b, e_c))
    resid_f, image_f = (ref.reshape(T * T, NZ) for ref in (resid_out, image_out))

    def prepare(f, n, stride):
        def at(shift=0):
            return pl.ds(f + shift, n) if stride == 1 else pl.ds(f + shift, n, stride=stride)
        c = cond_f[at()]
        g = guess_f[at()]
        we = jnp.minimum(c, cond_f[at(STRIDE)])
        ww = jnp.minimum(c, cond_f[at(-STRIDE)])
        wn = jnp.minimum(c, cond_f[at(1)])
        ws = jnp.minimum(c, cond_f[at(-1)])
        top = lax.broadcasted_iota(jnp.int32, (n, NZ), 1) == NZ - 1
        wa = jnp.where(top, 0.0, jnp.minimum(c, up(c)))
        w_east_f[at()] = we
        w_north_f[at()] = wn
        w_above_f[at()] = wa
        dg = screen + jnp.maximum(0.0, 1.0 - 2.0 * c) + ww + we + ws + wn + down(wa) + wa
        diag_f[at()] = dg
        total = ww * guess_f[at(-STRIDE)] + we * guess_f[at(STRIDE)]
        total = total + ws * guess_f[at(-1)] + wn * guess_f[at(1)]
        total = total + down(wa * g) + wa * up(g)
        r = right_f[at()] - dg * g + total
        di = relax / dg
        dinv_f[at()] = di
        first_f[at()] = di * r
        return r

    def own_rows(x, carry):
        resid_out[x] = prepare(pl.multiple_of((x + 4) * STRIDE, 8), T, 1)
        return carry

    lax.fori_loop(0, T, own_rows, 0, unroll=16)

    def cells(bx):
        def add(r, carry):
            acc, kd = carry
            at = pl.ds(pl.multiple_of((4 + BLK * bx + r) * STRIDE, 8), T)
            q = screen + jnp.maximum(0.0, 1.0 - 2.0 * cond_f[at])
            q_out[BLK * bx + r] = q
            return acc + (right_f[at] - q * guess_f[at]), kd + q
        zero = jnp.zeros((T, NZ), F32)
        return lax.fori_loop(0, BLK, add, (zero, zero), unroll=16)

    def halves(v):
        return [v[:BLK], v[BLK:]]

    def face(c0, g0, c1, g1):
        w = jnp.minimum(c0, c1)
        return halves(w * (g0 - g1)), w

    sums, k_cell = [], []
    for bx in range(2):
        acc, kd = cells(bx)
        sums.append(halves(acc))
        k_cell.append(halves(kd))
    mid_x, mid_xw = face(row(cond_f, 15), row(guess_f, 15), row(cond_f, 16), row(guess_f, 16))
    mid_y, mid_yw = face(column(cond_f, 15), column(guess_f, 15), column(cond_f, 16), column(guess_f, 16))
    for i in range(2):
        sums[0][i] -= mid_x[i]
        sums[1][i] += mid_x[i]
        sums[i][0] -= mid_y[i]
        sums[i][1] += mid_y[i]

    def totals(parts):
        found = []
        for base in range(0, len(parts), 8):
            group = parts[base:base + 8]
            stack = jnp.zeros((8, NZ), F32)
            for i, value in enumerate(group):
                stack = jnp.where(sub == i, jnp.sum(value, axis=0, keepdims=True), stack)
            stack = jnp.sum(stack, axis=1, keepdims=True)
            found += [stack[i:i + 1] for i in range(len(group))]
        return found

    blocks = [(bx, by) for bx in range(2) for by in range(2)]
    wx, wy = halves(mid_xw), halves(mid_yw)
    found = totals([sums[bx][by] for bx, by in blocks] + [k_cell[bx][by] for bx, by in blocks] + wx + wy)
    here = [lane == spot[bx][by] for bx, by in blocks]
    cell = [[here[i] & (sub == q) for i in range(4)] for q in range(5)]
    table = jnp.zeros((8, NZ), F32)
    for i in range(4):
        table = jnp.where(cell[0][i], packed[i:i + 1], table)
        table = jnp.where(cell[1][i], found[4 + i], table)
        table = jnp.where(cell[4][i], found[i], table)
    for i in range(2):
        table = jnp.where(cell[2][i], found[8 + i], table)
        table = jnp.where(cell[3][2 * i], found[10 + i], table)

    inside = [jnp.where(there, 1.0, 0.0) for there in (gx > 0, gx < n_gx - 1, gy > 0, gy < n_gy - 1)]
    for copy in ac:
        copy.wait_recv()
    beside, out, w_side = [], [], []
    for s in range(4):
        cond_line, guess_line = a_recv[s ^ 1, 0] * inside[s], a_recv[s ^ 1, 1]
        beside.append(cond_line)
        w_side.append(jnp.minimum(a_send[s, 0], cond_line))
        out.append(halves(w_side[s] * (a_send[s, 1] - guess_line)))
    found = totals([out[bx][by] + out[2 + by][bx] for bx, by in blocks] + halves(w_side[1]) + halves(w_side[3]))
    for i in range(4):
        table = jnp.where(cell[4][i], table - found[i], table)
    for i in range(2):
        table = jnp.where(cell[2][2 + i], found[4 + i], table)
        table = jnp.where(cell[3][2 * i + 1], found[6 + i], table)

    def send_plane(stage, value):
        p_send[stage] = value
        for o in offsets:
            pltpu.make_async_remote_copy(
                src_ref=p_send.at[stage], dst_ref=p_recv.at[stage, plane_slot(o)], send_sem=p_ss.at[stage],
                recv_sem=p_rs.at[stage], device_id=plane_peer(o), device_id_type=MESH).start()

    def settle(buffer, sem):
        pltpu.make_async_copy(buffer, buffer, sem).wait()

    def plane_sum(stage):
        settle(p_recv.at[stage], p_rs.at[stage])
        return p_send[stage] + jnp.sum(p_recv[stage], axis=0)

    def send_depth(src, dst, stage):
        for k in planes:
            pltpu.make_async_remote_copy(
                src_ref=src, dst_ref=dst.at[DEPTH - 1 - k], send_sem=z_ss.at[stage],
                recv_sem=z_rs.at[stage], device_id=depth_peer(k), device_id_type=MESH).start()

    send_plane(0, table)

    def clear(ref, start, n):
        ref[pl.ds(start, n)] = jnp.zeros((n, NZ), F32)

    def clear_column(ref, x, y, n):
        ref[pl.ds(flat_of(x, y), n, stride=STRIDE)] = jnp.zeros((n, NZ), F32)

    for s in range(4):
        put(cond_f, s, 0, beside[s ^ 1])
        put(guess_f, s, 0, a_recv[s, 1])
    for i, w in enumerate((w_side[0], mid_xw, w_side[1], w_side[2], mid_yw, w_side[3])):
        faces_out[i] = w

    for x in (0, T - 1):
        resid_f[pl.ds(T * x, T)] = prepare(flat_of(x, 0), T, 1)
    for y in (0, T - 1):
        resid_f[pl.ds(y, T, stride=T)] = prepare(flat_of(0, y), T, STRIDE)

    for s in (2, 3, 0, 1):
        bc[s].wait_recv()
        for i in range(2):
            for a in range(2):
                put(fields[a], s, 1 + i, b_recv[s, pl.ds(T * (2 * a + i), T)])
            put(right_f, s, i, b_recv[s, pl.ds(T * (4 + i), T)])
    for q in range(4):
        kc[q].wait_recv()
        sx, sy = q // 2, q % 2
        x3, y3 = (T, -3)[sx], (T, -3)[sy]
        x2, y2 = (T, -2)[sx], (T, -2)[sy]
        for a in range(2):
            for i in range(3):
                fields[a][pl.ds(flat_of(x3 + i, y3), 3)] = k_recv[q, pl.ds(9 * a + 3 * i, 3)]
        for i in range(2):
            right_f[pl.ds(flat_of(x2 + i, y2), 2)] = k_recv[q, pl.ds(18 + 2 * i, 2)]

    @pl.when(gx == 0)
    def _():
        clear(cond_f, flat_of(-3, -4), 3 * STRIDE)

    @pl.when(gx == n_gx - 1)
    def _():
        clear(cond_f, flat_of(T, -4), 3 * STRIDE)

    @pl.when(gy == 0)
    def _():
        for y in (-3, -2, -1):
            clear_column(cond_f, -3, y, T + 6)

    @pl.when(gy == n_gy - 1)
    def _():
        for y in (T, T + 1, T + 2):
            clear_column(cond_f, -3, y, T + 6)

    for x in (-2, -1, T, T + 1):
        prepare(flat_of(x, 0), T, 1)
    for y in (-2, -1, T, T + 1):
        prepare(flat_of(-2, y), T + 4, STRIDE)

    @pl.when(gx == 0)
    def _():
        clear(first_f, flat_of(-2, -4), 2 * STRIDE)

    @pl.when(gx == n_gx - 1)
    def _():
        clear(first_f, flat_of(T, -4), 2 * STRIDE)

    @pl.when(gy == 0)
    def _():
        for y in (-2, -1):
            clear_column(first_f, -2, y, T + 4)

    @pl.when(gy == n_gy - 1)
    def _():
        for y in (T, T + 1):
            clear_column(first_f, -2, y, T + 4)

    def around(ref, f, n):
        at = pl.ds(f, n)
        v = ref[at]
        wa = w_above_f[at]
        total = w_east_f[at] * ref[pl.ds(f + STRIDE, n)]
        total = total + w_east_f[pl.ds(f - STRIDE, n)] * ref[pl.ds(f - STRIDE, n)]
        total = total + w_north_f[at] * ref[pl.ds(f + 1, n)]
        total = total + w_north_f[pl.ds(f - 1, n)] * ref[pl.ds(f - 1, n)]
        return total + wa * up(v) + down(wa * v), v

    def relaxed(src, dst, f, n):
        at = pl.ds(f, n)
        total, v = around(src, f, n)
        dst[at] = (1.0 - relax) * v + first_f[at] + dinv_f[at] * total

    def sweep(src, dst):
        def step(i, carry):
            relaxed(src, dst, pl.multiple_of(LO + i * CHUNK, 8), CHUNK)
            return carry
        lax.fori_loop(0, STEPS, step, 0, unroll=13)

    sweep(first_f, e_a_f)
    sweep(e_a_f, e_b_f)
    def last_sweep(x, carry):
        relaxed(e_b_f, e_c_f, pl.multiple_of((x + 4) * STRIDE, 8), T)
        return carry

    lax.fori_loop(0, T, last_sweep, 0, unroll=16)
    lc = []
    for s in range(4):
        l_send[s] = line(e_c_f, s, 0)
        lc.append(remote(l_send.at[s], l_recv.at[s], l_ss.at[s], l_rs.at[s], sides[s]))

    table = plane_sum(0)
    node = table[0:1].astype(jnp.int32)
    by_row = jnp.where(sub == node // NZ, table[4:5], 0.0)
    is_lane = (lax.broadcasted_iota(jnp.int32, (NZ, NZ), 0) == lax.rem(node, NZ)).astype(F32).astype(jnp.bfloat16)
    pieces = []
    for _ in range(3):
        pieces.append(by_row.astype(jnp.bfloat16).astype(F32))
        by_row = by_row - pieces[-1]
    by_node = lax.dot_general(jnp.concatenate(pieces).astype(jnp.bfloat16), is_lane, (((1,), (1,)), ((), ())),
                              preferred_element_type=F32)
    z_send[0] = by_node[:8] + by_node[8:16] + by_node[16:]
    z_send[1] = table
    send_depth(z_send, z_recv, 0)

    def products(bx):
        def add(r, carry):
            al, lal, rl = carry
            x = BLK * bx + r
            f = pl.multiple_of((x + 4) * STRIDE, 8)
            total, v = around(e_c_f, f, T)
            im = diag_f[pl.ds(f, T)] * v - total
            image_out[x] = im
            l_out[x] = v
            guess_out[x] = guess_f[pl.ds(f, T)]
            return al + im, lal + v * im, rl + v * resid_out[x]
        zero = jnp.zeros((T, NZ), F32)
        return [halves(v) for v in lax.fori_loop(0, BLK, add, (zero, zero, zero), unroll=16)]

    sums = [products(0), products(1)]

    settle(z_recv, z_rs.at[0])
    near_out[pl.ds(0, DEPTH - 1)] = z_recv[:, 1]
    near_out[DEPTH - 1] = z_send[1]
    coarse_resid = z_send[0] + jnp.sum(z_recv[:, 0], axis=0)
    loads[4].wait()
    acc = jnp.zeros((4, NZ), F32)
    for k in range(8):
        acc = acc + inverse[:, pl.ds(NZ * k, NZ)] * coarse_resid[k:k + 1]
    acc = jnp.sum(acc, axis=1, keepdims=True)
    own_corr = [acc[i:i + 1] for i in range(4)]

    for copy in lc:
        copy.wait_recv()
    for s in range(4):
        out = w_side[s] * l_recv[s ^ 1]
        lost = halves(out), halves(out * l_send[s])
        for i in range(2):
            bx, by = (s % 2, i) if s < 2 else (i, s % 2)
            for q in range(2):
                sums[bx][q][by] -= lost[q][i]
        at = pl.ds((T - 1) * T * (s % 2), T) if s < 2 else pl.ds((T - 1) * (s % 2), T, stride=T)
        image_f[at] -= out

    found = totals([sums[bx][q][by] for q in range(3) for bx, by in blocks])
    table = jnp.zeros((8, NZ), F32)
    for i, (bx, by) in enumerate(blocks):
        for q in range(3):
            table = jnp.where((lane == spot[bx][by]) & (sub == q), found[4 * q + i], table)
    for i in range(4):
        table = jnp.where((lane == 16 * gx + 4 * chip_y + i) & (sub == 3), own_corr[i], table)
    send_plane(1, table)
    for copy in started:
        copy.wait_send()
    settle(p_recv.at[0], p_ss.at[0])
    settle(z_recv, z_ss.at[0])
    t_send[...] = plane_sum(1)
    send_depth(t_send, t_recv, 1)
    far_out[DEPTH - 1] = t_send[...]
    settle(p_recv.at[1], p_ss.at[1])
    settle(t_recv, z_rs.at[1])
    far_out[pl.ds(0, DEPTH - 1)] = t_recv[...]
    settle(t_recv, z_ss.at[1])


def finish(guess, l, image, resid, q, faces, near, far, pressure, residual, press_v, resid_v, out_sem):
    gx, gy = lax.axis_index("gx"), lax.axis_index("gy")
    chip_z, chip_y = gy // 4, lax.rem(gy, 4)
    near_f, far_f = near.reshape(DEPTH * 8, NZ), far.reshape(DEPTH * 8, NZ)

    def pick(ref, i):
        return ref[pl.ds(i, DEPTH, stride=8)]

    c = pick(far_f, 3)
    node = pick(near_f, 0).astype(jnp.int32)
    at_slot = lax.rem(lax.rem(node, NZ) // 16 + 2 * DEPTH - 1 - chip_z, DEPTH)
    at_lane = node // NZ * 16 + lax.rem(node, 16)
    block = jnp.zeros((DEPTH, NZ), F32)
    for s in range(DEPTH):
        line = jnp.broadcast_to(c[s:s + 1], (DEPTH, NZ))
        hit = jnp.take_along_axis(line, at_lane, axis=1, mode="promise_in_bounds")
        block = jnp.where(at_slot == s, hit, block)
    east = pltpu.roll(block, NZ - 8, 1)
    lane = lax.broadcasted_iota(jnp.int32, (DEPTH, NZ), 1)
    north = jnp.where(lax.rem(lane, 8) == 7, pltpu.roll(pltpu.roll(block, 7, 1), DEPTH - 1, 0),
                      pltpu.roll(block, NZ - 1, 1))
    to_east, to_north = block - east, block - north
    numer = pick(far_f, 2) + block * pick(near_f, 4)
    denom = (pick(far_f, 1) + 2.0 * block * pick(far_f, 0) + pick(near_f, 1) * block * block
             + pick(near_f, 2) * to_east * to_east + pick(near_f, 3) * to_north * to_north)

    def total(v):
        return jnp.sum(jnp.sum(v, axis=0, keepdims=True), axis=1, keepdims=True)

    step = total(numer) / total(denom)
    turn = lax.rem(NZ - 16 * gx - 2 * chip_y, NZ)
    block, to_east, to_north = (pltpu.roll(v, turn, 1) for v in (block, to_east, to_north))

    def value(v, slot, at):
        return v[slot:slot + 1, at % NZ:at % NZ + 1]

    high = lax.broadcasted_iota(jnp.int32, (T, NZ), 0) >= BLK

    def spread(lower, upper):
        return step * jnp.where(high, upper, lower)

    last = DEPTH - 1
    mine = [spread(value(block, last, 8 * bx), value(block, last, 8 * bx + 1)) for bx in range(2)]
    flux_x = [faces[i] * spread(value(to_east, last, 8 * (i - 1)), value(to_east, last, 8 * (i - 1) + 1))
              for i in range(3)]
    below = [jnp.where(chip_y > 0, value(to_north, last, 8 * bx - 1), value(to_north, last - 1, 8 * bx + 7))
             for bx in range(2)]
    flux_y = [faces[3] * spread(*below)] + [
        faces[3 + i] * spread(value(to_north, last, i - 1), value(to_north, last, 8 + i - 1)) for i in (1, 2)]
    flat = resid_v.reshape(T * T, NZ)
    copies = []
    for part in range(4):
        rows = pl.ds(8 * part, 8)
        add = mine[part // 2]
        press_v[rows] = guess[rows] + step * l[rows] + add
        copies.append(pltpu.make_async_copy(press_v.at[rows], pressure.at[rows], out_sem.at[2 * part]))
        copies[-1].start()
        resid_v[rows] = resid[rows] - step * image[rows] - q[rows] * add
        if part == 0:
            resid_v[0] += flux_x[0]
        elif part == 1:
            resid_v[15] -= flux_x[1]
        elif part == 2:
            resid_v[16] += flux_x[1]
        else:
            resid_v[31] -= flux_x[2]
        some = slice(8 * part, 8 * part + 8)
        for y, i, sign in ((0, 0, 1.0), (15, 1, -1.0), (16, 1, 1.0), (31, 2, -1.0)):
            flat[pl.ds(8 * part * T + y, 8, stride=T)] += sign * flux_y[i][some]
        copies.append(pltpu.make_async_copy(resid_v.at[rows], residual.at[rows], out_sem.at[2 * part + 1]))
        copies[-1].start()
    for copy in copies:
        copy.wait()


def body(right_side, guess, conductivity, wet_mask, coarse_map, coarse_inverse):
    tile = jax.ShapeDtypeStruct((T, T, NZ), F32)
    table = jax.ShapeDtypeStruct((DEPTH, 8, NZ), F32)
    hbm = pl.BlockSpec(memory_space=pltpu.HBM)
    vmem = pl.BlockSpec(memory_space=pltpu.VMEM)
    field = pltpu.VMEM((ROWS, STRIDE, NZ), F32)
    dma = pltpu.SemaphoreType.DMA
    state = pl.pallas_call(
        kernel,
        out_shape=(tile, tile, tile, tile, tile, jax.ShapeDtypeStruct((6, T, NZ), F32),
                   table, table),
        in_specs=[pl.BlockSpec(memory_space=pltpu.SMEM)] + [hbm] * 5,
        out_specs=(vmem,) * 8,
        scratch_shapes=[
            pltpu.VMEM((3, ROWS, STRIDE, NZ), F32), pltpu.VMEM((T, T, NZ), jnp.int32),
        ] + [field] * 9 + [
            pltpu.VMEM((4, NODES), F32),
            pltpu.VMEM((4, 2, T, NZ), F32), pltpu.VMEM((4, 2, T, NZ), F32),
            pltpu.VMEM((4, 6 * T + 8, NZ), F32), pltpu.VMEM((4, 6 * T + 8, NZ), F32),
            pltpu.VMEM((4, 24, NZ), F32), pltpu.VMEM((4, 24, NZ), F32),
            pltpu.VMEM((4, T, NZ), F32), pltpu.VMEM((4, T, NZ), F32),
            pltpu.VMEM((2, 8, NZ), F32), pltpu.VMEM((2, PLANE - 1, 8, NZ), F32),
            pltpu.VMEM((2, 8, NZ), F32), pltpu.VMEM((DEPTH - 1, 2, 8, NZ), F32),
            pltpu.VMEM((8, NZ), F32), pltpu.VMEM((DEPTH - 1, 8, NZ), F32),
            dma((5,)),
        ] + [dma((4,))] * 8 + [dma((2,))] * 4,
        compiler_params=pltpu.CompilerParams(
            collective_id=0, has_side_effects=True, vmem_limit_bytes=40 * 1024 * 1024),
    )(*(pltpu.with_memory_space_constraint(array, pltpu.HBM) for array in (
        coarse_map.transpose(0, 2, 1), coarse_inverse, right_side, guess, conductivity, wet_mask)))
    return pl.pallas_call(
        finish,
        out_shape=(tile, tile),
        in_specs=[vmem] * 8,
        out_specs=(hbm, hbm),
        scratch_shapes=[pltpu.VMEM((T, T, NZ), F32)] * 2 + [dma((8,))],
        compiler_params=pltpu.CompilerParams(vmem_limit_bytes=16 * 1024 * 1024),
    )(*state)


def solution(mesh):
    grid = P("gx", "gy", None)
    in_specs = (grid, grid, grid, grid, grid, P(("gx", "gy"), None))
    return jax.shard_map(body, mesh=mesh, in_specs=in_specs, out_specs=(grid, grid), check_vma=False)
```

```python
import jax
import jax.numpy as jnp
from jax import lax
from jax.experimental import pallas as pl
from jax.experimental.pallas import tpu as pltpu
from jax.sharding import PartitionSpec as P

F32 = jnp.float32
MESH = pl.DeviceIdType.MESH
BLK = 16
T = 32
NZ = 128
STRIDE = 40
ROWS = 40
FLAT = ROWS * STRIDE
NODES = 1024
PLANE, DEPTH = 32, 8
screen = 0.02
relax = 0.8
LO, CHUNK, STEPS = 72, 112, 13


def flat_of(x, y):
    return (x + 4) * STRIDE + y


def view(ref):
    return ref.reshape(FLAT, NZ)


def up(v):
    return pltpu.roll(v, NZ - 1, 1)


def down(v):
    return pltpu.roll(v, 1, 1)


def kernel(
    cmap, cinv, right, guess, conductivity, wet,
    guess_out, l_out, image_out, resid_out, q_out, faces_out, coarse_out, near_out, far_out,
    ext, mask, w_east, w_north, w_above, diag, dinv, first, e_a, e_b, e_c, inverse, inverse_recv,
    a_send, a_recv, b_send, b_recv, k_send, k_recv, l_send, l_recv,
    p_send, p_recv, z_send, z_recv, t_send, t_recv,
    load_sem, a_ss, a_rs, b_ss, b_rs, k_ss, k_rs, l_ss, l_rs, p_ss, p_rs, z_ss, z_rs, i_ss, i_rs,
):
    gx, gy = lax.axis_index("gx"), lax.axis_index("gy")
    n_gx, n_gy = lax.axis_size("gx"), lax.axis_size("gy")
    west = (lax.rem(gx + n_gx - 1, n_gx), gy)
    east = (lax.rem(gx + 1, n_gx), gy)
    south = (gx, lax.rem(gy + n_gy - 1, n_gy))
    north = (gx, lax.rem(gy + 1, n_gy))
    corners = [(px[0], py[1]) for px in (west, east) for py in (south, north)]
    sides = (west, east, south, north)
    chip_z, chip_y = gy // 4, lax.rem(gy, 4)
    chip_x, core = gx // 2, lax.rem(gx, 2)

    offsets = sorted(
        ((dx, dc, dy) for dx in range(4) for dc in range(2) for dy in range(4) if dx + dc + dy > 0),
        key=lambda o: (-min(o[0], 4 - o[0]) - min(o[2], 4 - o[2]), -o[1]))
    planes = (4, 3, 5, 2, 6, 1, 7)

    def plane_peer(o):
        return (lax.rem(chip_x + o[0], 4) * 2 + lax.rem(core + o[1], 2), chip_z * 4 + lax.rem(chip_y + o[2], 4))

    def plane_slot(o):
        return offsets.index(((4 - o[0]) % 4, o[1], (4 - o[2]) % 4))

    def depth_peer(k):
        return (gx, lax.rem(chip_z + k, DEPTH) * 4 + chip_y)

    own = (pl.ds(4, T), pl.ds(0, T))
    loads = [
        pltpu.make_async_copy(conductivity, ext.at[(0,) + own], load_sem.at[0]),
        pltpu.make_async_copy(wet, mask, load_sem.at[1]),
        pltpu.make_async_copy(guess, ext.at[(1,) + own], load_sem.at[2]),
        pltpu.make_async_copy(right, ext.at[(2,) + own], load_sem.at[3]),
        pltpu.make_async_copy(cinv, inverse, load_sem.at[4]),
    ]
    for copy in loads:
        copy.start()

    barrier = pltpu.get_barrier_semaphore()
    for peer in [depth_peer(k) for k in planes] + [plane_peer(o) for o in offsets] + corners + list(sides):
        pl.semaphore_signal(barrier, inc=1, device_id=peer, device_id_type=MESH)

    sub = lax.broadcasted_iota(jnp.int32, (8, NZ), 0)
    lane = lax.broadcasted_iota(jnp.int32, (8, NZ), 1)
    node_of = sub * NZ + lane
    nodes = [[cmap[bx, 0, by] for by in range(2)] for bx in range(2)]
    spot = [[16 * gx + 8 * bx + 2 * chip_y + by for by in range(2)] for bx in range(2)]
    packed = jnp.zeros((8, NZ), jnp.int32)
    for bx in range(2):
        for by in range(2):
            packed = jnp.where(sub == 2 * bx + by, nodes[bx][by], packed)
    packed = packed.astype(F32)
    started = []

    def remote(src, dst, ss, rs, peer):
        copy = pltpu.make_async_remote_copy(
            src_ref=src, dst_ref=dst, send_sem=ss, recv_sem=rs, device_id=peer, device_id_type=MESH)
        copy.start()
        started.append(copy)
        return copy

    loads[0].wait()
    loads[1].wait()

    def masked(r, carry):
        ext[0, r + 4, pl.ds(0, T)] = ext[0, r + 4, pl.ds(0, T)] * mask[r].astype(F32)
        return carry

    lax.fori_loop(0, T, masked, 0, unroll=16)
    loads[2].wait()
    cond_f, guess_f, right_f = (view(ext.at[a]) for a in range(3))
    fields = (cond_f, guess_f)

    def column(ref, y):
        return ref[pl.ds(flat_of(0, y), T, stride=STRIDE)]

    def row(ref, x):
        return ref[pl.ds(flat_of(x, 0), T)]

    def line(ref, s, n):
        at = n if s % 2 == 0 else T - 1 - n
        return row(ref, at) if s < 2 else column(ref, at)

    def put(ref, s, n, value):
        at = T + n if s % 2 == 0 else -1 - n
        if s < 2:
            ref[pl.ds(flat_of(at, 0), T)] = value
        else:
            ref[pl.ds(flat_of(0, at), T, stride=STRIDE)] = value

    for s in range(4):
        for a in range(2):
            a_send[s, a] = line(fields[a], s, 0)
    pl.semaphore_wait(barrier, 8 + len(planes) + len(offsets))
    ac = [remote(a_send.at[s], a_recv.at[s], a_ss.at[s], a_rs.at[s], sides[s]) for s in (2, 3, 0, 1)]
    ac = [ac[2], ac[3], ac[0], ac[1]]
    loads[3].wait()
    bc = [None] * 4
    for s in (2, 3, 0, 1):
        for i in range(2):
            for a in range(2):
                b_send[s, pl.ds(T * (2 * a + i), T)] = line(fields[a], s, 1 + i)
            b_send[s, pl.ds(T * (4 + i), T)] = line(right_f, s, i)
        b_send[s, pl.ds(T * 6, 8)] = packed
        bc[s] = remote(b_send.at[s], b_recv.at[s], b_ss.at[s], b_rs.at[s], sides[s])
    kc = []
    for q in range(4):
        sx, sy = q // 2, q % 2
        x3, y3 = (0, T - 3)[sx], (0, T - 3)[sy]
        x2, y2 = (0, T - 2)[sx], (0, T - 2)[sy]
        for a in range(2):
            for i in range(3):
                k_send[q, pl.ds(9 * a + 3 * i, 3)] = fields[a][pl.ds(flat_of(x3 + i, y3), 3)]
        k_send[q, pl.ds(22, 2)] = jnp.zeros((2, NZ), F32)
        for i in range(2):
            k_send[q, pl.ds(18 + 2 * i, 2)] = right_f[pl.ds(flat_of(x2 + i, y2), 2)]
        kc.append(remote(k_send.at[q], k_recv.at[q], k_ss.at[q], k_rs.at[q], corners[q]))

    pad = jnp.zeros((8, NZ), F32)
    wide = jnp.zeros((STRIDE, NZ), F32)
    for ref in [ext.at[a] for a in range(3)] + [w_east, w_north, w_above, dinv, first]:
        for r in (0, 1, 2, 3, 36, 37, 38, 39):
            ref[r] = wide
        for r in range(4, 36):
            ref[r, pl.ds(32, 8)] = pad
    for ref in (e_a, e_b):
        view(ref)[pl.ds(0, LO)] = jnp.zeros((LO, NZ), F32)
        view(ref)[pl.ds(LO + CHUNK * STEPS, FLAT - LO - CHUNK * STEPS)] = jnp.zeros(
            (FLAT - LO - CHUNK * STEPS, NZ), F32)
    for r in (3, 36):
        e_c[r] = wide
    for r in range(4, 36):
        e_c[r, pl.ds(32, 8)] = pad

    loads[4].wait()
    for k in planes:
        pltpu.make_async_remote_copy(
            src_ref=inverse, dst_ref=inverse_recv.at[DEPTH - 1 - k], send_sem=i_ss.at[0], recv_sem=i_rs.at[0],
            device_id=depth_peer(k), device_id_type=MESH).start()
    w_east_f, w_north_f, w_above_f, diag_f, dinv_f, first_f, e_a_f, e_b_f, e_c_f = (
        view(ref) for ref in (w_east, w_north, w_above, diag, dinv, first, e_a, e_b, e_c))
    resid_f, image_f = (ref.reshape(T * T, NZ) for ref in (resid_out, image_out))

    def prepare(f, n, stride):
        def at(shift=0):
            return pl.ds(f + shift, n) if stride == 1 else pl.ds(f + shift, n, stride=stride)
        c = cond_f[at()]
        g = guess_f[at()]
        we = jnp.minimum(c, cond_f[at(STRIDE)])
        ww = jnp.minimum(c, cond_f[at(-STRIDE)])
        wn = jnp.minimum(c, cond_f[at(1)])
        ws = jnp.minimum(c, cond_f[at(-1)])
        top = lax.broadcasted_iota(jnp.int32, (n, NZ), 1) == NZ - 1
        wa = jnp.where(top, 0.0, jnp.minimum(c, up(c)))
        w_east_f[at()] = we
        w_north_f[at()] = wn
        w_above_f[at()] = wa
        dg = screen + jnp.maximum(0.0, 1.0 - 2.0 * c) + ww + we + ws + wn + down(wa) + wa
        diag_f[at()] = dg
        total = ww * guess_f[at(-STRIDE)] + we * guess_f[at(STRIDE)]
        total = total + ws * guess_f[at(-1)] + wn * guess_f[at(1)]
        total = total + down(wa * g) + wa * up(g)
        r = right_f[at()] - dg * g + total
        di = relax / dg
        dinv_f[at()] = di
        first_f[at()] = di * r
        return r

    def own_rows(x, carry):
        resid_out[x] = prepare(pl.multiple_of((x + 4) * STRIDE, 8), T, 1)
        return carry

    lax.fori_loop(0, T, own_rows, 0, unroll=16)

    def cells(bx):
        def add(r, carry):
            acc, kd = carry
            at = pl.ds(pl.multiple_of((4 + BLK * bx + r) * STRIDE, 8), T)
            q = screen + jnp.maximum(0.0, 1.0 - 2.0 * cond_f[at])
            q_out[BLK * bx + r] = q
            return acc + (right_f[at] - q * guess_f[at]), kd + q
        zero = jnp.zeros((T, NZ), F32)
        return lax.fori_loop(0, BLK, add, (zero, zero), unroll=16)

    def halves(v):
        return [v[:BLK], v[BLK:]]

    def face(c0, g0, c1, g1):
        w = jnp.minimum(c0, c1)
        return halves(w * (g0 - g1)), w

    sums, k_cell = [], []
    for bx in range(2):
        acc, kd = cells(bx)
        sums.append(halves(acc))
        k_cell.append(halves(kd))
    mid_x, mid_xw = face(row(cond_f, 15), row(guess_f, 15), row(cond_f, 16), row(guess_f, 16))
    mid_y, mid_yw = face(column(cond_f, 15), column(guess_f, 15), column(cond_f, 16), column(guess_f, 16))
    for i in range(2):
        sums[0][i] -= mid_x[i]
        sums[1][i] += mid_x[i]
        sums[i][0] -= mid_y[i]
        sums[i][1] += mid_y[i]

    def totals(parts):
        found = []
        for base in range(0, len(parts), 8):
            group = parts[base:base + 8]
            stack = jnp.zeros((8, NZ), F32)
            for i, value in enumerate(group):
                stack = jnp.where(sub == i, jnp.sum(value, axis=0, keepdims=True), stack)
            stack = jnp.sum(stack, axis=1, keepdims=True)
            found += [stack[i:i + 1] for i in range(len(group))]
        return found

    blocks = [(bx, by) for bx in range(2) for by in range(2)]
    wx, wy = halves(mid_xw), halves(mid_yw)
    found = totals([sums[bx][by] for bx, by in blocks] + [k_cell[bx][by] for bx, by in blocks] + wx + wy)
    here = [lane == spot[bx][by] for bx, by in blocks]
    cell = [[here[i] & (sub == q) for i in range(4)] for q in range(5)]
    table = jnp.zeros((8, NZ), F32)
    for i in range(4):
        table = jnp.where(cell[0][i], packed[i:i + 1], table)
        table = jnp.where(cell[1][i], found[4 + i], table)
        table = jnp.where(cell[4][i], found[i], table)
    for i in range(2):
        table = jnp.where(cell[2][i], found[8 + i], table)
        table = jnp.where(cell[3][2 * i], found[10 + i], table)

    inside = [jnp.where(there, 1.0, 0.0) for there in (gx > 0, gx < n_gx - 1, gy > 0, gy < n_gy - 1)]
    for copy in ac:
        copy.wait_recv()
    beside, out, w_side = [], [], []
    for s in range(4):
        cond_line, guess_line = a_recv[s ^ 1, 0] * inside[s], a_recv[s ^ 1, 1]
        beside.append(cond_line)
        w_side.append(jnp.minimum(a_send[s, 0], cond_line))
        out.append(halves(w_side[s] * (a_send[s, 1] - guess_line)))
    found = totals([out[bx][by] + out[2 + by][bx] for bx, by in blocks] + halves(w_side[1]) + halves(w_side[3]))
    for i in range(4):
        table = jnp.where(cell[4][i], table - found[i], table)
    for i in range(2):
        table = jnp.where(cell[2][2 + i], found[4 + i], table)
        table = jnp.where(cell[3][2 * i + 1], found[6 + i], table)

    def send_plane(stage, value):
        p_send[stage] = value
        for o in offsets:
            pltpu.make_async_remote_copy(
                src_ref=p_send.at[stage], dst_ref=p_recv.at[stage, plane_slot(o)], send_sem=p_ss.at[stage],
                recv_sem=p_rs.at[stage], device_id=plane_peer(o), device_id_type=MESH).start()

    def settle(buffer, sem):
        pltpu.make_async_copy(buffer, buffer, sem).wait()

    def plane_sum(stage):
        settle(p_recv.at[stage], p_rs.at[stage])
        return p_send[stage] + jnp.sum(p_recv[stage], axis=0)

    def send_depth(src, dst, stage):
        for k in planes:
            pltpu.make_async_remote_copy(
                src_ref=src, dst_ref=dst.at[DEPTH - 1 - k], send_sem=z_ss.at[stage],
                recv_sem=z_rs.at[stage], device_id=depth_peer(k), device_id_type=MESH).start()

    send_plane(0, table)

    def clear(ref, start, n):
        ref[pl.ds(start, n)] = jnp.zeros((n, NZ), F32)

    def clear_column(ref, x, y, n):
        ref[pl.ds(flat_of(x, y), n, stride=STRIDE)] = jnp.zeros((n, NZ), F32)

    for s in range(4):
        put(cond_f, s, 0, beside[s ^ 1])
        put(guess_f, s, 0, a_recv[s, 1])
    for i, w in enumerate((w_side[0], mid_xw, w_side[1], w_side[2], mid_yw, w_side[3])):
        faces_out[i] = w

    for x in (0, T - 1):
        resid_f[pl.ds(T * x, T)] = prepare(flat_of(x, 0), T, 1)
    for y in (0, T - 1):
        resid_f[pl.ds(y, T, stride=T)] = prepare(flat_of(0, y), T, STRIDE)

    for s in (2, 3, 0, 1):
        bc[s].wait_recv()
        for i in range(2):
            for a in range(2):
                put(fields[a], s, 1 + i, b_recv[s, pl.ds(T * (2 * a + i), T)])
            put(right_f, s, i, b_recv[s, pl.ds(T * (4 + i), T)])
    for q in range(4):
        kc[q].wait_recv()
        sx, sy = q // 2, q % 2
        x3, y3 = (T, -3)[sx], (T, -3)[sy]
        x2, y2 = (T, -2)[sx], (T, -2)[sy]
        for a in range(2):
            for i in range(3):
                fields[a][pl.ds(flat_of(x3 + i, y3), 3)] = k_recv[q, pl.ds(9 * a + 3 * i, 3)]
        for i in range(2):
            right_f[pl.ds(flat_of(x2 + i, y2), 2)] = k_recv[q, pl.ds(18 + 2 * i, 2)]

    @pl.when(gx == 0)
    def _():
        clear(cond_f, flat_of(-3, -4), 3 * STRIDE)

    @pl.when(gx == n_gx - 1)
    def _():
        clear(cond_f, flat_of(T, -4), 3 * STRIDE)

    @pl.when(gy == 0)
    def _():
        for y in (-3, -2, -1):
            clear_column(cond_f, -3, y, T + 6)

    @pl.when(gy == n_gy - 1)
    def _():
        for y in (T, T + 1, T + 2):
            clear_column(cond_f, -3, y, T + 6)

    for x in (-2, -1, T, T + 1):
        prepare(flat_of(x, 0), T, 1)
    for y in (-2, -1, T, T + 1):
        prepare(flat_of(-2, y), T + 4, STRIDE)

    @pl.when(gx == 0)
    def _():
        clear(first_f, flat_of(-2, -4), 2 * STRIDE)

    @pl.when(gx == n_gx - 1)
    def _():
        clear(first_f, flat_of(T, -4), 2 * STRIDE)

    @pl.when(gy == 0)
    def _():
        for y in (-2, -1):
            clear_column(first_f, -2, y, T + 4)

    @pl.when(gy == n_gy - 1)
    def _():
        for y in (T, T + 1):
            clear_column(first_f, -2, y, T + 4)

    def around(ref, f, n, stride=1):
        def at(shift=0):
            return pl.ds(f + shift, n) if stride == 1 else pl.ds(f + shift, n, stride=stride)
        v = ref[at()]
        wa = w_above_f[at()]
        total = w_east_f[at()] * ref[at(STRIDE)]
        total = total + w_east_f[at(-STRIDE)] * ref[at(-STRIDE)]
        total = total + w_north_f[at()] * ref[at(1)]
        total = total + w_north_f[at(-1)] * ref[at(-1)]
        return total + wa * up(v) + down(wa * v), v

    def relaxed(src, f, n, stride=1):
        at = pl.ds(f, n) if stride == 1 else pl.ds(f, n, stride=stride)
        total, v = around(src, f, n, stride)
        return (1.0 - relax) * v + first_f[at] + dinv_f[at] * total

    def sweep(src, dst):
        def step(i, carry):
            f = pl.multiple_of(LO + i * CHUNK, 8)
            dst[pl.ds(f, CHUNK)] = relaxed(src, f, CHUNK)
            return carry
        lax.fori_loop(0, STEPS, step, 0, unroll=13)

    sweep(first_f, e_a_f)
    sweep(e_a_f, e_b_f)
    lc = [None] * 4
    for s in (2, 3, 0, 1):
        edge = (T - 1) * (s % 2)
        l_send[s] = relaxed(e_b_f, flat_of(edge, 0), T) if s < 2 else relaxed(e_b_f, flat_of(0, edge), T, STRIDE)
        lc[s] = remote(l_send.at[s], l_recv.at[s], l_ss.at[s], l_rs.at[s], sides[s])

    def last_sweep(x, carry):
        f = pl.multiple_of((x + 4) * STRIDE, 8)
        e_c_f[pl.ds(f, T)] = relaxed(e_b_f, f, T)
        return carry

    lax.fori_loop(0, T, last_sweep, 0, unroll=16)
    table = plane_sum(0)
    node = table[0:1].astype(jnp.int32)
    by_row = jnp.where(sub == node // NZ, table[4:5], 0.0)
    is_lane = (lax.broadcasted_iota(jnp.int32, (NZ, NZ), 0) == lax.rem(node, NZ)).astype(F32).astype(jnp.bfloat16)
    pieces = []
    for _ in range(3):
        pieces.append(by_row.astype(jnp.bfloat16).astype(F32))
        by_row = by_row - pieces[-1]
    by_node = lax.dot_general(jnp.concatenate(pieces).astype(jnp.bfloat16), is_lane, (((1,), (1,)), ((), ())),
                              preferred_element_type=F32)
    plane_resid = by_node[:8] + by_node[8:16] + by_node[16:]
    settle(inverse_recv, i_rs.at[0])
    corr = jnp.zeros((4, NZ), F32)
    for slot in range(DEPTH):
        rows = inverse if slot == DEPTH - 1 else inverse_recv.at[slot]
        acc = rows[:, pl.ds(0, NZ)] * plane_resid[0:1]
        for k in range(1, 8):
            acc = acc + rows[:, pl.ds(NZ * k, NZ)] * plane_resid[k:k + 1]
        place = 8 * (2 * gx + chip_y // 2) + lax.rem(chip_z + 1 + slot, DEPTH)
        corr = jnp.where(lane[:4] == place, jnp.sum(acc, axis=1, keepdims=True), corr)
    z_send[0] = jnp.where(sub // 4 == lax.rem(chip_y, 2), jnp.concatenate([corr, corr]), 0.0)
    z_send[1] = table
    send_depth(z_send, z_recv, 0)

    def products(bx):
        def add(r, carry):
            al, lal, rl = carry
            x = BLK * bx + r
            f = pl.multiple_of((x + 4) * STRIDE, 8)
            total, v = around(e_c_f, f, T)
            im = diag_f[pl.ds(f, T)] * v - total
            image_out[x] = im
            l_out[x] = v
            guess_out[x] = guess_f[pl.ds(f, T)]
            return al + im, lal + v * im, rl + v * resid_out[x]
        zero = jnp.zeros((T, NZ), F32)
        return [halves(v) for v in lax.fori_loop(0, BLK, add, (zero, zero, zero), unroll=16)]

    sums = [products(0), products(1)]

    for copy in lc:
        copy.wait_recv()
    for s in range(4):
        out = w_side[s] * l_recv[s ^ 1]
        lost = halves(out), halves(out * l_send[s])
        for i in range(2):
            bx, by = (s % 2, i) if s < 2 else (i, s % 2)
            for q in range(2):
                sums[bx][q][by] -= lost[q][i]
        at = pl.ds((T - 1) * T * (s % 2), T) if s < 2 else pl.ds((T - 1) * (s % 2), T, stride=T)
        image_f[at] -= out

    found = totals([sums[bx][q][by] for q in range(3) for bx, by in blocks])
    table = jnp.zeros((8, NZ), F32)
    for i, (bx, by) in enumerate(blocks):
        for q in range(3):
            table = jnp.where((lane == spot[bx][by]) & (sub == q), found[4 * q + i], table)
    send_plane(1, table)
    settle(z_recv, z_rs.at[0])
    send_plane(2, z_send[0] + jnp.sum(z_recv[:, 0], axis=0))
    near_out[pl.ds(0, DEPTH - 1)] = z_recv[:, 1]
    near_out[DEPTH - 1] = z_send[1]
    t_send[...] = plane_sum(1)
    send_depth(t_send, t_recv, 1)
    far_out[DEPTH - 1] = t_send[...]
    for copy in started:
        copy.wait_send()
    settle(inverse_recv, i_ss.at[0])
    settle(z_recv, z_ss.at[0])
    settle(p_recv.at[0], p_ss.at[0])
    settle(p_recv.at[1], p_ss.at[1])
    coarse_out[...] = plane_sum(2)
    settle(p_recv.at[2], p_ss.at[2])
    settle(t_recv, z_rs.at[1])
    far_out[pl.ds(0, DEPTH - 1)] = t_recv[...]
    settle(t_recv, z_ss.at[1])


def finish(guess, l, image, resid, q, faces, coarse, near, far, pressure, residual, press_v, resid_v, out_sem):
    gx, gy = lax.axis_index("gx"), lax.axis_index("gy")
    chip_z, chip_y = gy // 4, lax.rem(gy, 4)
    near_f, far_f = near.reshape(DEPTH * 8, NZ), far.reshape(DEPTH * 8, NZ)

    def pick(ref, i):
        return ref[pl.ds(i, DEPTH, stride=8)]

    c = coarse[...]
    node = pick(near_f, 0).astype(jnp.int32)
    in_y = lax.rem(node // 4, 4)
    at_row = lax.rem(node, 4) + 4 * lax.rem(in_y, 2)
    at_lane = lax.rem(node // 16, 8) + 8 * (2 * (node // NZ) + in_y // 2)
    block = jnp.zeros((DEPTH, NZ), F32)
    for s in range(DEPTH):
        line = jnp.broadcast_to(c[s:s + 1], (DEPTH, NZ))
        hit = jnp.take_along_axis(line, at_lane, axis=1, mode="promise_in_bounds")
        block = jnp.where(at_row == s, hit, block)
    east = pltpu.roll(block, NZ - 8, 1)
    lane = lax.broadcasted_iota(jnp.int32, (DEPTH, NZ), 1)
    north = jnp.where(lax.rem(lane, 8) == 7, pltpu.roll(pltpu.roll(block, 7, 1), DEPTH - 1, 0),
                      pltpu.roll(block, NZ - 1, 1))
    to_east, to_north = block - east, block - north
    numer = pick(far_f, 2) + block * pick(near_f, 4)
    denom = (pick(far_f, 1) + 2.0 * block * pick(far_f, 0) + pick(near_f, 1) * block * block
             + pick(near_f, 2) * to_east * to_east + pick(near_f, 3) * to_north * to_north)

    def total(v):
        return jnp.sum(jnp.sum(v, axis=0, keepdims=True), axis=1, keepdims=True)

    step = total(numer) / total(denom)
    turn = lax.rem(NZ - 16 * gx - 2 * chip_y, NZ)
    block, to_east, to_north = (pltpu.roll(v, turn, 1) for v in (block, to_east, to_north))

    def value(v, slot, at):
        return v[slot:slot + 1, at % NZ:at % NZ + 1]

    high = lax.broadcasted_iota(jnp.int32, (T, NZ), 0) >= BLK

    def spread(lower, upper):
        return step * jnp.where(high, upper, lower)

    last = DEPTH - 1
    mine = [spread(value(block, last, 8 * bx), value(block, last, 8 * bx + 1)) for bx in range(2)]
    flux_x = [faces[i] * spread(value(to_east, last, 8 * (i - 1)), value(to_east, last, 8 * (i - 1) + 1))
              for i in range(3)]
    below = [jnp.where(chip_y > 0, value(to_north, last, 8 * bx - 1), value(to_north, last - 1, 8 * bx + 7))
             for bx in range(2)]
    flux_y = [faces[3] * spread(*below)] + [
        faces[3 + i] * spread(value(to_north, last, i - 1), value(to_north, last, 8 + i - 1)) for i in (1, 2)]
    flat = resid_v.reshape(T * T, NZ)
    copies = []
    for part in range(4):
        rows = pl.ds(8 * part, 8)
        add = mine[part // 2]
        press_v[rows] = guess[rows] + step * l[rows] + add
        copies.append(pltpu.make_async_copy(press_v.at[rows], pressure.at[rows], out_sem.at[2 * part]))
        copies[-1].start()
        resid_v[rows] = resid[rows] - step * image[rows] - q[rows] * add
        if part == 0:
            resid_v[0] += flux_x[0]
        elif part == 1:
            resid_v[15] -= flux_x[1]
        elif part == 2:
            resid_v[16] += flux_x[1]
        else:
            resid_v[31] -= flux_x[2]
        some = slice(8 * part, 8 * part + 8)
        for y, i, sign in ((0, 0, 1.0), (15, 1, -1.0), (16, 1, 1.0), (31, 2, -1.0)):
            flat[pl.ds(8 * part * T + y, 8, stride=T)] += sign * flux_y[i][some]
        copies.append(pltpu.make_async_copy(resid_v.at[rows], residual.at[rows], out_sem.at[2 * part + 1]))
        copies[-1].start()
    for copy in copies:
        copy.wait()


def body(right_side, guess, conductivity, wet_mask, coarse_map, coarse_inverse):
    tile = jax.ShapeDtypeStruct((T, T, NZ), F32)
    table = jax.ShapeDtypeStruct((DEPTH, 8, NZ), F32)
    hbm = pl.BlockSpec(memory_space=pltpu.HBM)
    vmem = pl.BlockSpec(memory_space=pltpu.VMEM)
    field = pltpu.VMEM((ROWS, STRIDE, NZ), F32)
    dma = pltpu.SemaphoreType.DMA
    state = pl.pallas_call(
        kernel,
        out_shape=(tile, tile, tile, tile, tile, jax.ShapeDtypeStruct((6, T, NZ), F32),
                   jax.ShapeDtypeStruct((8, NZ), F32), table, table),
        in_specs=[pl.BlockSpec(memory_space=pltpu.SMEM)] + [hbm] * 5,
        out_specs=(vmem,) * 9,
        scratch_shapes=[
            pltpu.VMEM((3, ROWS, STRIDE, NZ), F32), pltpu.VMEM((T, T, NZ), jnp.int32),
        ] + [field] * 9 + [
            pltpu.VMEM((4, NODES), F32), pltpu.VMEM((DEPTH - 1, 4, NODES), F32),
            pltpu.VMEM((4, 2, T, NZ), F32), pltpu.VMEM((4, 2, T, NZ), F32),
            pltpu.VMEM((4, 6 * T + 8, NZ), F32), pltpu.VMEM((4, 6 * T + 8, NZ), F32),
            pltpu.VMEM((4, 24, NZ), F32), pltpu.VMEM((4, 24, NZ), F32),
            pltpu.VMEM((4, T, NZ), F32), pltpu.VMEM((4, T, NZ), F32),
            pltpu.VMEM((3, 8, NZ), F32), pltpu.VMEM((3, PLANE - 1, 8, NZ), F32),
            pltpu.VMEM((2, 8, NZ), F32), pltpu.VMEM((DEPTH - 1, 2, 8, NZ), F32),
            pltpu.VMEM((8, NZ), F32), pltpu.VMEM((DEPTH - 1, 8, NZ), F32),
            dma((5,)),
        ] + [dma((4,))] * 8 + [dma((3,))] * 2 + [dma((2,))] * 2 + [dma((1,))] * 2,
        compiler_params=pltpu.CompilerParams(
            collective_id=0, has_side_effects=True, vmem_limit_bytes=40 * 1024 * 1024),
    )(*(pltpu.with_memory_space_constraint(array, pltpu.HBM) for array in (
        coarse_map.transpose(0, 2, 1), coarse_inverse, right_side, guess, conductivity, wet_mask)))
    return pl.pallas_call(
        finish,
        out_shape=(tile, tile),
        in_specs=[vmem] * 9,
        out_specs=(hbm, hbm),
        scratch_shapes=[pltpu.VMEM((T, T, NZ), F32)] * 2 + [dma((8,))],
        compiler_params=pltpu.CompilerParams(vmem_limit_bytes=16 * 1024 * 1024),
    )(*state)


def solution(mesh):
    grid = P("gx", "gy", None)
    in_specs = (grid, grid, grid, grid, grid, P(("gx", "gy"), None))
    return jax.shard_map(body, mesh=mesh, in_specs=in_specs, out_specs=(grid, grid), check_vma=False)
```

```python
import jax
import jax.numpy as jnp
from jax import lax
from jax.experimental import pallas as pl
from jax.experimental.pallas import tpu as pltpu
from jax.sharding import PartitionSpec as P

F32 = jnp.float32
MESH = pl.DeviceIdType.MESH
BLK = 16
T = 32
NZ = 128
STRIDE = 40
ROWS = 44
FLAT = ROWS * STRIDE
NODES = 1024
PLANE, DEPTH = 32, 8
screen = 0.02
relax = 0.8
LO, CHUNK, STEPS = 72, 112, 13


def flat_of(x, y):
    return (x + 4) * STRIDE + y


def view(ref):
    return ref.reshape(FLAT, NZ)


def up(v):
    return pltpu.roll(v, NZ - 1, 1)


def down(v):
    return pltpu.roll(v, 1, 1)


def kernel(
    cmap, cinv, right, guess, conductivity, wet,
    guess_out, l_out, image_out, resid_out, q_out, faces_out, coarse_out, near_out, far_out,
    ext, mask, w_east, w_north, w_above, diag, dinv, first, e_a, e_b, e_c, inverse, inverse_recv,
    a_send, a_recv, b_send, b_recv, k_send, k_recv, l_send, l_recv,
    p_send, p_recv, z_send, z_recv, t_send, t_recv,
    load_sem, a_ss, a_rs, b_ss, b_rs, k_ss, k_rs, l_ss, l_rs, p_ss, p_rs, z_ss, z_rs, i_ss, i_rs,
):
    gx, gy = lax.axis_index("gx"), lax.axis_index("gy")
    n_gx, n_gy = lax.axis_size("gx"), lax.axis_size("gy")
    west = (lax.rem(gx + n_gx - 1, n_gx), gy)
    east = (lax.rem(gx + 1, n_gx), gy)
    south = (gx, lax.rem(gy + n_gy - 1, n_gy))
    north = (gx, lax.rem(gy + 1, n_gy))
    corners = [(px[0], py[1]) for px in (west, east) for py in (south, north)]
    sides = (west, east, south, north)
    chip_z, chip_y = gy // 4, lax.rem(gy, 4)
    chip_x, core = gx // 2, lax.rem(gx, 2)

    offsets = sorted(
        ((dx, dc, dy) for dx in range(4) for dc in range(2) for dy in range(4) if dx + dc + dy > 0),
        key=lambda o: (-min(o[0], 4 - o[0]) - min(o[2], 4 - o[2]), -o[1]))
    planes = (4, 3, 5, 2, 6, 1, 7)

    def plane_peer(o):
        return (lax.rem(chip_x + o[0], 4) * 2 + lax.rem(core + o[1], 2), chip_z * 4 + lax.rem(chip_y + o[2], 4))

    def plane_slot(o):
        return offsets.index(((4 - o[0]) % 4, o[1], (4 - o[2]) % 4))

    def depth_peer(k):
        return (gx, lax.rem(chip_z + k, DEPTH) * 4 + chip_y)

    own = (pl.ds(4, T), pl.ds(0, T))
    loads = [
        pltpu.make_async_copy(conductivity, ext.at[(0,) + own], load_sem.at[0]),
        pltpu.make_async_copy(wet, mask, load_sem.at[1]),
        pltpu.make_async_copy(guess, ext.at[(1,) + own], load_sem.at[2]),
        pltpu.make_async_copy(right, ext.at[(2,) + own], load_sem.at[3]),
        pltpu.make_async_copy(cinv, inverse, load_sem.at[4]),
    ]
    for copy in loads:
        copy.start()

    barrier = pltpu.get_barrier_semaphore()
    for peer in [depth_peer(k) for k in planes] + [plane_peer(o) for o in offsets] + corners + list(sides):
        pl.semaphore_signal(barrier, inc=1, device_id=peer, device_id_type=MESH)

    sub = lax.broadcasted_iota(jnp.int32, (8, NZ), 0)
    lane = lax.broadcasted_iota(jnp.int32, (8, NZ), 1)
    node_of = sub * NZ + lane
    nodes = [[cmap[bx, 0, by] for by in range(2)] for bx in range(2)]
    spot = [[16 * gx + 8 * bx + 2 * chip_y + by for by in range(2)] for bx in range(2)]
    packed = jnp.zeros((8, NZ), jnp.int32)
    for bx in range(2):
        for by in range(2):
            packed = jnp.where(sub == 2 * bx + by, nodes[bx][by], packed)
    packed = packed.astype(F32)
    started = []

    def remote(src, dst, ss, rs, peer):
        copy = pltpu.make_async_remote_copy(
            src_ref=src, dst_ref=dst, send_sem=ss, recv_sem=rs, device_id=peer, device_id_type=MESH)
        copy.start()
        started.append(copy)
        return copy

    loads[0].wait()
    loads[1].wait()

    def masked(r, carry):
        ext[0, r + 4, pl.ds(0, T)] = ext[0, r + 4, pl.ds(0, T)] * mask[r].astype(F32)
        return carry

    lax.fori_loop(0, T, masked, 0, unroll=16)
    loads[2].wait()
    cond_f, guess_f, right_f = (view(ext.at[a]) for a in range(3))
    fields = (cond_f, guess_f)

    def column(ref, y):
        return ref[pl.ds(flat_of(0, y), T, stride=STRIDE)]

    def row(ref, x):
        return ref[pl.ds(flat_of(x, 0), T)]

    def line(ref, s, n):
        at = n if s % 2 == 0 else T - 1 - n
        return row(ref, at) if s < 2 else column(ref, at)

    def put(ref, s, n, value):
        at = T + n if s % 2 == 0 else -1 - n
        if s < 2:
            ref[pl.ds(flat_of(at, 0), T)] = value
        else:
            ref[pl.ds(flat_of(0, at), T, stride=STRIDE)] = value

    for s in range(4):
        for a in range(2):
            a_send[s, a] = line(fields[a], s, 0)
    pl.semaphore_wait(barrier, 8 + len(planes) + len(offsets))
    ac = [remote(a_send.at[s], a_recv.at[s], a_ss.at[s], a_rs.at[s], sides[s]) for s in (2, 3, 0, 1)]
    ac = [ac[2], ac[3], ac[0], ac[1]]
    loads[3].wait()
    bc = [None] * 4
    for s in (2, 3, 0, 1):
        for i in range(2):
            for a in range(2):
                b_send[s, pl.ds(T * (2 * a + i), T)] = line(fields[a], s, 1 + i)
            b_send[s, pl.ds(T * (4 + i), T)] = line(right_f, s, i)
        b_send[s, pl.ds(T * 6, 8)] = packed
        bc[s] = remote(b_send.at[s], b_recv.at[s], b_ss.at[s], b_rs.at[s], sides[s])
    kc = []
    for q in range(4):
        sx, sy = q // 2, q % 2
        x3, y3 = (0, T - 3)[sx], (0, T - 3)[sy]
        x2, y2 = (0, T - 2)[sx], (0, T - 2)[sy]
        for a in range(2):
            for i in range(3):
                k_send[q, pl.ds(9 * a + 3 * i, 3)] = fields[a][pl.ds(flat_of(x3 + i, y3), 3)]
        k_send[q, pl.ds(22, 2)] = jnp.zeros((2, NZ), F32)
        for i in range(2):
            k_send[q, pl.ds(18 + 2 * i, 2)] = right_f[pl.ds(flat_of(x2 + i, y2), 2)]
        kc.append(remote(k_send.at[q], k_recv.at[q], k_ss.at[q], k_rs.at[q], corners[q]))

    pad = jnp.zeros((8, NZ), F32)
    wide = jnp.zeros((STRIDE, NZ), F32)
    for ref in [ext.at[a] for a in range(3)] + [w_east, w_north, w_above, dinv, first, e_a]:
        for r in (0, 1, 2, 3, 36, 37, 38, 39):
            ref[r] = wide
        for r in range(4, 36):
            ref[r, pl.ds(32, 8)] = pad
    for ref in (e_b,):
        view(ref)[pl.ds(0, LO)] = jnp.zeros((LO, NZ), F32)
        view(ref)[pl.ds(LO + CHUNK * STEPS, LO)] = jnp.zeros((LO, NZ), F32)
    for r in (3, 36):
        e_c[r] = wide
    for r in range(4, 36):
        e_c[r, pl.ds(32, 8)] = pad

    w_east_f, w_north_f, w_above_f, diag_f, dinv_f, first_f, e_a_f, e_b_f, e_c_f = (
        view(ref) for ref in (w_east, w_north, w_above, diag, dinv, first, e_a, e_b, e_c))
    resid_f, image_f = (ref.reshape(T * T, NZ) for ref in (resid_out, image_out))

    def prepare(f, n, stride):
        def at(shift=0):
            return pl.ds(f + shift, n) if stride == 1 else pl.ds(f + shift, n, stride=stride)
        c = cond_f[at()]
        g = guess_f[at()]
        we = jnp.minimum(c, cond_f[at(STRIDE)])
        ww = jnp.minimum(c, cond_f[at(-STRIDE)])
        wn = jnp.minimum(c, cond_f[at(1)])
        ws = jnp.minimum(c, cond_f[at(-1)])
        top = lax.broadcasted_iota(jnp.int32, (n, NZ), 1) == NZ - 1
        wa = jnp.where(top, 0.0, jnp.minimum(c, up(c)))
        w_east_f[at()] = we
        w_north_f[at()] = wn
        w_above_f[at()] = wa
        dg = screen + jnp.maximum(0.0, 1.0 - 2.0 * c) + ww + we + ws + wn + down(wa) + wa
        diag_f[at()] = dg
        total = ww * guess_f[at(-STRIDE)] + we * guess_f[at(STRIDE)]
        total = total + ws * guess_f[at(-1)] + wn * guess_f[at(1)]
        total = total + down(wa * g) + wa * up(g)
        r = right_f[at()] - dg * g + total
        di = relax / dg
        dinv_f[at()] = di
        first_f[at()] = di * r
        return r

    def own_rows(x, carry):
        resid_out[x] = prepare(pl.multiple_of((x + 4) * STRIDE, 8), T, 1)
        return carry

    lax.fori_loop(0, T, own_rows, 0, unroll=16)

    def around(ref, f, n, stride=1):
        def at(shift=0):
            return pl.ds(f + shift, n) if stride == 1 else pl.ds(f + shift, n, stride=stride)
        v = ref[at()]
        wa = w_above_f[at()]
        total = w_east_f[at()] * ref[at(STRIDE)]
        total = total + w_east_f[at(-STRIDE)] * ref[at(-STRIDE)]
        total = total + w_north_f[at()] * ref[at(1)]
        total = total + w_north_f[at(-1)] * ref[at(-1)]
        return total + wa * up(v) + down(wa * v), v

    def relaxed(src, f, n, stride=1):
        at = pl.ds(f, n) if stride == 1 else pl.ds(f, n, stride=stride)
        total, v = around(src, f, n, stride)
        return (1.0 - relax) * v + first_f[at] + dinv_f[at] * total

    def own_second(x, carry):
        f = pl.multiple_of((x + 4) * STRIDE, 8)
        e_a_f[pl.ds(f, T)] = relaxed(first_f, f, T)
        return carry

    lax.fori_loop(0, T, own_second, 0, unroll=16)

    loads[4].wait()
    for k in planes:
        pltpu.make_async_remote_copy(
            src_ref=inverse, dst_ref=inverse_recv.at[DEPTH - 1 - k], send_sem=i_ss.at[0], recv_sem=i_rs.at[0],
            device_id=depth_peer(k), device_id_type=MESH).start()

    def cells(bx):
        def add(r, carry):
            acc, kd = carry
            at = pl.ds(pl.multiple_of((4 + BLK * bx + r) * STRIDE, 8), T)
            q = screen + jnp.maximum(0.0, 1.0 - 2.0 * cond_f[at])
            q_out[BLK * bx + r] = q
            return acc + (right_f[at] - q * guess_f[at]), kd + q
        zero = jnp.zeros((T, NZ), F32)
        return lax.fori_loop(0, BLK, add, (zero, zero), unroll=16)

    def halves(v):
        return [v[:BLK], v[BLK:]]

    def face(c0, g0, c1, g1):
        w = jnp.minimum(c0, c1)
        return halves(w * (g0 - g1)), w

    sums, k_cell = [], []
    for bx in range(2):
        acc, kd = cells(bx)
        sums.append(halves(acc))
        k_cell.append(halves(kd))
    mid_x, mid_xw = face(row(cond_f, 15), row(guess_f, 15), row(cond_f, 16), row(guess_f, 16))
    mid_y, mid_yw = face(column(cond_f, 15), column(guess_f, 15), column(cond_f, 16), column(guess_f, 16))
    for i in range(2):
        sums[0][i] -= mid_x[i]
        sums[1][i] += mid_x[i]
        sums[i][0] -= mid_y[i]
        sums[i][1] += mid_y[i]

    def totals(parts):
        found = []
        for base in range(0, len(parts), 8):
            group = parts[base:base + 8]
            stack = jnp.zeros((8, NZ), F32)
            for i, value in enumerate(group):
                stack = jnp.where(sub == i, jnp.sum(value, axis=0, keepdims=True), stack)
            stack = jnp.sum(stack, axis=1, keepdims=True)
            found += [stack[i:i + 1] for i in range(len(group))]
        return found

    blocks = [(bx, by) for bx in range(2) for by in range(2)]
    wx, wy = halves(mid_xw), halves(mid_yw)
    found = totals([sums[bx][by] for bx, by in blocks] + [k_cell[bx][by] for bx, by in blocks] + wx + wy)
    here = [lane == spot[bx][by] for bx, by in blocks]
    cell = [[here[i] & (sub == q) for i in range(4)] for q in range(5)]
    table = jnp.zeros((8, NZ), F32)
    for i in range(4):
        table = jnp.where(cell[0][i], packed[i:i + 1], table)
        table = jnp.where(cell[1][i], found[4 + i], table)
        table = jnp.where(cell[4][i], found[i], table)
    for i in range(2):
        table = jnp.where(cell[2][i], found[8 + i], table)
        table = jnp.where(cell[3][2 * i], found[10 + i], table)

    inside = [jnp.where(there, 1.0, 0.0) for there in (gx > 0, gx < n_gx - 1, gy > 0, gy < n_gy - 1)]
    for copy in ac:
        copy.wait_recv()
    beside, out, w_side = [], [], []
    for s in range(4):
        cond_line, guess_line = a_recv[s ^ 1, 0] * inside[s], a_recv[s ^ 1, 1]
        beside.append(cond_line)
        w_side.append(jnp.minimum(a_send[s, 0], cond_line))
        out.append(halves(w_side[s] * (a_send[s, 1] - guess_line)))
    found = totals([out[bx][by] + out[2 + by][bx] for bx, by in blocks] + halves(w_side[1]) + halves(w_side[3]))
    for i in range(4):
        table = jnp.where(cell[4][i], table - found[i], table)
    for i in range(2):
        table = jnp.where(cell[2][2 + i], found[4 + i], table)
        table = jnp.where(cell[3][2 * i + 1], found[6 + i], table)

    def send_plane(stage, value):
        p_send[stage] = value
        for o in offsets:
            pltpu.make_async_remote_copy(
                src_ref=p_send.at[stage], dst_ref=p_recv.at[stage, plane_slot(o)], send_sem=p_ss.at[stage],
                recv_sem=p_rs.at[stage], device_id=plane_peer(o), device_id_type=MESH).start()

    def settle(buffer, sem):
        pltpu.make_async_copy(buffer, buffer, sem).wait()

    def plane_sum(stage):
        settle(p_recv.at[stage], p_rs.at[stage])
        return p_send[stage] + jnp.sum(p_recv[stage], axis=0)

    def send_depth(src, dst, stage):
        for k in planes:
            pltpu.make_async_remote_copy(
                src_ref=src, dst_ref=dst.at[DEPTH - 1 - k], send_sem=z_ss.at[stage],
                recv_sem=z_rs.at[stage], device_id=depth_peer(k), device_id_type=MESH).start()

    send_plane(0, table)

    def clear(ref, start, n):
        ref[pl.ds(start, n)] = jnp.zeros((n, NZ), F32)

    def clear_column(ref, x, y, n):
        ref[pl.ds(flat_of(x, y), n, stride=STRIDE)] = jnp.zeros((n, NZ), F32)

    for s in range(4):
        put(cond_f, s, 0, beside[s ^ 1])
        put(guess_f, s, 0, a_recv[s, 1])
    for i, w in enumerate((w_side[0], mid_xw, w_side[1], w_side[2], mid_yw, w_side[3])):
        faces_out[i] = w

    for x in (0, T - 1):
        resid_f[pl.ds(T * x, T)] = prepare(flat_of(x, 0), T, 1)
    for y in (0, T - 1):
        resid_f[pl.ds(y, T, stride=T)] = prepare(flat_of(0, y), T, STRIDE)

    for s in (2, 3, 0, 1):
        bc[s].wait_recv()
        for i in range(2):
            for a in range(2):
                put(fields[a], s, 1 + i, b_recv[s, pl.ds(T * (2 * a + i), T)])
            put(right_f, s, i, b_recv[s, pl.ds(T * (4 + i), T)])
    for q in range(4):
        kc[q].wait_recv()
        sx, sy = q // 2, q % 2
        x3, y3 = (T, -3)[sx], (T, -3)[sy]
        x2, y2 = (T, -2)[sx], (T, -2)[sy]
        for a in range(2):
            for i in range(3):
                fields[a][pl.ds(flat_of(x3 + i, y3), 3)] = k_recv[q, pl.ds(9 * a + 3 * i, 3)]
        for i in range(2):
            right_f[pl.ds(flat_of(x2 + i, y2), 2)] = k_recv[q, pl.ds(18 + 2 * i, 2)]

    @pl.when(gx == 0)
    def _():
        clear(cond_f, flat_of(-3, -4), 3 * STRIDE)

    @pl.when(gx == n_gx - 1)
    def _():
        clear(cond_f, flat_of(T, -4), 3 * STRIDE)

    @pl.when(gy == 0)
    def _():
        for y in (-3, -2, -1):
            clear_column(cond_f, -3, y, T + 6)

    @pl.when(gy == n_gy - 1)
    def _():
        for y in (T, T + 1, T + 2):
            clear_column(cond_f, -3, y, T + 6)

    for x in (-2, -1, T, T + 1):
        prepare(flat_of(x, 0), T, 1)
    for y in (-2, -1, T, T + 1):
        prepare(flat_of(-2, y), T + 4, STRIDE)

    @pl.when(gx == 0)
    def _():
        clear(first_f, flat_of(-2, -4), 2 * STRIDE)

    @pl.when(gx == n_gx - 1)
    def _():
        clear(first_f, flat_of(T, -4), 2 * STRIDE)

    @pl.when(gy == 0)
    def _():
        for y in (-2, -1):
            clear_column(first_f, -2, y, T + 4)

    @pl.when(gy == n_gy - 1)
    def _():
        for y in (T, T + 1):
            clear_column(first_f, -2, y, T + 4)

    def sweep(src, dst):
        def step(i, carry):
            f = pl.multiple_of(LO + i * CHUNK, 8)
            dst[pl.ds(f, CHUNK)] = relaxed(src, f, CHUNK)
            return carry
        lax.fori_loop(0, STEPS, step, 0, unroll=13)

    for x in (-2, -1, 0, 1, T - 2, T - 1, T, T + 1):
        e_a_f[pl.ds(flat_of(x, 0), T)] = relaxed(first_f, flat_of(x, 0), T)
    for y in (-2, -1, 0, 1, T - 2, T - 1, T, T + 1):
        at = flat_of(-2, y)
        e_a_f[pl.ds(at, T + 4, stride=STRIDE)] = relaxed(first_f, at, T + 4, STRIDE)
    sweep(e_a_f, e_b_f)
    lc = [None] * 4
    for s in (2, 3, 0, 1):
        edge = (T - 1) * (s % 2)
        l_send[s] = relaxed(e_b_f, flat_of(edge, 0), T) if s < 2 else relaxed(e_b_f, flat_of(0, edge), T, STRIDE)
        lc[s] = remote(l_send.at[s], l_recv.at[s], l_ss.at[s], l_rs.at[s], sides[s])

    def last_sweep(x, carry):
        f = pl.multiple_of((x + 4) * STRIDE, 8)
        e_c_f[pl.ds(f, T)] = relaxed(e_b_f, f, T)
        return carry

    lax.fori_loop(0, T, last_sweep, 0, unroll=16)
    def products(bx):
        def add(r, carry):
            al, lal, rl = carry
            x = BLK * bx + r
            f = pl.multiple_of((x + 4) * STRIDE, 8)
            total, v = around(e_c_f, f, T)
            im = diag_f[pl.ds(f, T)] * v - total
            image_out[x] = im
            l_out[x] = v
            guess_out[x] = guess_f[pl.ds(f, T)]
            return al + im, lal + v * im, rl + v * resid_out[x]
        zero = jnp.zeros((T, NZ), F32)
        return [halves(v) for v in lax.fori_loop(0, BLK, add, (zero, zero, zero), unroll=16)]

    sums = [products(0), products(1)]

    table = plane_sum(0)
    node = table[0:1].astype(jnp.int32)
    by_row = jnp.where(sub == node // NZ, table[4:5], 0.0)
    is_lane = (lax.broadcasted_iota(jnp.int32, (NZ, NZ), 0) == lax.rem(node, NZ)).astype(F32).astype(jnp.bfloat16)
    pieces = []
    for _ in range(3):
        pieces.append(by_row.astype(jnp.bfloat16).astype(F32))
        by_row = by_row - pieces[-1]
    by_node = lax.dot_general(jnp.concatenate(pieces).astype(jnp.bfloat16), is_lane, (((1,), (1,)), ((), ())),
                              preferred_element_type=F32)
    plane_resid = by_node[:8] + by_node[8:16] + by_node[16:]
    settle(inverse_recv, i_rs.at[0])
    corr = jnp.zeros((4, NZ), F32)
    for slot in range(DEPTH):
        rows = inverse if slot == DEPTH - 1 else inverse_recv.at[slot]
        acc = rows[:, pl.ds(0, NZ)] * plane_resid[0:1]
        for k in range(1, 8):
            acc = acc + rows[:, pl.ds(NZ * k, NZ)] * plane_resid[k:k + 1]
        place = 8 * (2 * gx + chip_y // 2) + lax.rem(chip_z + 1 + slot, DEPTH)
        corr = jnp.where(lane[:4] == place, jnp.sum(acc, axis=1, keepdims=True), corr)
    z_send[0] = jnp.where(sub // 4 == lax.rem(chip_y, 2), jnp.concatenate([corr, corr]), 0.0)
    z_send[1] = table
    send_depth(z_send, z_recv, 0)

    found = totals([sums[bx][q][by] for q in range(3) for bx, by in blocks])
    table = jnp.zeros((8, NZ), F32)
    for i in range(4):
        for q in range(3):
            table = jnp.where(cell[q][i], found[4 * q + i], table)

    for copy in lc:
        copy.wait_recv()
    losses = [[], []]
    outs = []
    for s in range(4):
        out = w_side[s] * l_recv[s ^ 1]
        outs.append(out)
        losses[0].append(halves(out))
        losses[1].append(halves(out * l_send[s]))
    lost = totals([losses[q][bx][by] + losses[q][2 + by][bx] for q in range(2) for bx, by in blocks])
    for i in range(4):
        for q in range(2):
            table = jnp.where(cell[q][i], table - lost[4 * q + i], table)
    send_plane(1, table)
    for s in range(4):
        at = pl.ds((T - 1) * T * (s % 2), T) if s < 2 else pl.ds((T - 1) * (s % 2), T, stride=T)
        image_f[at] -= outs[s]
    settle(z_recv, z_rs.at[0])
    send_plane(2, z_send[0] + jnp.sum(z_recv[:, 0], axis=0))
    near_out[pl.ds(0, DEPTH - 1)] = z_recv[:, 1]
    near_out[DEPTH - 1] = z_send[1]
    t_send[...] = plane_sum(1)
    send_depth(t_send, t_recv, 1)
    far_out[DEPTH - 1] = t_send[...]
    for copy in started:
        copy.wait_send()
    settle(inverse_recv, i_ss.at[0])
    settle(z_recv, z_ss.at[0])
    settle(p_recv.at[0], p_ss.at[0])
    settle(p_recv.at[1], p_ss.at[1])
    coarse_out[...] = plane_sum(2)
    settle(p_recv.at[2], p_ss.at[2])
    settle(t_recv, z_rs.at[1])
    far_out[pl.ds(0, DEPTH - 1)] = t_recv[...]
    settle(t_recv, z_ss.at[1])


def finish(guess, l, image, resid, q, faces, coarse, near, far, pressure, residual, press_v, resid_v, out_sem):
    gx, gy = lax.axis_index("gx"), lax.axis_index("gy")
    chip_z, chip_y = gy // 4, lax.rem(gy, 4)
    near_f, far_f = near.reshape(DEPTH * 8, NZ), far.reshape(DEPTH * 8, NZ)

    def pick(ref, i):
        return ref[pl.ds(i, DEPTH, stride=8)]

    c = coarse[...]
    node = pick(near_f, 0).astype(jnp.int32)
    in_y = lax.rem(node // 4, 4)
    at_row = lax.rem(node, 4) + 4 * lax.rem(in_y, 2)
    at_lane = lax.rem(node // 16, 8) + 8 * (2 * (node // NZ) + in_y // 2)
    block = jnp.zeros((DEPTH, NZ), F32)
    for s in range(DEPTH):
        line = jnp.broadcast_to(c[s:s + 1], (DEPTH, NZ))
        hit = jnp.take_along_axis(line, at_lane, axis=1, mode="promise_in_bounds")
        block = jnp.where(at_row == s, hit, block)
    east = pltpu.roll(block, NZ - 8, 1)
    lane = lax.broadcasted_iota(jnp.int32, (DEPTH, NZ), 1)
    north = jnp.where(lax.rem(lane, 8) == 7, pltpu.roll(pltpu.roll(block, 7, 1), DEPTH - 1, 0),
                      pltpu.roll(block, NZ - 1, 1))
    to_east, to_north = block - east, block - north
    numer = pick(far_f, 2) + block * pick(near_f, 4)
    denom = (pick(far_f, 1) + 2.0 * block * pick(far_f, 0) + pick(near_f, 1) * block * block
             + pick(near_f, 2) * to_east * to_east + pick(near_f, 3) * to_north * to_north)

    def total(v):
        return jnp.sum(jnp.sum(v, axis=0, keepdims=True), axis=1, keepdims=True)

    step = total(numer) / total(denom)
    turn = lax.rem(NZ - 16 * gx - 2 * chip_y, NZ)
    block, to_east, to_north = (pltpu.roll(v, turn, 1) for v in (block, to_east, to_north))

    def value(v, slot, at):
        return v[slot:slot + 1, at % NZ:at % NZ + 1]

    high = lax.broadcasted_iota(jnp.int32, (T, NZ), 0) >= BLK

    def spread(lower, upper):
        return step * jnp.where(high, upper, lower)

    last = DEPTH - 1
    mine = [spread(value(block, last, 8 * bx), value(block, last, 8 * bx + 1)) for bx in range(2)]
    flux_x = [faces[i] * spread(value(to_east, last, 8 * (i - 1)), value(to_east, last, 8 * (i - 1) + 1))
              for i in range(3)]
    below = [jnp.where(chip_y > 0, value(to_north, last, 8 * bx - 1), value(to_north, last - 1, 8 * bx + 7))
             for bx in range(2)]
    flux_y = [faces[3] * spread(*below)] + [
        faces[3 + i] * spread(value(to_north, last, i - 1), value(to_north, last, 8 + i - 1)) for i in (1, 2)]
    flat = resid_v.reshape(T * T, NZ)
    copies = []
    for part in range(4):
        rows = pl.ds(8 * part, 8)
        add = mine[part // 2]
        press_v[rows] = guess[rows] + step * l[rows] + add
        copies.append(pltpu.make_async_copy(press_v.at[rows], pressure.at[rows], out_sem.at[2 * part]))
        copies[-1].start()
        resid_v[rows] = resid[rows] - step * image[rows] - q[rows] * add
        if part == 0:
            resid_v[0] += flux_x[0]
        elif part == 1:
            resid_v[15] -= flux_x[1]
        elif part == 2:
            resid_v[16] += flux_x[1]
        else:
            resid_v[31] -= flux_x[2]
        some = slice(8 * part, 8 * part + 8)
        for y, i, sign in ((0, 0, 1.0), (15, 1, -1.0), (16, 1, 1.0), (31, 2, -1.0)):
            flat[pl.ds(8 * part * T + y, 8, stride=T)] += sign * flux_y[i][some]
        copies.append(pltpu.make_async_copy(resid_v.at[rows], residual.at[rows], out_sem.at[2 * part + 1]))
        copies[-1].start()
    for copy in copies:
        copy.wait()


def body(right_side, guess, conductivity, wet_mask, coarse_map, coarse_inverse):
    tile = jax.ShapeDtypeStruct((T, T, NZ), F32)
    table = jax.ShapeDtypeStruct((DEPTH, 8, NZ), F32)
    hbm = pl.BlockSpec(memory_space=pltpu.HBM)
    vmem = pl.BlockSpec(memory_space=pltpu.VMEM)
    field = pltpu.VMEM((ROWS, STRIDE, NZ), F32)
    dma = pltpu.SemaphoreType.DMA
    state = pl.pallas_call(
        kernel,
        out_shape=(tile, tile, tile, tile, tile, jax.ShapeDtypeStruct((6, T, NZ), F32),
                   jax.ShapeDtypeStruct((8, NZ), F32), table, table),
        in_specs=[pl.BlockSpec(memory_space=pltpu.SMEM)] + [hbm] * 5,
        out_specs=(vmem,) * 9,
        scratch_shapes=[
            pltpu.VMEM((3, ROWS, STRIDE, NZ), F32), pltpu.VMEM((T, T, NZ), jnp.int32),
        ] + [field] * 9 + [
            pltpu.VMEM((4, NODES), F32), pltpu.VMEM((DEPTH - 1, 4, NODES), F32),
            pltpu.VMEM((4, 2, T, NZ), F32), pltpu.VMEM((4, 2, T, NZ), F32),
            pltpu.VMEM((4, 6 * T + 8, NZ), F32), pltpu.VMEM((4, 6 * T + 8, NZ), F32),
            pltpu.VMEM((4, 24, NZ), F32), pltpu.VMEM((4, 24, NZ), F32),
            pltpu.VMEM((4, T, NZ), F32), pltpu.VMEM((4, T, NZ), F32),
            pltpu.VMEM((3, 8, NZ), F32), pltpu.VMEM((3, PLANE - 1, 8, NZ), F32),
            pltpu.VMEM((2, 8, NZ), F32), pltpu.VMEM((DEPTH - 1, 2, 8, NZ), F32),
            pltpu.VMEM((8, NZ), F32), pltpu.VMEM((DEPTH - 1, 8, NZ), F32),
            dma((5,)),
        ] + [dma((4,))] * 8 + [dma((3,))] * 2 + [dma((2,))] * 2 + [dma((1,))] * 2,
        compiler_params=pltpu.CompilerParams(
            collective_id=0, has_side_effects=True, vmem_limit_bytes=40 * 1024 * 1024),
    )(*(pltpu.with_memory_space_constraint(array, pltpu.HBM) for array in (
        coarse_map.transpose(0, 2, 1), coarse_inverse, right_side, guess, conductivity, wet_mask)))
    return pl.pallas_call(
        finish,
        out_shape=(tile, tile),
        in_specs=[vmem] * 9,
        out_specs=(hbm, hbm),
        scratch_shapes=[pltpu.VMEM((T, T, NZ), F32)] * 2 + [dma((8,))],
        compiler_params=pltpu.CompilerParams(vmem_limit_bytes=16 * 1024 * 1024),
    )(*state)


def solution(mesh):
    grid = P("gx", "gy", None)
    in_specs = (grid, grid, grid, grid, grid, P(("gx", "gy"), None))
    return jax.shard_map(body, mesh=mesh, in_specs=in_specs, out_specs=(grid, grid), check_vma=False)
```

```python
import jax
import jax.numpy as jnp
from jax import lax
from jax.experimental import pallas as pl
from jax.experimental.pallas import tpu as pltpu
from jax.sharding import PartitionSpec as P

F32 = jnp.float32
MESH = pl.DeviceIdType.MESH
BLK = 16
T = 32
NZ = 128
STRIDE = 40
ROWS = 44
FLAT = ROWS * STRIDE
NODES = 1024
PLANE, DEPTH = 32, 8
screen = 0.02
relax = 0.8
LO, CHUNK, STEPS = 72, 112, 13


def flat_of(x, y):
    return (x + 4) * STRIDE + y


def view(ref):
    return ref.reshape(FLAT, NZ)


def up(v):
    return pltpu.roll(v, NZ - 1, 1)


def down(v):
    return pltpu.roll(v, 1, 1)


def kernel(
    cmap, cinv, right, guess, conductivity, wet,
    guess_out, l_out, image_out, resid_out, q_out, faces_out, coarse_out, near_out, far_out,
    ext, mask, w_east, w_north, w_above, diag, dinv, first, e_a, e_b, e_c, inverse, inverse_recv,
    a_send, a_recv, b_send, b_recv, k_send, k_recv, l_send, l_recv,
    p_send, p_recv, z_send, z_recv, t_send, t_recv,
    load_sem, a_ss, a_rs, b_ss, b_rs, k_ss, k_rs, l_ss, l_rs, p_ss, p_rs, z_ss, z_rs, i_ss, i_rs,
):
    gx, gy = lax.axis_index("gx"), lax.axis_index("gy")
    n_gx, n_gy = lax.axis_size("gx"), lax.axis_size("gy")
    west = (lax.rem(gx + n_gx - 1, n_gx), gy)
    east = (lax.rem(gx + 1, n_gx), gy)
    south = (gx, lax.rem(gy + n_gy - 1, n_gy))
    north = (gx, lax.rem(gy + 1, n_gy))
    corners = [(px[0], py[1]) for px in (west, east) for py in (south, north)]
    sides = (west, east, south, north)
    chip_z, chip_y = gy // 4, lax.rem(gy, 4)
    chip_x, core = gx // 2, lax.rem(gx, 2)

    offsets = sorted(
        ((dx, dc, dy) for dx in range(4) for dc in range(2) for dy in range(4) if dx + dc + dy > 0),
        key=lambda o: (-min(o[0], 4 - o[0]) - min(o[2], 4 - o[2]), -o[1]))
    planes = (4, 3, 5, 2, 6, 1, 7)

    def plane_peer(o):
        return (lax.rem(chip_x + o[0], 4) * 2 + lax.rem(core + o[1], 2), chip_z * 4 + lax.rem(chip_y + o[2], 4))

    def plane_slot(o):
        return offsets.index(((4 - o[0]) % 4, o[1], (4 - o[2]) % 4))

    def depth_peer(k):
        return (gx, lax.rem(chip_z + k, DEPTH) * 4 + chip_y)

    own = (pl.ds(4, T), pl.ds(0, T))
    loads = [
        pltpu.make_async_copy(conductivity, ext.at[(0,) + own], load_sem.at[0]),
        pltpu.make_async_copy(wet, mask, load_sem.at[1]),
        pltpu.make_async_copy(guess, ext.at[(1,) + own], load_sem.at[2]),
        pltpu.make_async_copy(right, ext.at[(2,) + own], load_sem.at[3]),
        pltpu.make_async_copy(cinv, inverse, load_sem.at[4]),
    ]
    for copy in loads:
        copy.start()

    barrier = pltpu.get_barrier_semaphore()
    for peer in [depth_peer(k) for k in planes] + [plane_peer(o) for o in offsets] + corners + list(sides):
        pl.semaphore_signal(barrier, inc=1, device_id=peer, device_id_type=MESH)

    sub = lax.broadcasted_iota(jnp.int32, (8, NZ), 0)
    lane = lax.broadcasted_iota(jnp.int32, (8, NZ), 1)
    node_of = sub * NZ + lane
    nodes = [[cmap[bx, 0, by] for by in range(2)] for bx in range(2)]
    spot = [[16 * gx + 8 * bx + 2 * chip_y + by for by in range(2)] for bx in range(2)]
    packed = jnp.zeros((8, NZ), jnp.int32)
    for bx in range(2):
        for by in range(2):
            packed = jnp.where(sub == 2 * bx + by, nodes[bx][by], packed)
    packed = packed.astype(F32)
    started = []

    def remote(src, dst, ss, rs, peer):
        copy = pltpu.make_async_remote_copy(
            src_ref=src, dst_ref=dst, send_sem=ss, recv_sem=rs, device_id=peer, device_id_type=MESH)
        copy.start()
        started.append(copy)
        return copy

    loads[0].wait()
    loads[1].wait()

    def masked(r, carry):
        ext[0, r + 4, pl.ds(0, T)] = ext[0, r + 4, pl.ds(0, T)] * mask[r].astype(F32)
        return carry

    lax.fori_loop(0, T, masked, 0, unroll=16)
    loads[2].wait()
    cond_f, guess_f, right_f = (view(ext.at[a]) for a in range(3))
    fields = (cond_f, guess_f)

    def column(ref, y):
        return ref[pl.ds(flat_of(0, y), T, stride=STRIDE)]

    def row(ref, x):
        return ref[pl.ds(flat_of(x, 0), T)]

    def line(ref, s, n):
        at = n if s % 2 == 0 else T - 1 - n
        return row(ref, at) if s < 2 else column(ref, at)

    def put(ref, s, n, value):
        at = T + n if s % 2 == 0 else -1 - n
        if s < 2:
            ref[pl.ds(flat_of(at, 0), T)] = value
        else:
            ref[pl.ds(flat_of(0, at), T, stride=STRIDE)] = value

    for s in range(4):
        for a in range(2):
            a_send[s, a] = line(fields[a], s, 0)
    pl.semaphore_wait(barrier, 8 + len(planes) + len(offsets))
    ac = [remote(a_send.at[s], a_recv.at[s], a_ss.at[s], a_rs.at[s], sides[s]) for s in (2, 3, 0, 1)]
    ac = [ac[2], ac[3], ac[0], ac[1]]
    loads[3].wait()
    bc = [None] * 4
    for s in (2, 3, 0, 1):
        for i in range(2):
            for a in range(2):
                b_send[s, pl.ds(T * (2 * a + i), T)] = line(fields[a], s, 1 + i)
            b_send[s, pl.ds(T * (4 + i), T)] = line(right_f, s, i)
        b_send[s, pl.ds(T * 6, 8)] = packed
        bc[s] = remote(b_send.at[s], b_recv.at[s], b_ss.at[s], b_rs.at[s], sides[s])
    kc = []
    for q in range(4):
        sx, sy = q // 2, q % 2
        x3, y3 = (0, T - 3)[sx], (0, T - 3)[sy]
        x2, y2 = (0, T - 2)[sx], (0, T - 2)[sy]
        for a in range(2):
            for i in range(3):
                k_send[q, pl.ds(9 * a + 3 * i, 3)] = fields[a][pl.ds(flat_of(x3 + i, y3), 3)]
        k_send[q, pl.ds(22, 2)] = jnp.zeros((2, NZ), F32)
        for i in range(2):
            k_send[q, pl.ds(18 + 2 * i, 2)] = right_f[pl.ds(flat_of(x2 + i, y2), 2)]
        kc.append(remote(k_send.at[q], k_recv.at[q], k_ss.at[q], k_rs.at[q], corners[q]))

    pad = jnp.zeros((8, NZ), F32)
    wide = jnp.zeros((STRIDE, NZ), F32)
    for ref in [ext.at[a] for a in range(3)] + [w_east, w_north, w_above, dinv, first, e_a]:
        for r in (0, 1, 2, 3, 36, 37, 38, 39):
            ref[r] = wide
        for r in range(4, 36):
            ref[r, pl.ds(32, 8)] = pad
    for ref in (e_b,):
        view(ref)[pl.ds(0, LO)] = jnp.zeros((LO, NZ), F32)
        view(ref)[pl.ds(LO + CHUNK * STEPS, LO)] = jnp.zeros((LO, NZ), F32)
    for r in (3, 36):
        e_c[r] = wide
    for r in range(4, 36):
        e_c[r, pl.ds(32, 8)] = pad

    w_east_f, w_north_f, w_above_f, diag_f, dinv_f, first_f, e_a_f, e_b_f, e_c_f = (
        view(ref) for ref in (w_east, w_north, w_above, diag, dinv, first, e_a, e_b, e_c))
    resid_f, image_f = (ref.reshape(T * T, NZ) for ref in (resid_out, image_out))

    def prepare(f, n, stride):
        def at(shift=0):
            return pl.ds(f + shift, n) if stride == 1 else pl.ds(f + shift, n, stride=stride)
        c = cond_f[at()]
        g = guess_f[at()]
        we = jnp.minimum(c, cond_f[at(STRIDE)])
        ww = jnp.minimum(c, cond_f[at(-STRIDE)])
        wn = jnp.minimum(c, cond_f[at(1)])
        ws = jnp.minimum(c, cond_f[at(-1)])
        top = lax.broadcasted_iota(jnp.int32, (n, NZ), 1) == NZ - 1
        wa = jnp.where(top, 0.0, jnp.minimum(c, up(c)))
        w_east_f[at()] = we
        w_north_f[at()] = wn
        w_above_f[at()] = wa
        dg = screen + jnp.maximum(0.0, 1.0 - 2.0 * c) + ww + we + ws + wn + down(wa) + wa
        diag_f[at()] = dg
        total = ww * guess_f[at(-STRIDE)] + we * guess_f[at(STRIDE)]
        total = total + ws * guess_f[at(-1)] + wn * guess_f[at(1)]
        total = total + down(wa * g) + wa * up(g)
        r = right_f[at()] - dg * g + total
        di = relax / dg
        dinv_f[at()] = di
        first_f[at()] = di * r
        return r

    def own_rows(x, carry):
        resid_out[x] = prepare(pl.multiple_of((x + 4) * STRIDE, 8), T, 1)
        return carry

    lax.fori_loop(0, T, own_rows, 0, unroll=16)

    def around(ref, f, n, stride=1):
        def at(shift=0):
            return pl.ds(f + shift, n) if stride == 1 else pl.ds(f + shift, n, stride=stride)
        v = ref[at()]
        wa = w_above_f[at()]
        total = w_east_f[at()] * ref[at(STRIDE)]
        total = total + w_east_f[at(-STRIDE)] * ref[at(-STRIDE)]
        total = total + w_north_f[at()] * ref[at(1)]
        total = total + w_north_f[at(-1)] * ref[at(-1)]
        return total + wa * up(v) + down(wa * v), v

    def relaxed(src, f, n, stride=1):
        at = pl.ds(f, n) if stride == 1 else pl.ds(f, n, stride=stride)
        total, v = around(src, f, n, stride)
        return (1.0 - relax) * v + first_f[at] + dinv_f[at] * total

    def own_second(x, carry):
        f = pl.multiple_of((x + 4) * STRIDE, 8)
        e_a_f[pl.ds(f, T)] = relaxed(first_f, f, T)
        return carry

    lax.fori_loop(0, T, own_second, 0, unroll=16)

    loads[4].wait()
    for k in planes:
        pltpu.make_async_remote_copy(
            src_ref=inverse, dst_ref=inverse_recv.at[DEPTH - 1 - k], send_sem=i_ss.at[0], recv_sem=i_rs.at[0],
            device_id=depth_peer(k), device_id_type=MESH).start()

    def cells(bx):
        def add(r, carry):
            acc, kd = carry
            at = pl.ds(pl.multiple_of((4 + BLK * bx + r) * STRIDE, 8), T)
            q = screen + jnp.maximum(0.0, 1.0 - 2.0 * cond_f[at])
            q_out[BLK * bx + r] = q
            return acc + (right_f[at] - q * guess_f[at]), kd + q
        zero = jnp.zeros((T, NZ), F32)
        return lax.fori_loop(0, BLK, add, (zero, zero), unroll=16)

    def halves(v):
        return [v[:BLK], v[BLK:]]

    def face(c0, g0, c1, g1):
        w = jnp.minimum(c0, c1)
        return halves(w * (g0 - g1)), w

    sums, k_cell = [], []
    for bx in range(2):
        acc, kd = cells(bx)
        sums.append(halves(acc))
        k_cell.append(halves(kd))
    mid_x, mid_xw = face(row(cond_f, 15), row(guess_f, 15), row(cond_f, 16), row(guess_f, 16))
    mid_y, mid_yw = face(column(cond_f, 15), column(guess_f, 15), column(cond_f, 16), column(guess_f, 16))
    for i in range(2):
        sums[0][i] -= mid_x[i]
        sums[1][i] += mid_x[i]
        sums[i][0] -= mid_y[i]
        sums[i][1] += mid_y[i]

    def totals(parts):
        found = []
        for base in range(0, len(parts), 8):
            group = parts[base:base + 8]
            stack = jnp.zeros((8, NZ), F32)
            for i, value in enumerate(group):
                stack = jnp.where(sub == i, jnp.sum(value, axis=0, keepdims=True), stack)
            stack = jnp.sum(stack, axis=1, keepdims=True)
            found += [stack[i:i + 1] for i in range(len(group))]
        return found

    blocks = [(bx, by) for bx in range(2) for by in range(2)]
    wx, wy = halves(mid_xw), halves(mid_yw)
    found = totals([sums[bx][by] for bx, by in blocks] + [k_cell[bx][by] for bx, by in blocks] + wx + wy)
    here = [lane == spot[bx][by] for bx, by in blocks]
    cell = [[here[i] & (sub == q) for i in range(4)] for q in range(5)]
    table = jnp.zeros((8, NZ), F32)
    for i in range(4):
        table = jnp.where(cell[0][i], packed[i:i + 1], table)
        table = jnp.where(cell[1][i], found[4 + i], table)
        table = jnp.where(cell[4][i], found[i], table)
    for i in range(2):
        table = jnp.where(cell[2][i], found[8 + i], table)
        table = jnp.where(cell[3][2 * i], found[10 + i], table)

    inside = [jnp.where(there, 1.0, 0.0) for there in (gx > 0, gx < n_gx - 1, gy > 0, gy < n_gy - 1)]
    for copy in ac:
        copy.wait_recv()
    beside, out, w_side = [], [], []
    for s in range(4):
        cond_line, guess_line = a_recv[s ^ 1, 0] * inside[s], a_recv[s ^ 1, 1]
        beside.append(cond_line)
        w_side.append(jnp.minimum(a_send[s, 0], cond_line))
        out.append(halves(w_side[s] * (a_send[s, 1] - guess_line)))
    found = totals([out[bx][by] + out[2 + by][bx] for bx, by in blocks] + halves(w_side[1]) + halves(w_side[3]))
    for i in range(4):
        table = jnp.where(cell[4][i], table - found[i], table)
    for i in range(2):
        table = jnp.where(cell[2][2 + i], found[4 + i], table)
        table = jnp.where(cell[3][2 * i + 1], found[6 + i], table)

    def send_plane(stage, value):
        p_send[stage] = value
        for o in offsets:
            pltpu.make_async_remote_copy(
                src_ref=p_send.at[stage], dst_ref=p_recv.at[stage, plane_slot(o)], send_sem=p_ss.at[stage],
                recv_sem=p_rs.at[stage], device_id=plane_peer(o), device_id_type=MESH).start()

    def settle(buffer, sem):
        pltpu.make_async_copy(buffer, buffer, sem).wait()

    def plane_sum(stage):
        settle(p_recv.at[stage], p_rs.at[stage])
        return p_send[stage] + jnp.sum(p_recv[stage], axis=0)

    def send_depth(src, dst, stage):
        for k in planes:
            pltpu.make_async_remote_copy(
                src_ref=src, dst_ref=dst.at[DEPTH - 1 - k], send_sem=z_ss.at[stage],
                recv_sem=z_rs.at[stage], device_id=depth_peer(k), device_id_type=MESH).start()

    send_plane(0, table)

    def clear(ref, start, n):
        ref[pl.ds(start, n)] = jnp.zeros((n, NZ), F32)

    def clear_column(ref, x, y, n):
        ref[pl.ds(flat_of(x, y), n, stride=STRIDE)] = jnp.zeros((n, NZ), F32)

    for s in range(4):
        put(cond_f, s, 0, beside[s ^ 1])
        put(guess_f, s, 0, a_recv[s, 1])
    for i, w in enumerate((w_side[0], mid_xw, w_side[1], w_side[2], mid_yw, w_side[3])):
        faces_out[i] = w

    for x in (0, T - 1):
        resid_f[pl.ds(T * x, T)] = prepare(flat_of(x, 0), T, 1)
    for y in (0, T - 1):
        resid_f[pl.ds(y, T, stride=T)] = prepare(flat_of(0, y), T, STRIDE)

    for s in (2, 3, 0, 1):
        bc[s].wait_recv()
        for i in range(2):
            for a in range(2):
                put(fields[a], s, 1 + i, b_recv[s, pl.ds(T * (2 * a + i), T)])
            put(right_f, s, i, b_recv[s, pl.ds(T * (4 + i), T)])
    for q in range(4):
        kc[q].wait_recv()
        sx, sy = q // 2, q % 2
        x3, y3 = (T, -3)[sx], (T, -3)[sy]
        x2, y2 = (T, -2)[sx], (T, -2)[sy]
        for a in range(2):
            for i in range(3):
                fields[a][pl.ds(flat_of(x3 + i, y3), 3)] = k_recv[q, pl.ds(9 * a + 3 * i, 3)]
        for i in range(2):
            right_f[pl.ds(flat_of(x2 + i, y2), 2)] = k_recv[q, pl.ds(18 + 2 * i, 2)]

    @pl.when(gx == 0)
    def _():
        clear(cond_f, flat_of(-3, -4), 3 * STRIDE)

    @pl.when(gx == n_gx - 1)
    def _():
        clear(cond_f, flat_of(T, -4), 3 * STRIDE)

    @pl.when(gy == 0)
    def _():
        for y in (-3, -2, -1):
            clear_column(cond_f, -3, y, T + 6)

    @pl.when(gy == n_gy - 1)
    def _():
        for y in (T, T + 1, T + 2):
            clear_column(cond_f, -3, y, T + 6)

    for x in (-2, -1, T, T + 1):
        prepare(flat_of(x, 0), T, 1)
    for y in (-2, -1, T, T + 1):
        prepare(flat_of(-2, y), T + 4, STRIDE)

    @pl.when(gx == 0)
    def _():
        clear(first_f, flat_of(-2, -4), 2 * STRIDE)

    @pl.when(gx == n_gx - 1)
    def _():
        clear(first_f, flat_of(T, -4), 2 * STRIDE)

    @pl.when(gy == 0)
    def _():
        for y in (-2, -1):
            clear_column(first_f, -2, y, T + 4)

    @pl.when(gy == n_gy - 1)
    def _():
        for y in (T, T + 1):
            clear_column(first_f, -2, y, T + 4)

    def sweep(src, dst):
        def step(i, carry):
            f = pl.multiple_of(LO + i * CHUNK, 8)
            dst[pl.ds(f, CHUNK)] = relaxed(src, f, CHUNK)
            return carry
        lax.fori_loop(0, STEPS, step, 0, unroll=13)

    for x in (-2, -1, 0, 1, T - 2, T - 1, T, T + 1):
        e_a_f[pl.ds(flat_of(x, 0), T)] = relaxed(first_f, flat_of(x, 0), T)
    for y in (-2, -1, 0, 1, T - 2, T - 1, T, T + 1):
        at = flat_of(-2, y)
        e_a_f[pl.ds(at, T + 4, stride=STRIDE)] = relaxed(first_f, at, T + 4, STRIDE)
    sweep(e_a_f, e_b_f)
    lc = [None] * 4
    for s in (2, 3, 0, 1):
        edge = (T - 1) * (s % 2)
        l_send[s] = relaxed(e_b_f, flat_of(edge, 0), T) if s < 2 else relaxed(e_b_f, flat_of(0, edge), T, STRIDE)
        lc[s] = remote(l_send.at[s], l_recv.at[s], l_ss.at[s], l_rs.at[s], sides[s])

    def last_sweep(x, carry):
        f = pl.multiple_of((x + 4) * STRIDE, 8)
        e_c_f[pl.ds(f, T)] = relaxed(e_b_f, f, T)
        return carry

    lax.fori_loop(0, T, last_sweep, 0, unroll=16)
    def products(bx):
        def add(r, carry):
            al, lal, rl = carry
            x = BLK * bx + r
            f = pl.multiple_of((x + 4) * STRIDE, 8)
            total, v = around(e_c_f, f, T)
            im = diag_f[pl.ds(f, T)] * v - total
            image_out[x] = im
            l_out[x] = v
            guess_out[x] = guess_f[pl.ds(f, T)]
            return al + im, lal + v * im, rl + v * resid_out[x]
        zero = jnp.zeros((T, NZ), F32)
        return [halves(v) for v in lax.fori_loop(0, BLK, add, (zero, zero, zero), unroll=16)]

    sums = [products(0), products(1)]

    table = plane_sum(0)
    node = table[0:1].astype(jnp.int32)
    by_row = jnp.where(sub == node // NZ, table[4:5], 0.0)
    is_lane = (lax.broadcasted_iota(jnp.int32, (NZ, NZ), 0) == lax.rem(node, NZ)).astype(F32).astype(jnp.bfloat16)
    pieces = []
    for _ in range(3):
        pieces.append(by_row.astype(jnp.bfloat16).astype(F32))
        by_row = by_row - pieces[-1]
    by_node = lax.dot_general(jnp.concatenate(pieces).astype(jnp.bfloat16), is_lane, (((1,), (1,)), ((), ())),
                              preferred_element_type=F32)
    plane_resid = by_node[:8] + by_node[8:16] + by_node[16:]
    settle(inverse_recv, i_rs.at[0])
    corr = jnp.zeros((4, NZ), F32)
    for slot in range(DEPTH):
        rows = inverse if slot == DEPTH - 1 else inverse_recv.at[slot]
        acc = rows[:, pl.ds(0, NZ)] * plane_resid[0:1]
        for k in range(1, 8):
            acc = acc + rows[:, pl.ds(NZ * k, NZ)] * plane_resid[k:k + 1]
        place = 8 * (2 * gx + chip_y // 2) + lax.rem(chip_z + 1 + slot, DEPTH)
        corr = jnp.where(lane[:4] == place, jnp.sum(acc, axis=1, keepdims=True), corr)
    z_send[0] = jnp.where(sub // 4 == lax.rem(chip_y, 2), jnp.concatenate([corr, corr]), 0.0)
    z_send[1] = table
    send_depth(z_send, z_recv, 0)

    found = totals([sums[bx][q][by] for q in range(3) for bx, by in blocks])
    table = jnp.zeros((8, NZ), F32)
    for i in range(4):
        for q in range(3):
            table = jnp.where(cell[q][i], found[4 * q + i], table)

    for copy in lc:
        copy.wait_recv()
    losses = [[], []]
    outs = []
    for s in range(4):
        out = w_side[s] * l_recv[s ^ 1]
        outs.append(out)
        losses[0].append(halves(out))
        losses[1].append(halves(out * l_send[s]))
    lost = totals([losses[q][bx][by] + losses[q][2 + by][bx] for q in range(2) for bx, by in blocks])
    for i in range(4):
        for q in range(2):
            table = jnp.where(cell[q][i], table - lost[4 * q + i], table)
    send_plane(1, table)
    for s in range(4):
        at = pl.ds((T - 1) * T * (s % 2), T) if s < 2 else pl.ds((T - 1) * (s % 2), T, stride=T)
        image_f[at] -= outs[s]
    settle(z_recv, z_rs.at[0])
    send_plane(2, z_send[0] + jnp.sum(z_recv[:, 0], axis=0))
    near_out[pl.ds(0, DEPTH - 1)] = z_recv[:, 1]
    near_out[DEPTH - 1] = z_send[1]
    t_send[...] = plane_sum(1)
    send_depth(t_send, t_recv, 1)
    far_out[DEPTH - 1] = t_send[...]
    for copy in started:
        copy.wait_send()
    settle(inverse_recv, i_ss.at[0])
    settle(z_recv, z_ss.at[0])
    settle(p_recv.at[0], p_ss.at[0])
    settle(p_recv.at[1], p_ss.at[1])
    coarse_out[...] = plane_sum(2)
    settle(p_recv.at[2], p_ss.at[2])
    settle(t_recv, z_rs.at[1])
    far_out[pl.ds(0, DEPTH - 1)] = t_recv[...]
    settle(t_recv, z_ss.at[1])


def finish(guess, l, image, resid, q, faces, coarse, near, far, pressure, residual, press_v, resid_v, out_sem):
    gx, gy = lax.axis_index("gx"), lax.axis_index("gy")
    chip_z, chip_y = gy // 4, lax.rem(gy, 4)
    near_f, far_f = near.reshape(DEPTH * 8, NZ), far.reshape(DEPTH * 8, NZ)

    def pick(ref, i):
        return ref[pl.ds(i, DEPTH, stride=8)]

    c = coarse[...]
    node = pick(near_f, 0).astype(jnp.int32)
    in_y = lax.rem(node // 4, 4)
    at_row = lax.rem(node, 4) + 4 * lax.rem(in_y, 2)
    at_lane = lax.rem(node // 16, 8) + 8 * (2 * (node // NZ) + in_y // 2)
    block = jnp.zeros((DEPTH, NZ), F32)
    for s in range(DEPTH):
        line = jnp.broadcast_to(c[s:s + 1], (DEPTH, NZ))
        hit = jnp.take_along_axis(line, at_lane, axis=1, mode="promise_in_bounds")
        block = jnp.where(at_row == s, hit, block)
    east = pltpu.roll(block, NZ - 8, 1)
    lane = lax.broadcasted_iota(jnp.int32, (DEPTH, NZ), 1)
    north = jnp.where(lax.rem(lane, 8) == 7, pltpu.roll(pltpu.roll(block, 7, 1), DEPTH - 1, 0),
                      pltpu.roll(block, NZ - 1, 1))
    to_east, to_north = block - east, block - north
    numer = pick(far_f, 2) + block * pick(near_f, 4)
    denom = (pick(far_f, 1) + 2.0 * block * pick(far_f, 0) + pick(near_f, 1) * block * block
             + pick(near_f, 2) * to_east * to_east + pick(near_f, 3) * to_north * to_north)

    def total(v):
        return jnp.sum(jnp.sum(v, axis=0, keepdims=True), axis=1, keepdims=True)

    step = total(numer) / total(denom)
    turn = lax.rem(NZ - 16 * gx - 2 * chip_y, NZ)
    block, to_east, to_north = (pltpu.roll(v, turn, 1) for v in (block, to_east, to_north))

    def value(v, slot, at):
        return v[slot:slot + 1, at % NZ:at % NZ + 1]

    high = lax.broadcasted_iota(jnp.int32, (T, NZ), 0) >= BLK

    def spread(lower, upper):
        return step * jnp.where(high, upper, lower)

    last = DEPTH - 1
    mine = [spread(value(block, last, 8 * bx), value(block, last, 8 * bx + 1)) for bx in range(2)]
    flux_x = [faces[i] * spread(value(to_east, last, 8 * (i - 1)), value(to_east, last, 8 * (i - 1) + 1))
              for i in range(3)]
    below = [jnp.where(chip_y > 0, value(to_north, last, 8 * bx - 1), value(to_north, last - 1, 8 * bx + 7))
             for bx in range(2)]
    flux_y = [faces[3] * spread(*below)] + [
        faces[3 + i] * spread(value(to_north, last, i - 1), value(to_north, last, 8 + i - 1)) for i in (1, 2)]
    flat = resid_v.reshape(T * T, NZ)
    copies = []
    for part in range(2):
        rows = pl.ds(BLK * part, BLK)
        add = mine[part]
        press_v[rows] = guess[rows] + step * l[rows] + add
        copies.append(pltpu.make_async_copy(press_v.at[rows], pressure.at[rows], out_sem.at[2 * part]))
        copies[-1].start()
        resid_v[rows] = resid[rows] - step * image[rows] - q[rows] * add
        if part == 0:
            resid_v[0] += flux_x[0]
            resid_v[15] -= flux_x[1]
        else:
            resid_v[16] += flux_x[1]
            resid_v[31] -= flux_x[2]
        some = slice(BLK * part, BLK * part + BLK)
        for y, i, sign in ((0, 0, 1.0), (15, 1, -1.0), (16, 1, 1.0), (31, 2, -1.0)):
            flat[pl.ds(BLK * part * T + y, BLK, stride=T)] += sign * flux_y[i][some]
        copies.append(pltpu.make_async_copy(resid_v.at[rows], residual.at[rows], out_sem.at[2 * part + 1]))
        copies[-1].start()
    for copy in copies:
        copy.wait()


def body(right_side, guess, conductivity, wet_mask, coarse_map, coarse_inverse):
    tile = jax.ShapeDtypeStruct((T, T, NZ), F32)
    table = jax.ShapeDtypeStruct((DEPTH, 8, NZ), F32)
    hbm = pl.BlockSpec(memory_space=pltpu.HBM)
    vmem = pl.BlockSpec(memory_space=pltpu.VMEM)
    field = pltpu.VMEM((ROWS, STRIDE, NZ), F32)
    dma = pltpu.SemaphoreType.DMA
    state = pl.pallas_call(
        kernel,
        out_shape=(tile, tile, tile, tile, tile, jax.ShapeDtypeStruct((6, T, NZ), F32),
                   jax.ShapeDtypeStruct((8, NZ), F32), table, table),
        in_specs=[pl.BlockSpec(memory_space=pltpu.SMEM)] + [hbm] * 5,
        out_specs=(vmem,) * 9,
        scratch_shapes=[
            pltpu.VMEM((3, ROWS, STRIDE, NZ), F32), pltpu.VMEM((T, T, NZ), jnp.int32),
        ] + [field] * 9 + [
            pltpu.VMEM((4, NODES), F32), pltpu.VMEM((DEPTH - 1, 4, NODES), F32),
            pltpu.VMEM((4, 2, T, NZ), F32), pltpu.VMEM((4, 2, T, NZ), F32),
            pltpu.VMEM((4, 6 * T + 8, NZ), F32), pltpu.VMEM((4, 6 * T + 8, NZ), F32),
            pltpu.VMEM((4, 24, NZ), F32), pltpu.VMEM((4, 24, NZ), F32),
            pltpu.VMEM((4, T, NZ), F32), pltpu.VMEM((4, T, NZ), F32),
            pltpu.VMEM((3, 8, NZ), F32), pltpu.VMEM((3, PLANE - 1, 8, NZ), F32),
            pltpu.VMEM((2, 8, NZ), F32), pltpu.VMEM((DEPTH - 1, 2, 8, NZ), F32),
            pltpu.VMEM((8, NZ), F32), pltpu.VMEM((DEPTH - 1, 8, NZ), F32),
            dma((5,)),
        ] + [dma((4,))] * 8 + [dma((3,))] * 2 + [dma((2,))] * 2 + [dma((1,))] * 2,
        compiler_params=pltpu.CompilerParams(
            collective_id=0, has_side_effects=True, vmem_limit_bytes=40 * 1024 * 1024),
    )(*(pltpu.with_memory_space_constraint(array, pltpu.HBM) for array in (
        coarse_map.transpose(0, 2, 1), coarse_inverse, right_side, guess, conductivity, wet_mask)))
    return pl.pallas_call(
        finish,
        out_shape=(tile, tile),
        in_specs=[vmem] * 9,
        out_specs=(hbm, hbm),
        scratch_shapes=[pltpu.VMEM((T, T, NZ), F32)] * 2 + [dma((8,))],
        compiler_params=pltpu.CompilerParams(vmem_limit_bytes=16 * 1024 * 1024),
    )(*state)


def solution(mesh):
    grid = P("gx", "gy", None)
    in_specs = (grid, grid, grid, grid, grid, P(("gx", "gy"), None))
    return jax.shard_map(body, mesh=mesh, in_specs=in_specs, out_specs=(grid, grid), check_vma=False)
```
